128 devices in a mesh: dp: 8 (over y, x_hi), tensor: 16 (over z, x_lo, core).
Axes of the slice: x: 4 (x_hi: 2, x_lo: 2; x = x_hi * 2 + x_lo), y: 4, z: 4, core: 2. Of those that a mesh axis runs over, the one named last changes fastest.
Arguments:
- tokens: bfloat16 [9232, 1024], P('dp', 'tensor'), may hold values from -6 to 6
- counts: int32 [8], replicated, may hold values from 1 to 2, 12 in all
- cotangent: bfloat16 [9232, 1024], P('dp', 'tensor'), may hold values from -6 to 6
- qkv_weight: bfloat16 [2, 1024, 3072], P(None, 'dp', 'tensor'), may hold values from -0.1875 to 0.1875
- out_weight: bfloat16 [2, 1024, 1024], P(None, 'tensor', 'dp'), may hold values from -0.75 to 0.75
- fc1_weight: bfloat16 [2, 1024, 4096], P(None, 'dp', 'tensor'), may hold values from -0.1875 to 0.1875
- fc2_weight: bfloat16 [2, 4096, 1024], P(None, 'tensor', 'dp'), may hold values from -0.09375 to 0.09375
- norm_gains: bfloat16 [2, 2, 16, 64], P(None, None, 'tensor', 'dp'), may hold values from 0.25 to 1.75
- shifts: bfloat16 [2, 4, 16, 64], P(None, None, 'tensor', 'dp'), may hold values from -3 to 3
- qv_bias: bfloat16 [2, 16, 128], P(None, 'tensor', 'dp'), may hold values from -3 to 3
- fc1_bias: bfloat16 [2, 16, 256], P(None, 'tensor', 'dp'), may hold values from -3 to 3
Outputs:
- out_stream: bfloat16 [9232, 1024], P('dp', 'tensor')
- grad_input: float32 [9232, 1024], P('dp', 'tensor')
- grad_qkv: float32 [2, 1024, 3072], P(None, 'dp', 'tensor')
- grad_out: float32 [2, 1024, 1024], P(None, 'tensor', 'dp')
- grad_fc1: float32 [2, 1024, 4096], P(None, 'dp', 'tensor')
- grad_fc2: float32 [2, 4096, 1024], P(None, 'tensor', 'dp')
- grad_gains: float32 [2, 2, 16, 64], P(None, None, 'tensor', 'dp')
- grad_shifts: float32 [2, 4, 16, 64], P(None, None, 'tensor', 'dp')
- grad_qv_bias: float32 [2, 16, 128], P(None, 'tensor', 'dp')
- grad_fc1_bias: float32 [2, 16, 256], P(None, 'tensor', 'dp')
The draws below stay inside these ranges and needn't reach their ends.
Inputs may be any that keep to these rules, and one draw needn't show every extreme that they name: Live image slots of dp index i are the first counts[i] of its 2; the counts sum to 12 and the largest is 2.
All inputs are finite; a program needn't handle non-finite values.
Results may differ from the reference program's by a relative error of at most 0.023.
Values may be sent and summed in bfloat16 or wider, within the bound.
A program may use at most 128 MiB of HBM per device.

```python
import math
import jax
import jax.numpy as jnp
import numpy as np
from jax import lax

D = 1024
HEADS = 16
HD = 64
FF = 4096
SEQ = 577
LAYERS = 2
SLOTS = 2
IMAGES = 12
TOKENS = 9232
N_DP = 8


def block_scale(rng, shape, shards, low, largest):
    gain = 1.0
    for position, parts in shards:
        draws = jax.random.uniform(jax.random.fold_in(jax.random.fold_in(rng, 6), position), (parts,), jnp.float32, low / len(shards), largest / len(shards))
        gain = gain * jnp.repeat(jnp.exp(draws), shape[position] // parts).reshape((-1,) + (1,) * (len(shape) - 1 - position))
    return gain


def profile(amount, total, reach, skew):
    portions = [(1 << 20) // math.isqrt(grade ** skew) + 1 for grade in range(2, amount + 1)]
    surplus, given = total - reach - (amount - 1), [1] * (amount - 1)
    while surplus > 0:
        candidates = [i for i in range(amount - 1) if given[i] < reach]
        mass, left = sum([portions[i] for i in candidates]), surplus
        for i in candidates:
            addition = min(reach - given[i], max(1, left * portions[i] // mass), surplus)
            given[i] = given[i] + addition
            surplus = surplus - addition
    return np.array([reach] + given)


def uneven(rng, number_of, total, reach, lean):
    if number_of == 2:
        one = jax.random.randint(rng, (), max(1, total - reach), min(reach, total - 1) + 1)
        return jnp.stack([one, total - one])
    tallies = jnp.asarray(profile(number_of, total, reach, lean), jnp.int32)
    couples = (number_of - 1) // 2
    giver, receiver = tallies[1:1 + 2 * couples:2], tallies[2:2 + 2 * couples:2]
    margin = jnp.minimum(giver - 1, reach - receiver)
    shifted = jax.random.randint(jax.random.fold_in(rng, 1), (couples,), 0, 1 << 20) % (margin + 1)
    tallies = tallies.at[1:1 + 2 * couples:2].set(giver - shifted).at[2:2 + 2 * couples:2].set(receiver + shifted)
    return tallies[jax.random.permutation(jax.random.fold_in(rng, 2), number_of)]


def normal_values(rng, dims, width, limit, split=(), held_as=jnp.bfloat16):
    factor_of = block_scale(rng, dims, split, -0.22, 0.18) if split else 1.0
    array = jax.random.normal(rng, dims, jnp.float32) * width * factor_of
    return jnp.minimum(jnp.maximum(array, -limit), limit).astype(held_as)


def setup_inputs(seed: int = 0) -> dict:
    seeds = jax.random.split(jax.random.key(seed), 12)
    tokens = normal_values(seeds[0], (TOKENS, D), 1.0, 6.0, ((0, 8), (1, 16)))
    counts = uneven(seeds[1], N_DP, IMAGES, SLOTS, 2).astype(jnp.int32)
    cotangent = normal_values(seeds[2], (TOKENS, D), 1.0, 6.0, ((0, 8), (1, 16)))
    qkv_weight = normal_values(seeds[3], (LAYERS, D, 3 * D), D ** -0.5, 0.1875, ((1, 8), (2, 16)))
    out_weight = normal_values(seeds[4], (LAYERS, D, D), (D // 16) ** -0.5, 0.75, ((1, 16), (2, 8)))
    fc1_weight = normal_values(seeds[5], (LAYERS, D, FF), D ** -0.5, 0.1875, ((1, 8), (2, 16)))
    fc2_weight = normal_values(seeds[6], (LAYERS, FF, D), FF ** -0.5, 0.09375, ((1, 16), (2, 8)))
    norm_gains = jnp.clip(1.0 + 0.15 * jax.random.normal(seeds[7], (LAYERS, 2, HEADS, HD), jnp.float32), 0.25, 1.75).astype(jnp.bfloat16)
    shifts = normal_values(seeds[8], (LAYERS, 4, HEADS, HD), 0.5, 3.0, ((2, 16), (3, 8)))
    qv_bias = normal_values(seeds[9], (LAYERS, HEADS, 2 * HD), 0.5, 3.0, ((1, 16), (2, 8)))
    fc1_bias = normal_values(seeds[10], (LAYERS, HEADS, FF // HEADS), 0.5, 3.0, ((1, 16), (2, 8)))
    return {"tokens": tokens, "counts": counts, "cotangent": cotangent, "qkv_weight": qkv_weight, "out_weight": out_weight, "fc1_weight": fc1_weight, "fc2_weight": fc2_weight, "norm_gains": norm_gains, "shifts": shifts, "qv_bias": qv_bias, "fc1_bias": fc1_bias}


epsilon = 1e-06

@jax.custom_vjp
def low(v):
    return lax.optimization_barrier(v.astype(jnp.bfloat16)).astype(jnp.float32)

@jax.custom_vjp
def low_back(v):
    return v

def low_keep(v):
    return (low(v), None)

def low_pass(kept, grad):
    return (grad,)

def back_keep(v):
    return (v, None)

def back_low(kept, grad):
    return (low(grad),)
low.defvjp(low_keep, low_pass)
low_back.defvjp(back_keep, back_low)

def matmul(lhs_matrix, rhs_matrix):
    return jnp.dot(lhs_matrix, rhs_matrix, precision=lax.Precision.HIGHEST)

def norm_rows(values, gain_row, shift_row):
    row_mean = lax.optimization_barrier(jnp.mean(values, axis=-1, keepdims=True))
    variance = lax.optimization_barrier(jnp.mean(values * values, axis=-1, keepdims=True)) - row_mean * row_mean
    return (values - row_mean) * lax.rsqrt(variance + epsilon) * gain_row + shift_row

def layer_step(state, proj_qkv, proj_out, proj_up, proj_down, gain_set, shift_set, bias_qv, bias_up):
    first_in = low(norm_rows(state, gain_set[0].reshape(D), shift_set[0].reshape(D)))
    qkv_shift = jnp.stack([bias_qv[:, :HD], jnp.zeros((HEADS, HD), jnp.float32), bias_qv[:, HD:]], axis=1).reshape(3 * D)
    mixed_rows = (matmul(first_in, proj_qkv) + qkv_shift).reshape(SEQ, HEADS, 3, HD)
    queries = low(low_back(mixed_rows[:, :, 0]))
    key_rows = low(low_back(mixed_rows[:, :, 1]))
    value_rows = low(low_back(mixed_rows[:, :, 2]))
    scores = low_back(HD ** (-0.5) * jnp.einsum('qhc,khc->hqk', queries, key_rows, precision=lax.Precision.HIGHEST))
    soft_weights = low(jax.nn.softmax(scores, axis=-1))
    attended = jnp.einsum('hqk,khc->qhc', soft_weights, value_rows, precision=lax.Precision.HIGHEST).reshape(SEQ, D)
    attended = low(low_back(attended))
    middle = state + low_back(matmul(attended, proj_out) + shift_set[1].reshape(D))
    second_in = low(norm_rows(middle, gain_set[1].reshape(D), shift_set[2].reshape(D)))
    pre_act = low_back(matmul(second_in, proj_up) + bias_up.reshape(FF))
    activated = low(jax.nn.gelu(pre_act, approximate=False))
    return middle + low_back(matmul(activated, proj_down) + shift_set[3].reshape(D))

def forward_image(image_rows, params):
    state = image_rows
    for layer_index in range(LAYERS):
        state = layer_step(state, *[member[layer_index] for member in params])
    return state

def reference(tokens, counts, cotangent, qkv_weight, out_weight, fc1_weight, fc2_weight, norm_gains, shifts, qv_bias, fc1_bias):
    params = tuple((member.astype(jnp.float32) for member in (qkv_weight, out_weight, fc1_weight, fc2_weight, norm_gains, shifts, qv_bias, fc1_bias)))
    total_slots = N_DP * SLOTS
    images = tokens.astype(jnp.float32).reshape(total_slots, SEQ, D)
    cot_images = cotangent.astype(jnp.float32).reshape(total_slots, SEQ, D)
    slot_ids = jnp.arange(total_slots, dtype=jnp.int32)
    live_slots = (slot_ids % SLOTS < counts[slot_ids // SLOTS]).astype(jnp.float32)

    def one_image(grad_sums, slot_item):
        image_rows, cot_rows, live_flag = slot_item
        result, pullback = jax.vjp(forward_image, image_rows, params)
        d_image, d_params = pullback(cot_rows * live_flag)
        return (jax.tree.map(jnp.add, grad_sums, d_params), (result * live_flag, d_image))
    zero_sums = jax.tree.map(jnp.zeros_like, params)
    grad_totals, (results, d_images) = lax.scan(one_image, zero_sums, (images, cot_images, live_slots))
    return (results.reshape(TOKENS, D).astype(jnp.bfloat16), d_images.reshape(TOKENS, D), grad_totals[0], grad_totals[1], grad_totals[2], grad_totals[3], grad_totals[4], grad_totals[5], grad_totals[6], grad_totals[7])
```

```python
import functools

import jax
import jax.numpy as jnp
from jax import lax
from jax.experimental import pallas as pl
from jax.experimental.pallas import tpu as pltpu
from jax.sharding import PartitionSpec as P

MESH = pl.DeviceIdType.MESH
F32 = jnp.float32
BF16 = jnp.bfloat16
SEQ = 577
LAYERS = 2
BLOCK = 80
ROWS = 8 * BLOCK
D = 1024
EPS = 1e-06
VMEM = pl.BlockSpec(memory_space=pltpu.VMEM)
ANY = pl.BlockSpec(memory_space=pl.ANY)


class Place:
    def __init__(self):
        self.t = lax.axis_index("tensor")
        self.d = lax.axis_index("dp")
        self.z = self.t // 4
        self.xl = (self.t // 2) % 2
        self.c = self.t % 2
        self.w = self.d * 2 + self.xl
        self.j = self.z * 2 + self.c
        self.zf = (self.z + 5 - 2 * self.c) % 4
        self.zb = (self.z + 3 + 2 * self.c) % 4
        self.zo = (self.z + 2) % 4

    def member(self, z, c):
        return (self.d, z * 4 + self.xl * 2 + c)

    def member_at(self, k):
        j = (self.j + k) % 8
        return self.member(j // 2, j % 2)

    def sharer(self, k):
        w = (self.w + k) % 16
        return w // 2, w % 2, (w // 2, self.z * 4 + (w % 2) * 2 + self.c)


def remote(src, dst, sems, role, device):
    return pltpu.make_async_remote_copy(
        src_ref=src,
        dst_ref=dst,
        send_sem=sems[0].at[role],
        recv_sem=sems[1].at[role],
        device_id=device,
        device_id_type=MESH,
    )


def greet(devices):
    barrier = pltpu.get_barrier_semaphore()
    for device in devices:
        pl.semaphore_signal(barrier, inc=1, device_id=device, device_id_type=MESH)
    pl.semaphore_wait(barrier, len(devices))


def near(me):
    return [me.member(me.zf, me.c), me.member(me.zb, me.c), me.member(me.z, 1 - me.c)]


def sharers(me):
    return [me.sharer(k)[2] for k in range(1, 16)]


def gather(out, me, sems):
    def pair(z, role, device):
        copy = remote(out.at[z, me.c], out.at[z, me.c], sems, role, device)
        copy.start()
        return copy

    ahead, back, other = near(me)
    first = pair(me.z, 0, ahead)
    second = pair(me.z, 1, back)
    over = [pair(me.z, 3, other)]
    first.wait_recv()
    third = pair(me.zb, 2, ahead)
    over.append(pair(me.zb, 4, other))
    second.wait_recv()
    over.append(pair(me.zf, 5, other))
    third.wait_recv()
    over.append(pair(me.zo, 6, other))
    for copy in over:
        copy.wait_recv()
    for copy in [first, second, third] + over:
        copy.wait_send()


def reduce(part, crossed, held, landed, me, sems):
    ahead, back, other = near(me)
    copies = []
    for role, z in enumerate((me.zo, me.zf, me.zb, me.z)):
        copies.append(remote(part.at[z, 1 - me.c], crossed.at[role], sems, role, other))
        copies[-1].start()

    def both(role, z):
        copies[role].wait_recv()
        return part[z, me.c].astype(F32) + crossed[role].astype(F32)

    def send(slot, value, device):
        held[slot] = value.astype(BF16)
        copy = remote(held.at[slot], landed.at[slot], sems, 4 + slot, device)
        copy.start()
        copies.append(copy)
        return copy

    long = send(0, both(0, me.zo), ahead)
    short = send(1, both(1, me.zb), back)
    relay = both(2, me.zf)
    long.wait_recv()
    last = send(2, relay + landed[0].astype(F32), ahead)
    total = both(3, me.z)
    short.wait_recv()
    total = total + landed[1].astype(F32)
    last.wait_recv()
    total = total + landed[2].astype(F32)
    return total, copies


def reduce_scratch():
    return [
        pltpu.VMEM((4, BLOCK, D), BF16),
        pltpu.VMEM((3, BLOCK, D), BF16),
        pltpu.VMEM((3, BLOCK, D), BF16),
        pltpu.SemaphoreType.DMA((7,)),
        pltpu.SemaphoreType.DMA((7,)),
    ]


def pair_sems(count):
    return [pltpu.SemaphoreType.DMA((count,)), pltpu.SemaphoreType.DMA((count,))]


def spread_start(src, dst, me, sems, local_sem):
    place = dst.at[me.xl, :, pl.ds(pl.multiple_of(me.d * 128, 128), 128)]
    mine = pltpu.make_async_copy(src, place, local_sem)
    mine.start()
    copies = [remote(src, place, sems, k - 1, me.sharer(k)[2]) for k in range(1, 16)]
    for copy in copies:
        copy.start()
    return mine, copies


def collect_start(src, dst, me, sems, local_sem):
    mine = pltpu.make_async_copy(
        src.at[me.xl, :, pl.ds(pl.multiple_of(me.d * 128, 128), 128)], dst.at[me.w], local_sem
    )
    mine.start()
    copies = []
    for k in range(1, 16):
        d, xl, device = me.sharer(k)
        part = src.at[xl, :, pl.ds(pl.multiple_of(d * 128, 128), 128)]
        copies.append(remote(part, dst.at[me.w], sems, k - 1, device))
        copies[-1].start()
    return mine, copies


def finish(started):
    mine, copies = started
    mine.wait()
    for copy in copies:
        copy.wait()


def row_stats(v):
    mean = jnp.sum(v, axis=1, keepdims=True) / D
    square = jnp.sum(v * v, axis=1, keepdims=True) / D
    return mean, lax.rsqrt(square - mean * mean + EPS)


def normed(v, gain, bias):
    mean, inv = row_stats(v)
    return ((v - mean) * inv * gain + bias).astype(BF16)


def tall(refs, shape):
    return [jax.ShapeDtypeStruct(shape, F32)] * refs


def call(body, identity, inputs, in_specs, out_shape, out_specs, scratch):
    return pl.pallas_call(
        body,
        out_shape=out_shape,
        in_specs=in_specs,
        out_specs=out_specs,
        scratch_shapes=scratch,
        compiler_params=pltpu.CompilerParams(
            collective_id=identity, has_side_effects=True, vmem_limit_bytes=48 * 1024 * 1024
        ),
    )(*inputs)


def open_kernel(x_ref, w_ref, s_ref, y_ref, wide_ref, sw_ref, st_ref, comp, *sems):
    me = Place()
    greet(sharers(me) + [me.member_at(k) for k in range(1, 8)])
    swap = remote(x_ref.at[1 - me.xl], y_ref.at[me.z, me.c, me.xl], sems[0:2], 0, (me.d, me.z * 4 + (1 - me.xl) * 2 + me.c))
    swap.start()
    local = sems[8]
    keep = pltpu.make_async_copy(x_ref.at[me.xl], y_ref.at[me.z, me.c, me.xl], local.at[0])
    keep.start()
    sw_ref[me.w] = s_ref[...]
    small = [remote(s_ref, sw_ref.at[me.w], sems[4:6], k - 1, me.sharer(k)[2]) for k in range(1, 16)]
    for copy in small:
        copy.start()
    wide = spread_start(w_ref, wide_ref, me, sems[2:4], local.at[1])
    keep.wait()
    swap.wait()
    gather(y_ref, me, sems[9:11])
    for copy in small:
        copy.wait()
    for w in range(16):
        comp[w : w + 1, :] = sw_ref[w, 0:1, :]
    st_ref[me.z, me.c] = comp[...]
    spread = [remote(comp, st_ref.at[me.z, me.c], sems[6:8], k - 1, me.member_at(k)) for k in range(1, 8)]
    for copy in spread:
        copy.start()
    for copy in spread:
        copy.wait()
    finish(wide)


def open_call(x, w, s):
    return call(
        open_kernel,
        0,
        (x, w, s),
        [VMEM, ANY, VMEM],
        [
            jax.ShapeDtypeStruct((4, 2, 2, ROWS, 128), BF16),
            jax.ShapeDtypeStruct((2, w.shape[0], D), BF16),
            jax.ShapeDtypeStruct((16, 8, 128), F32),
            jax.ShapeDtypeStruct((4, 2, 16, 128), F32),
        ],
        [VMEM, ANY, VMEM, VMEM],
        [pltpu.VMEM((16, 128), F32)]
        + pair_sems(1)
        + pair_sems(15)
        + pair_sems(15)
        + pair_sems(7)
        + [pltpu.SemaphoreType.DMA((2,))]
        + pair_sems(7),
    )


def forward_kernel(spreads, last, part, state, shift, gain, bias, *refs):
    refs = list(refs)
    w_ref = refs.pop(0) if spreads else None
    new_ref = refs.pop(0)
    out_ref = None if last else refs.pop(0)
    wide_ref = refs.pop(0) if spreads else None
    crossed, held, landed, s0, s1, s2, s3, s4, s5, local = refs
    me = Place()
    greet(near(me) + (sharers(me) if spreads else []))
    wide = spread_start(w_ref, wide_ref, me, (s4, s5), local.at[0]) if spreads else None
    total, copies = reduce(part, crossed, held, landed, me, (s0, s1))
    value = state[...] + (total + shift[...])
    new_ref[...] = value
    if not last:
        out_ref[me.z, me.c] = normed(value, gain[...], bias[...])
        gather(out_ref, me, (s2, s3))
    for copy in copies:
        copy.wait_send()
    if spreads:
        finish(wide)


def forward_call(identity, part, state, shift, gain, bias, w=None, last=False):
    out_shape = [jax.ShapeDtypeStruct((BLOCK, D), F32)]
    out_specs = [VMEM]
    if not last:
        out_shape.append(jax.ShapeDtypeStruct((4, 2, BLOCK, D), BF16))
        out_specs.append(VMEM)
    inputs = [part.reshape(4, 2, BLOCK, D), state, shift, gain, bias]
    in_specs = [VMEM] * 5
    if w is not None:
        inputs.append(w)
        in_specs.append(ANY)
        out_shape.append(jax.ShapeDtypeStruct((2, w.shape[0], D), BF16))
        out_specs.append(ANY)
    return call(
        functools.partial(forward_kernel, w is not None, last),
        identity,
        inputs,
        in_specs,
        out_shape,
        out_specs,
        reduce_scratch() + pair_sems(7) + pair_sems(15) + [pltpu.SemaphoreType.DMA((1,))],
    )


def backward_kernel(collects, last, part, base, above, gain, *refs):
    refs = list(refs)
    w_ref = refs.pop(0) if collects else None
    new_ref = refs.pop(0)
    sums_ref = refs.pop(0)
    out_ref = None if last else refs.pop(0)
    slots_ref = refs.pop(0) if collects else None
    crossed, held, landed, s0, s1, s2, s3, s4, s5, local = refs
    me = Place()
    greet(near(me) + (sharers(me) if collects else []))
    slots = collect_start(w_ref, slots_ref, me, (s4, s5), local.at[0]) if collects else None
    total, copies = reduce(part, crossed, held, landed, me, (s0, s1))
    v = base[...]
    mean, inv = row_stats(v)
    hat = (v - mean) * inv
    weighted = total * gain[...]
    first = jnp.sum(weighted, axis=1, keepdims=True) / D
    second = jnp.sum(weighted * hat, axis=1, keepdims=True) / D
    value = above[...] + inv * (weighted - first - hat * second)
    new_ref[...] = value
    low = value.astype(BF16)
    if not last:
        out_ref[me.z, me.c] = low
    sums_ref[...] = jnp.zeros_like(sums_ref)
    sums_ref[0:1, :] = jnp.sum(total * hat, axis=0, keepdims=True)
    sums_ref[1:2, :] = jnp.sum(total, axis=0, keepdims=True)
    sums_ref[2:3, :] = jnp.sum(low.astype(F32), axis=0, keepdims=True)
    if not last:
        gather(out_ref, me, (s2, s3))
    for copy in copies:
        copy.wait_send()
    if collects:
        finish(slots)


def backward_call(identity, part, base, above, gain, w=None, last=False):
    out_shape = [jax.ShapeDtypeStruct((BLOCK, D), F32), jax.ShapeDtypeStruct((8, D), F32)]
    out_specs = [VMEM, VMEM]
    if not last:
        out_shape.append(jax.ShapeDtypeStruct((4, 2, BLOCK, D), BF16))
        out_specs.append(VMEM)
    inputs = [part.reshape(4, 2, BLOCK, D), base, above, gain]
    in_specs = [VMEM] * 4
    if w is not None:
        inputs.append(w)
        in_specs.append(ANY)
        out_shape.append(jax.ShapeDtypeStruct((16, w.shape[1], 128), BF16))
        out_specs.append(ANY)
    return call(
        functools.partial(backward_kernel, w is not None, last),
        identity,
        inputs,
        in_specs,
        out_shape,
        out_specs,
        reduce_scratch() + pair_sems(7) + pair_sems(15) + [pltpu.SemaphoreType.DMA((1,))],
    )


def close_kernel(rows_ref, vec_ref, bias_ref, w_ref, out_ref, sum_ref, slots_ref, mine, from_t, from_w, *sems):
    me = Place()
    tensor = [(me.d, (me.t + k) % 16) for k in range(1, 16)]
    extra = [((me.d + k) % 8, me.z * 4 + xl * 2 + me.c) for k in range(1, 8) for xl in range(2)]
    greet(tensor + extra)
    local = sems[8]
    slots = collect_start(w_ref, slots_ref, me, sems[6:8], local.at[2])

    def vec(z):
        return vec_ref.at[:, pl.ds(pl.multiple_of(z * 256, 256), 256)]

    keep_vec = pltpu.make_async_copy(vec(me.z), from_t.at[me.j], local.at[0])
    keep_vec.start()
    first = []
    for k in range(1, 8):
        j = (me.j + k) % 8
        first.append(remote(vec(j // 2), from_t.at[me.j], sems[0:2], k - 1, me.member(j // 2, j % 2)))
        first[-1].start()

    def lanes(t):
        return rows_ref.at[:, :, pl.ds(pl.multiple_of((t // 2) * 128, 128), 128)]

    keep_rows = pltpu.make_async_copy(lanes(me.t), out_ref.at[me.xl, me.j], local.at[1])
    keep_rows.start()
    rows = []
    for k in range(1, 16):
        t = (me.t + k) % 16
        rows.append(remote(lanes(t), out_ref.at[me.xl, me.j], sems[2:4], k - 1, (me.d, t)))
        rows[-1].start()
    keep_vec.wait()
    for copy in first:
        copy.wait()
    total = from_t[0]
    for j in range(1, 8):
        total = total + from_t[j]
    mine[0:16, :] = total
    mine[16:24, :] = bias_ref[...]
    from_w[me.w] = mine[...]
    second = [remote(mine, from_w.at[me.w], sems[4:6], k - 1, me.sharer(k)[2]) for k in range(1, 16)]
    for copy in second:
        copy.start()
    for copy in second:
        copy.wait()
    total = from_w[0]
    for w in range(1, 16):
        total = total + from_w[w]
    sum_ref[...] = total
    keep_rows.wait()
    for copy in rows:
        copy.wait()
    finish(slots)


def close_call(identity, rows, vectors, bias, w):
    return call(
        close_kernel,
        identity,
        (rows, vectors, bias, w),
        [VMEM, VMEM, VMEM, ANY],
        [
            jax.ShapeDtypeStruct((2, 8, 2, BLOCK, 128), BF16),
            jax.ShapeDtypeStruct((24, 256), F32),
            jax.ShapeDtypeStruct((16, w.shape[1], 128), BF16),
        ],
        [VMEM, VMEM, ANY],
        [pltpu.VMEM((24, 256), F32), pltpu.VMEM((8, 16, 256), F32), pltpu.VMEM((16, 24, 256), F32)]
        + pair_sems(7)
        + pair_sems(15)
        + pair_sems(15)
        + pair_sems(15)
        + [pltpu.SemaphoreType.DMA((3,))],
    )


def matmul(a, b):
    return jnp.dot(a, b, preferred_element_type=F32)


def inner_left(a, b):
    return lax.dot_general(a, b, (((0,), (0,)), ((), ())), preferred_element_type=F32)


def inner_right(a, b):
    return lax.dot_general(a, b, (((1,), (1,)), ((), ())), preferred_element_type=F32)


def scores_of(queries, key_rows):
    scores = 64 ** (-0.5) * jnp.einsum("hqc,hkc->hqk", queries, key_rows, preferred_element_type=F32)
    return jnp.where(lax.broadcasted_iota(jnp.int32, scores.shape, 2) < SEQ, scores, -1e30)


def attend(queries, key_rows, value_rows):
    scores = scores_of(queries, key_rows)
    row_max = jnp.max(scores, axis=-1, keepdims=True)
    shifted = jnp.exp(scores - row_max)
    row_total = jnp.sum(shifted, axis=-1, keepdims=True)
    soft = (shifted / row_total).astype(BF16)
    attended = jnp.einsum("hqk,hkc->hqc", soft, value_rows, preferred_element_type=F32)
    return attended.astype(BF16), row_max + jnp.log(row_total)


def attend_back(queries, key_rows, value_rows, d_attended, log_total):
    soft = jnp.exp(scores_of(queries, key_rows) - log_total)
    d_soft = jnp.einsum("hqc,hkc->hqk", d_attended, value_rows, preferred_element_type=F32)
    d_values = jnp.einsum("hqk,hqc->hkc", soft.astype(BF16), d_attended, preferred_element_type=F32)
    d_scores = (soft * (d_soft - jnp.sum(soft * d_soft, axis=-1, keepdims=True))).astype(BF16)
    d_queries = 64 ** (-0.5) * jnp.einsum("hqk,hkc->hqc", d_scores, key_rows, preferred_element_type=F32)
    d_keys = 64 ** (-0.5) * jnp.einsum("hqk,hqc->hkc", d_scores, queries, preferred_element_type=F32)
    return d_queries.astype(BF16), d_keys.astype(BF16), d_values.astype(BF16)


def gelu(v):
    return 0.5 * v * (1.0 + lax.erf(v * 0.5**0.5))


def gelu_slope(v):
    return 0.5 * (1.0 + lax.erf(v * 0.5**0.5)) + v * jnp.exp(-0.5 * v * v) * (0.5 / jnp.pi) ** 0.5


def heads_first(v):
    return v.reshape(ROWS, 2, -1).transpose(1, 0, 2)


def heads_last(v):
    return v.transpose(1, 0, 2).reshape(ROWS, -1)


def local(
    tokens,
    counts,
    cotangent,
    qkv_weight,
    out_weight,
    fc1_weight,
    fc2_weight,
    norm_gains,
    shifts,
    qv_bias,
    fc1_bias,
):
    me = Place()
    live = me.xl < lax.dynamic_index_in_dim(counts, me.d, keepdims=False)

    def images(v):
        return jnp.pad(v.reshape(2, SEQ, 64), ((0, 0), (0, ROWS - SEQ), (0, 0)))

    x = jnp.concatenate([images(tokens), images(cotangent)], axis=2)
    packs = [
        (
            jnp.concatenate([qkv_weight[l].T, out_weight[l]], axis=0),
            jnp.concatenate([fc1_weight[l].T, fc2_weight[l]], axis=0),
        )
        for l in range(LAYERS)
    ]
    zeros = jnp.zeros((32,), F32)
    small = jnp.stack(
        [
            jnp.concatenate([norm_gains.reshape(32).astype(F32), shifts.reshape(64).astype(F32), zeros]),
            jnp.concatenate([qv_bias.reshape(32).astype(F32), fc1_bias.reshape(64).astype(F32), zeros]),
        ]
    )
    small = jnp.pad(small, ((0, 6), (0, 0)))
    y, wide_a, shared, vectors = open_call(x, packs[0][0], small)

    def features(v):
        return v.transpose(3, 0, 2, 1, 4).reshape(ROWS, D)

    token_rows = features(y[..., :64]).astype(F32)
    gradient_full = jnp.where(live, features(y[..., 64:]), jnp.zeros((), BF16))

    def vector_set(part, count):
        part = part.reshape(4, 2, 8, 2, LAYERS, count, 8)
        return part.transpose(4, 5, 0, 3, 1, 2, 6).reshape(LAYERS, count, 1, D)

    gains = vector_set(vectors[..., :32], 2)
    biases = vector_set(vectors[..., 32:96], 4)
    qv = shared[:, 1, :32].reshape(8, 2, LAYERS, 16).transpose(2, 1, 0, 3).reshape(LAYERS, 2, 128)
    up_bias = shared[:, 1, 32:96].reshape(8, 2, LAYERS, 32).transpose(2, 1, 0, 3).reshape(LAYERS, 512)
    qkv_shift = jnp.concatenate([qv[:, :, :64], jnp.zeros((LAYERS, 2, 64), F32), qv[:, :, 64:]], axis=2)
    qkv_shift = qkv_shift.reshape(LAYERS, 384)

    state = lax.dynamic_slice(token_rows, (me.j * BLOCK, 0), (BLOCK, D))
    first_in = normed(token_rows, gains[0, 0], biases[0, 0])
    saved = []
    wides = []
    for l in range(LAYERS):
        proj_qkv = wide_a[:, :192].reshape(384, D)
        proj_out = wide_a[:, 192:].reshape(128, D)
        mixed = (inner_right(first_in, proj_qkv) + qkv_shift[l]).astype(BF16)
        mixed = mixed.reshape(ROWS, 2, 3, 64).transpose(2, 1, 0, 3)
        queries, key_rows, value_rows = mixed[0], mixed[1], mixed[2]
        attended, log_total = attend(queries, key_rows, value_rows)
        attended = heads_last(attended)
        part = matmul(attended, proj_out).astype(BF16)
        middle, second_in, wide_b = forward_call(
            1 + 2 * l, part, state, biases[l, 1], gains[l, 1], biases[l, 2], packs[l][1]
        )
        second_in = second_in.reshape(ROWS, D)
        proj_up = wide_b[:, :256].reshape(512, D)
        proj_down = wide_b[:, 256:].reshape(512, D)
        pre_act = inner_right(second_in, proj_up) + up_bias[l]
        activated = gelu(pre_act).astype(BF16)
        part = matmul(activated, proj_down).astype(BF16)
        saved.append((state, middle, first_in, queries, key_rows, value_rows, attended, log_total, second_in, pre_act, activated))
        wides.append((proj_qkv, proj_out, proj_up, proj_down))
        if l < LAYERS - 1:
            state, first_in, wide_a = forward_call(
                2 + 2 * l, part, middle, biases[l, 3], gains[l + 1, 0], biases[l + 1, 0], packs[l + 1][0]
            )
            first_in = first_in.reshape(ROWS, D)
        else:
            (state,) = forward_call(2 + 2 * l, part, middle, biases[l, 3], gains[0, 0], biases[0, 0], last=True)
    out_rows = jnp.where(live, state, 0.0).astype(BF16)

    def halves(*parts):
        return jnp.concatenate([p.reshape(2, -1, D) for p in parts], axis=1).astype(BF16)

    gradient = lax.dynamic_slice(gradient_full, (me.j * BLOCK, 0), (BLOCK, D)).astype(F32)
    vector_sums = {(1, 3): jnp.sum(gradient, axis=0)}
    bias_sums = [None] * LAYERS
    slot_lists = {}
    pending = None
    for l in reversed(range(LAYERS)):
        state, middle, first_in, queries, key_rows, value_rows, attended, log_total, second_in, pre_act, activated = saved[l]
        proj_qkv, proj_out, proj_up, proj_down = wides[l]
        d_down = inner_left(activated, gradient_full)
        d_pre = (inner_right(gradient_full, proj_down) * gelu_slope(pre_act)).astype(BF16)
        d_up_bias = jnp.sum(d_pre.astype(F32), axis=0)
        d_up = inner_left(d_pre, second_in)
        part = matmul(d_pre, proj_up).astype(BF16)
        base = 5 + 2 * (LAYERS - 1 - l)
        gradient, sums, low, slot_lists["b", l] = backward_call(
            base, part, middle, gradient, gains[l, 1], halves(d_up, d_down)
        )
        vector_sums["g", l, 1] = sums[0]
        vector_sums[l, 2] = sums[1]
        vector_sums[l, 1] = sums[2]
        low = low.reshape(ROWS, D)
        d_out = inner_left(attended, low)
        d_attended = heads_first(inner_right(low, proj_out).astype(BF16))
        d_mixed = attend_back(queries, key_rows, value_rows, d_attended, log_total)
        d_mixed = jnp.stack(d_mixed).transpose(2, 1, 0, 3).reshape(ROWS, 384)
        d_qkv = inner_left(d_mixed, first_in)
        part = matmul(d_mixed, proj_qkv).astype(BF16)
        mixed_sums = jnp.sum(d_mixed.astype(F32), axis=0).reshape(2, 3, 64)
        d_qv = jnp.concatenate([mixed_sums[:, 0], mixed_sums[:, 2]], axis=1)
        bias_sums[l] = (d_up_bias.reshape(2, 256), d_qv.reshape(1, 256))
        weight_part = halves(d_qkv, d_out)
        if l > 0:
            gradient, sums, low, slot_lists["a", l] = backward_call(
                base + 1, part, state, gradient, gains[l, 0], weight_part
            )
            gradient_full = low.reshape(ROWS, D)
            vector_sums[l - 1, 3] = sums[2]
        else:
            gradient, sums = backward_call(base + 1, part, state, gradient, gains[l, 0], last=True)
        vector_sums["g", l, 0] = sums[0]
        vector_sums[l, 0] = sums[1]
    rows = jnp.stack([out_rows, gradient.astype(BF16)])
    order = [("g", l, n) for l in range(LAYERS) for n in range(2)] + [(l, n) for l in range(LAYERS) for n in range(4)]
    vectors = jnp.pad(jnp.stack([vector_sums[key] for key in order]), ((0, 4), (0, 0)))
    bias_rows = jnp.pad(jnp.concatenate([bias_sums[0][0], bias_sums[1][0], bias_sums[0][1], bias_sums[1][1]]), ((0, 2), (0, 0)))
    landed, sums, slot_lists["a", 0] = close_call(9, rows, vectors, bias_rows, weight_part)

    def side(v, width, at):
        return lax.dynamic_slice_in_dim(v, at * width, width, axis=-1)

    whole = side(landed, 64, me.c).transpose(2, 0, 1, 3, 4).reshape(2, 2, ROWS, 64)[:, :, :SEQ].reshape(2, 2 * SEQ, 64)
    owned = {key: jnp.sum(value.astype(F32), axis=0) for key, value in slot_lists.items()}
    vec = side(sums[:12], 8, me.xl * 16 + me.c * 8 + me.d)
    d_fc1_bias = side(sums[16:20].reshape(LAYERS, 512), 32, me.xl * 8 + me.d).reshape(LAYERS, 1, 32)
    d_qv_bias = side(sums[20:22], 16, me.xl * 8 + me.d).reshape(LAYERS, 1, 16)
    return (
        whole[0],
        whole[1].astype(F32),
        jnp.stack([owned["a", l][:192].T for l in range(LAYERS)]),
        jnp.stack([owned["a", l][192:] for l in range(LAYERS)]),
        jnp.stack([owned["b", l][:256].T for l in range(LAYERS)]),
        jnp.stack([owned["b", l][256:] for l in range(LAYERS)]),
        vec[:4].reshape(LAYERS, 2, 1, 8),
        vec[4:].reshape(LAYERS, 4, 1, 8),
        d_qv_bias,
        d_fc1_bias,
    )


def solution(mesh):
    placed = (
        P("dp", "tensor"),
        P(),
        P("dp", "tensor"),
        P(None, "dp", "tensor"),
        P(None, "tensor", "dp"),
        P(None, "dp", "tensor"),
        P(None, "tensor", "dp"),
        P(None, None, "tensor", "dp"),
        P(None, None, "tensor", "dp"),
        P(None, "tensor", "dp"),
        P(None, "tensor", "dp"),
    )
    return jax.shard_map(
        local,
        mesh=mesh,
        in_specs=placed,
        out_specs=(
            P("dp", "tensor"),
            P("dp", "tensor"),
            P(None, "dp", "tensor"),
            P(None, "tensor", "dp"),
            P(None, "dp", "tensor"),
            P(None, "tensor", "dp"),
            P(None, None, "tensor", "dp"),
            P(None, None, "tensor", "dp"),
            P(None, "tensor", "dp"),
            P(None, "tensor", "dp"),
        ),
        check_vma=False,
    )
```

```python
import functools

import jax
import jax.numpy as jnp
from jax import lax
from jax.experimental import pallas as pl
from jax.experimental.pallas import tpu as pltpu
from jax.sharding import PartitionSpec as P

MESH = pl.DeviceIdType.MESH
F32 = jnp.float32
BF16 = jnp.bfloat16
SEQ = 577
LAYERS = 2
BLOCK = 80
ROWS = 8 * BLOCK
D = 1024
EPS = 1e-06
VMEM = pl.BlockSpec(memory_space=pltpu.VMEM)
ANY = pl.BlockSpec(memory_space=pl.ANY)


class Place:
    def __init__(self):
        self.t = lax.axis_index("tensor")
        self.d = lax.axis_index("dp")
        self.z = self.t // 4
        self.xl = (self.t // 2) % 2
        self.c = self.t % 2
        self.w = self.d * 2 + self.xl
        self.j = self.z * 2 + self.c
        self.y = self.d // 2
        self.x = (self.d % 2) * 2 + self.xl
        self.zf, self.zb, self.zo = self.around(self.z)
        self.xf, self.xb, self.xo = self.around(self.x)
        self.yf, self.yb, self.yo = self.around(self.y)

    def around(self, at):
        return (at + 5 - 2 * self.c) % 4, (at + 3 + 2 * self.c) % 4, (at + 2) % 4

    def member(self, z, c):
        return (self.d, z * 4 + self.xl * 2 + c)

    def member_at(self, k):
        j = (self.j + k) % 8
        return self.member(j // 2, j % 2)

    def sharer(self, k):
        w = (self.w + k) % 16
        return (w // 2, self.z * 4 + (w % 2) * 2 + self.c)

    def plane(self, y, x):
        return (y * 2 + x // 2, self.z * 4 + (x % 2) * 2 + self.c)


def remote(src, dst, sems, role, device):
    return pltpu.make_async_remote_copy(
        src_ref=src,
        dst_ref=dst,
        send_sem=sems[0].at[role],
        recv_sem=sems[1].at[role],
        device_id=device,
        device_id_type=MESH,
    )


def greet(devices):
    barrier = pltpu.get_barrier_semaphore()
    for device in devices:
        pl.semaphore_signal(barrier, inc=1, device_id=device, device_id_type=MESH)
    pl.semaphore_wait(barrier, len(devices))


def near(me):
    return [me.member(me.zf, me.c), me.member(me.zb, me.c), me.member(me.z, 1 - me.c)]


def cross(me):
    return [me.plane(me.y, me.xf), me.plane(me.y, me.xb), me.plane(me.yf, me.x), me.plane(me.yb, me.x)]


def nothing(point):
    pass


def gather(out, me, sems, beside=nothing):
    def pair(z, role, device):
        copy = remote(out.at[z, me.c], out.at[z, me.c], sems, role, device)
        copy.start()
        return copy

    ahead, back, other = near(me)
    first = pair(me.z, 0, ahead)
    second = pair(me.z, 1, back)
    over = [pair(me.z, 3, other)]
    beside(3)
    first.wait_recv()
    third = pair(me.zb, 2, ahead)
    over.append(pair(me.zb, 4, other))
    beside(4)
    second.wait_recv()
    over.append(pair(me.zf, 5, other))
    third.wait_recv()
    over.append(pair(me.zo, 6, other))
    beside(5)
    for copy in over:
        copy.wait_recv()
    for copy in [first, second, third] + over:
        copy.wait_send()


def reduce(part, crossed, held, landed, me, sems, beside=nothing):
    ahead, back, other = near(me)
    copies = []
    for role, z in enumerate((me.zo, me.zf, me.zb, me.z)):
        copies.append(remote(part.at[z, 1 - me.c], crossed.at[role], sems, role, other))
        copies[-1].start()
    beside(0)

    def both(role, z):
        copies[role].wait_recv()
        return part[z, me.c].astype(F32) + crossed[role].astype(F32)

    def send(slot, value, device):
        held[slot] = value.astype(BF16)
        copy = remote(held.at[slot], landed.at[slot], sems, 4 + slot, device)
        copy.start()
        copies.append(copy)
        return copy

    long = send(0, both(0, me.zo), ahead)
    short = send(1, both(1, me.zb), back)
    beside(1)
    long.wait_recv()
    last = send(2, both(2, me.zf) + landed[0].astype(F32), ahead)
    beside(2)
    total = both(3, me.z)
    short.wait_recv()
    total = total + landed[1].astype(F32)
    last.wait_recv()
    total = total + landed[2].astype(F32)
    return total, copies


def reduce_scratch():
    return [
        pltpu.VMEM((4, BLOCK, D), BF16),
        pltpu.VMEM((3, BLOCK, D), BF16),
        pltpu.VMEM((3, BLOCK, D), BF16),
        pltpu.SemaphoreType.DMA((7,)),
        pltpu.SemaphoreType.DMA((7,)),
    ]


def pair_sems(count):
    return [pltpu.SemaphoreType.DMA((count,)), pltpu.SemaphoreType.DMA((count,))]


def lanes(at, width):
    return pl.ds(pl.multiple_of(at * 128, 128), width)


class Spread:
    def __init__(self, src, dst, me, sems, local):
        self.src, self.dst, self.me, self.sems = src, dst, me, sems
        half = src.shape[0] // 2
        self.a, self.b = pl.ds(0, half), pl.ds(half, half)
        self.copies = {}
        self.keep = pltpu.make_async_copy(src, dst.at[me.xl, :, lanes((me.x // 2) * 4 + me.y, 128)], local)

    def send(self, role, src, dst, device):
        self.copies[role] = remote(src, dst, self.sems, role, device)
        self.copies[role].start()

    def arrived(self, *roles):
        for role in roles:
            self.copies[role].wait_recv()

    def block(self, y, x, rows):
        return self.dst.at[x % 2, rows, lanes((x // 2) * 4 + y, 128)]

    def row(self, role, y, device):
        for hi in range(2):
            part = self.dst.at[:, self.a, lanes(hi * 4 + y, 128)]
            self.send(role + hi, part, part, device)

    def column(self, role, x, device):
        part = self.dst.at[x % 2, self.b, lanes((x // 2) * 4, 512)]
        self.send(role, part, part, device)

    def step(self, number):
        me = self.me
        xf, xb, yf, yb = cross(me)
        if number == 0:
            self.keep.start()
            for role, rows, device in ((0, self.a, xf), (1, self.a, xb), (2, self.b, yf), (3, self.b, yb)):
                self.send(role, self.src.at[rows], self.block(me.y, me.x, rows), device)
        elif number == 1:
            self.arrived(0, 2)
            self.send(4, self.block(me.y, me.xb, self.a), self.block(me.y, me.xb, self.a), xf)
            self.send(5, self.block(me.yb, me.x, self.b), self.block(me.yb, me.x, self.b), yf)
        elif number == 2:
            self.keep.wait()
            self.arrived(1, 4)
            self.row(6, me.y, yf)
            self.row(8, me.y, yb)
            self.arrived(3, 5)
            self.column(10, me.x, xf)
            self.column(11, me.x, xb)
        elif number == 3:
            self.arrived(6, 7)
            self.row(12, me.yb, yf)
            self.arrived(10)
            self.column(14, me.xb, xf)
        else:
            self.arrived(8, 9, 11, 12, 13, 14)
            for copy in self.copies.values():
                copy.wait_send()


def spread_scratch():
    return pair_sems(15) + [pltpu.SemaphoreType.DMA((1,))]


class Collect:
    def __init__(self, src, out, me, bufs):
        self.src, self.out, self.me = src, out, me
        self.rows_in, self.rows_held, self.cols_in, self.cols_held, self.one_in, self.one_held, *self.sems = bufs
        half = src.shape[1] // 2
        self.a, self.b = pl.ds(0, half), pl.ds(half, half)
        self.half = half
        self.copies = {}

    def send(self, role, src, dst, device):
        self.copies[role] = remote(src, dst, self.sems, role, device)
        self.copies[role].start()

    def arrived(self, *roles):
        for role in roles:
            self.copies[role].wait_recv()

    def column(self, x):
        return self.src.at[x % 2, self.a, lanes((x // 2) * 4, 512)]

    def row(self, y, hi):
        return self.src.at[:, self.b, lanes(hi * 4 + y, 128)]

    def step(self, number):
        me = self.me
        xf, xb, yf, yb = cross(me)
        if number == 0:
            self.send(0, self.column(me.xo), self.cols_in.at[0], xf)
            self.send(1, self.column(me.xb), self.cols_in.at[1], xb)
            for hi in range(2):
                self.send(3 + hi, self.row(me.yo, hi), self.rows_in.at[0, hi], yf)
                self.send(5 + hi, self.row(me.yb, hi), self.rows_in.at[1, hi], yb)
        elif number == 1:
            self.arrived(0)
            self.cols_held[0] = (self.column(me.xf)[...].astype(F32) + self.cols_in[0].astype(F32)).astype(BF16)
            self.send(2, self.cols_held.at[0], self.cols_in.at[2], xf)
            self.arrived(3, 4)
            for hi in range(2):
                self.rows_held[0, hi] = (self.row(me.yf, hi)[...].astype(F32) + self.rows_in[0, hi].astype(F32)).astype(BF16)
                self.send(7 + hi, self.rows_held.at[0, hi], self.rows_in.at[2, hi], yf)
        elif number == 2:
            self.arrived(1, 2)
            self.cols_held[1] = (
                self.column(me.x)[...].astype(F32) + self.cols_in[1].astype(F32) + self.cols_in[2].astype(F32)
            ).astype(BF16)
            self.send(9, self.cols_held.at[1, :, lanes(me.yo, 128)], self.one_in.at[0], yf)
            self.send(10, self.cols_held.at[1, :, lanes(me.yb, 128)], self.one_in.at[1], yb)
            self.arrived(5, 6, 7, 8)
            for hi in range(2):
                self.rows_held[1, hi] = (
                    self.row(me.y, hi)[...].astype(F32)
                    + self.rows_in[1, hi].astype(F32)
                    + self.rows_in[2, hi].astype(F32)
                ).astype(BF16)
            self.send(12, self.rows_held.at[1, me.xo // 2, me.xo % 2], self.one_in.at[3], xf)
            self.send(13, self.rows_held.at[1, me.xb // 2, me.xb % 2], self.one_in.at[4], xb)
        elif number == 3:
            self.arrived(9)
            self.one_held[0] = (self.cols_held[1, :, lanes(me.yf, 128)].astype(F32) + self.one_in[0].astype(F32)).astype(BF16)
            self.send(11, self.one_held.at[0], self.one_in.at[2], yf)
            self.arrived(12)
            self.one_held[1] = (self.rows_held[1, me.xf // 2, me.xf % 2].astype(F32) + self.one_in[3].astype(F32)).astype(BF16)
            self.send(14, self.one_held.at[1], self.one_in.at[5], xf)
        else:
            self.arrived(10, 11)
            self.out[self.a, :] = (
                self.cols_held[1, :, lanes(me.y, 128)].astype(F32)
                + self.one_in[1].astype(F32)
                + self.one_in[2].astype(F32)
            )
            self.arrived(13, 14)
            self.out[self.b, :] = (
                self.rows_held[1, me.x // 2, me.x % 2].astype(F32)
                + self.one_in[4].astype(F32)
                + self.one_in[5].astype(F32)
            )
            for copy in self.copies.values():
                copy.wait_send()


def collect_scratch(n):
    half = n // 2
    return [
        pltpu.VMEM((3, 2, 2, half, 128), BF16),
        pltpu.VMEM((2, 2, 2, half, 128), BF16),
        pltpu.VMEM((3, half, 512), BF16),
        pltpu.VMEM((2, half, 512), BF16),
        pltpu.VMEM((6, half, 128), BF16),
        pltpu.VMEM((2, half, 128), BF16),
    ] + pair_sems(15)


def row_stats(v):
    mean = jnp.sum(v, axis=1, keepdims=True) / D
    square = jnp.sum(v * v, axis=1, keepdims=True) / D
    return mean, lax.rsqrt(square - mean * mean + EPS)


def normed(v, gain, bias):
    mean, inv = row_stats(v)
    return ((v - mean) * inv * gain + bias).astype(BF16)


def call(body, identity, inputs, in_specs, out_shape, out_specs, scratch):
    return pl.pallas_call(
        body,
        out_shape=out_shape,
        in_specs=in_specs,
        out_specs=out_specs,
        scratch_shapes=scratch,
        compiler_params=pltpu.CompilerParams(
            collective_id=identity, has_side_effects=True, vmem_limit_bytes=48 * 1024 * 1024
        ),
    )(*inputs)


def open_kernel(x_ref, w_ref, s_ref, tok_ref, cot_ref, wide_ref, sw_ref, st_ref, y_ref, comp, local, *sems):
    me = Place()
    greet([me.sharer(k) for k in range(1, 16)] + [me.member_at(k) for k in range(1, 8)])
    mine = y_ref.at[me.z, me.c, me.xl]
    swap = remote(x_ref.at[1 - me.xl], mine, sems[0:2], 0, (me.d, me.z * 4 + (1 - me.xl) * 2 + me.c))
    swap.start()
    keep = pltpu.make_async_copy(x_ref.at[me.xl], mine, local.at[0])
    keep.start()
    small = [remote(s_ref, sw_ref.at[me.w], sems[2:4], k - 1, me.sharer(k)) for k in range(1, 16)]
    for copy in small:
        copy.start()
    wide = Spread(w_ref, wide_ref, me, sems[4:6], local.at[1])
    wide.step(0)
    sw_ref[me.w] = s_ref[...]
    keep.wait()
    swap.wait()
    spread = []

    def beside(point):
        wide.step(point - 2)
        if point == 3:
            for copy in small:
                copy.wait()
            for w in range(16):
                comp[w : w + 1, :] = sw_ref[w, 0:1, :]
            st_ref[me.z, me.c] = comp[...]
            for k in range(1, 8):
                spread.append(remote(comp, st_ref.at[me.z, me.c], sems[6:8], k - 1, me.member_at(k)))
                spread[-1].start()

    gather(y_ref, me, sems[8:10], beside)
    low = lax.broadcasted_iota(jnp.int32, (ROWS, 128), 1) < 64
    for z in range(4):
        for p in range(2):
            left, right = y_ref[z, 0, p].astype(F32), y_ref[z, 1, p].astype(F32)
            at = (p * 4 + z) * 128
            tok_ref[:, at : at + 128] = jnp.where(low, left, pltpu.roll(right, 64, 1)).astype(BF16)
            cot_ref[:, at : at + 128] = jnp.where(low, pltpu.roll(left, 64, 1), right).astype(BF16)
    for copy in spread:
        copy.wait()
    wide.step(4)


def open_call(x, w, s):
    return call(
        open_kernel,
        0,
        (x, w, s),
        [VMEM, ANY, VMEM],
        [
            jax.ShapeDtypeStruct((ROWS, D), BF16),
            jax.ShapeDtypeStruct((ROWS, D), BF16),
            jax.ShapeDtypeStruct((2, w.shape[0], D), BF16),
            jax.ShapeDtypeStruct((16, 8, 128), F32),
            jax.ShapeDtypeStruct((4, 2, 16, 128), F32),
        ],
        [VMEM, VMEM, ANY, VMEM, VMEM],
        [pltpu.VMEM((4, 2, 2, ROWS, 128), BF16), pltpu.VMEM((16, 128), F32), pltpu.SemaphoreType.DMA((2,))]
        + pair_sems(1)
        + pair_sems(15)
        + pair_sems(15)
        + pair_sems(7)
        + pair_sems(7),
    )


def forward_kernel(spreads, last, part, state, shift, gain, bias, *refs):
    refs = list(refs)
    w_ref = refs.pop(0) if spreads else None
    new_ref = refs.pop(0)
    out_ref = None if last else refs.pop(0)
    wide_ref = refs.pop(0) if spreads else None
    crossed, held, landed, s0, s1, s2, s3, *rest = refs
    me = Place()
    greet(near(me) + (cross(me) if spreads else []))
    if spreads:
        wide = Spread(w_ref, wide_ref, me, rest[0:2], rest[2].at[0])

    def beside(point):
        if spreads and point in (0, 1, 2, 4):
            wide.step((0, 1, 2, None, 3)[point])

    total, copies = reduce(part, crossed, held, landed, me, (s0, s1), beside)
    value = state[...] + (total + shift[...])
    new_ref[...] = value
    if not last:
        out_ref[me.z, me.c] = normed(value, gain[...], bias[...])
        gather(out_ref, me, (s2, s3), beside)
    for copy in copies:
        copy.wait_send()
    if spreads:
        wide.step(4)


def forward_call(identity, part, state, shift, gain, bias, w=None, last=False):
    out_shape = [jax.ShapeDtypeStruct((BLOCK, D), F32)]
    out_specs = [VMEM]
    scratch = reduce_scratch() + pair_sems(7)
    if not last:
        out_shape.append(jax.ShapeDtypeStruct((4, 2, BLOCK, D), BF16))
        out_specs.append(VMEM)
    inputs = [part.reshape(4, 2, BLOCK, D), state, shift, gain, bias]
    in_specs = [VMEM] * 5
    if w is not None:
        inputs.append(w)
        in_specs.append(ANY)
        out_shape.append(jax.ShapeDtypeStruct((2, w.shape[0], D), BF16))
        out_specs.append(ANY)
        scratch += spread_scratch()
    return call(
        functools.partial(forward_kernel, w is not None, last), identity, inputs, in_specs, out_shape, out_specs, scratch
    )


def weight_product(left, right, out, heads):
    size = left.shape[1] // 2

    def tile(index, carry):
        at = lanes(index * 2, 256)
        value = lax.dot_general(left[...], right[:, at], (((0,), (0,)), ((), ())), preferred_element_type=F32).astype(BF16)
        for p in range(2):
            out[p, pl.ds(heads, size), at] = value[p * size : (p + 1) * size]
        return carry

    lax.fori_loop(0, 4, tile, 0)


def backward_kernel(collects, last, part, base, above, gain, left0, right0, left1, right1, *refs):
    refs = list(refs)
    w_ref = refs.pop(0) if collects else None
    new_ref, sums_ref, weight_ref = refs[:3]
    refs = refs[3:]
    out_ref = None if last else refs.pop(0)
    owned_ref = refs.pop(0) if collects else None
    crossed, held, landed, s0, s1, s2, s3, *rest = refs
    me = Place()
    greet(near(me) + (cross(me) if collects else []))
    if collects:
        slots = Collect(w_ref, owned_ref, me, rest)

    def beside(point):
        if point == 1:
            weight_product(left0, right0, weight_ref, 0)
        if point == (2 if last else 3):
            weight_product(left1, right1, weight_ref, left0.shape[1] // 2)
        if collects and point in (0, 2, 3, 4):
            slots.step((0, None, 1, 2, 3)[point])

    total, copies = reduce(part, crossed, held, landed, me, (s0, s1), beside)
    v = base[...]
    mean, inv = row_stats(v)
    hat = (v - mean) * inv
    weighted = total * gain[...]
    first = jnp.sum(weighted, axis=1, keepdims=True) / D
    second = jnp.sum(weighted * hat, axis=1, keepdims=True) / D
    value = above[...] + inv * (weighted - first - hat * second)
    new_ref[...] = value
    low = value.astype(BF16)
    if not last:
        out_ref[me.z, me.c] = low
    sums_ref[...] = jnp.zeros_like(sums_ref)
    sums_ref[0:1, :] = jnp.sum(total * hat, axis=0, keepdims=True)
    sums_ref[1:2, :] = jnp.sum(total, axis=0, keepdims=True)
    sums_ref[2:3, :] = jnp.sum(low.astype(F32), axis=0, keepdims=True)
    if last:
        beside(3)
        beside(4)
    else:
        gather(out_ref, me, (s2, s3), beside)
    for copy in copies:
        copy.wait_send()
    if collects:
        slots.step(4)


def backward_call(identity, part, base, above, gain, products, w=None, last=False):
    rows = sum(left.shape[1] // 2 for left, _ in products)
    out_shape = [
        jax.ShapeDtypeStruct((BLOCK, D), F32),
        jax.ShapeDtypeStruct((8, D), F32),
        jax.ShapeDtypeStruct((2, rows, D), BF16),
    ]
    scratch = reduce_scratch() + pair_sems(7)
    if not last:
        out_shape.append(jax.ShapeDtypeStruct((4, 2, BLOCK, D), BF16))
    inputs = [part.reshape(4, 2, BLOCK, D), base, above, gain, *products[0], *products[1]]
    if w is not None:
        inputs.append(w)
        out_shape.append(jax.ShapeDtypeStruct((w.shape[1], 128), F32))
        scratch += collect_scratch(w.shape[1])
    return call(
        functools.partial(backward_kernel, w is not None, last),
        identity,
        inputs,
        [VMEM] * len(inputs),
        out_shape,
        [VMEM] * len(out_shape),
        scratch,
    )


def close_kernel(rows_ref, vec_ref, bias_ref, w_ref, out_ref, sum_ref, owned_ref, mine, from_t, from_w, local, *rest):
    me = Place()
    sems, bufs = rest[:6], rest[6:]
    tensor = [(me.d, (me.t + k) % 16) for k in range(1, 16)]
    plane = [((me.d + k) % 8, me.z * 4 + xl * 2 + me.c) for k in range(1, 8) for xl in range(2)]
    greet(tensor + plane)
    slots = Collect(w_ref, owned_ref, me, bufs)
    slots.step(0)

    def vec(z):
        return vec_ref.at[:, :, lanes(z, 128)]

    keep_vec = pltpu.make_async_copy(vec(me.z), from_t.at[me.j], local.at[0])
    keep_vec.start()
    first = []
    for k in range(1, 8):
        j = (me.j + k) % 8
        first.append(remote(vec(j // 2), from_t.at[me.j], sems[0:2], k - 1, me.member(j // 2, j % 2)))
        first[-1].start()

    def features(t):
        return rows_ref.at[:, :, lanes(((t // 2) % 2) * 4 + t // 4, 128)]

    keep_rows = pltpu.make_async_copy(features(me.t), out_ref.at[me.xl, me.j], local.at[1])
    keep_rows.start()
    rows = []
    for k in range(1, 16):
        t = (me.t + k) % 16
        rows.append(remote(features(t), out_ref.at[me.xl, me.j], sems[2:4], k - 1, (me.d, t)))
        rows[-1].start()
    slots.step(1)
    keep_vec.wait()
    for copy in first:
        copy.wait()
    total = from_t[0]
    for j in range(1, 8):
        total = total + from_t[j]
    mine[:, 0:16, :] = total
    mine[:, 16:24, :] = bias_ref[...]
    from_w[me.w] = mine[...]
    second = [remote(mine, from_w.at[me.w], sems[4:6], k - 1, me.sharer(k)) for k in range(1, 16)]
    for copy in second:
        copy.start()
    slots.step(2)
    for copy in second:
        copy.wait()
    total = from_w[0]
    for w in range(1, 16):
        total = total + from_w[w]
    sum_ref[...] = total
    slots.step(3)
    keep_rows.wait()
    for copy in rows:
        copy.wait()
    slots.step(4)


def close_call(identity, rows, vectors, bias, w):
    return call(
        close_kernel,
        identity,
        (rows, vectors, bias, w),
        [VMEM] * 4,
        [
            jax.ShapeDtypeStruct((2, 8, 2, BLOCK, 128), BF16),
            jax.ShapeDtypeStruct((2, 24, 128), F32),
            jax.ShapeDtypeStruct((w.shape[1], 128), F32),
        ],
        [VMEM] * 3,
        [
            pltpu.VMEM((2, 24, 128), F32),
            pltpu.VMEM((8, 2, 16, 128), F32),
            pltpu.VMEM((16, 2, 24, 128), F32),
            pltpu.SemaphoreType.DMA((2,)),
        ]
        + pair_sems(7)
        + pair_sems(15)
        + pair_sems(15)
        + collect_scratch(w.shape[1]),
    )


def matmul(a, b):
    return jnp.dot(a, b, preferred_element_type=F32)


def inner_left(a, b):
    return lax.dot_general(a, b, (((0,), (0,)), ((), ())), preferred_element_type=F32)


def inner_right(a, b):
    return lax.dot_general(a, b, (((1,), (1,)), ((), ())), preferred_element_type=F32)


def scores_of(queries, key_rows):
    scores = 64 ** (-0.5) * jnp.einsum("hqc,hkc->hqk", queries, key_rows, preferred_element_type=F32)
    return jnp.where(lax.broadcasted_iota(jnp.int32, scores.shape, 2) < SEQ, scores, -1e30)


def attend(queries, key_rows, value_rows):
    scores = scores_of(queries, key_rows)
    row_max = jnp.max(scores, axis=-1, keepdims=True)
    shifted = jnp.exp(scores - row_max)
    row_total = jnp.sum(shifted, axis=-1, keepdims=True)
    soft = (shifted / row_total).astype(BF16)
    attended = jnp.einsum("hqk,hkc->hqc", soft, value_rows, preferred_element_type=F32)
    return attended.astype(BF16), row_max + jnp.log(row_total)


def attend_back(queries, key_rows, value_rows, d_attended, log_total):
    soft = jnp.exp(scores_of(queries, key_rows) - log_total)
    d_soft = jnp.einsum("hqc,hkc->hqk", d_attended, value_rows, preferred_element_type=F32)
    d_values = jnp.einsum("hqk,hqc->hkc", soft.astype(BF16), d_attended, preferred_element_type=F32)
    d_scores = (soft * (d_soft - jnp.sum(soft * d_soft, axis=-1, keepdims=True))).astype(BF16)
    d_queries = 64 ** (-0.5) * jnp.einsum("hqk,hkc->hqc", d_scores, key_rows, preferred_element_type=F32)
    d_keys = 64 ** (-0.5) * jnp.einsum("hqk,hqc->hkc", d_scores, queries, preferred_element_type=F32)
    return d_queries.astype(BF16), d_keys.astype(BF16), d_values.astype(BF16)


def gelu(v):
    return 0.5 * v * (1.0 + lax.erf(v * 0.5**0.5))


def gelu_slope(v):
    return 0.5 * (1.0 + lax.erf(v * 0.5**0.5)) + v * jnp.exp(-0.5 * v * v) * (0.5 / jnp.pi) ** 0.5


def heads_first(v):
    return v.reshape(ROWS, 2, -1).transpose(1, 0, 2)


def heads_last(v):
    return v.transpose(1, 0, 2).reshape(ROWS, -1)


def local(
    tokens,
    counts,
    cotangent,
    qkv_weight,
    out_weight,
    fc1_weight,
    fc2_weight,
    norm_gains,
    shifts,
    qv_bias,
    fc1_bias,
):
    me = Place()
    live = me.xl < lax.dynamic_index_in_dim(counts, me.d, keepdims=False)

    def images(v):
        return jnp.pad(v.reshape(2, SEQ, 64), ((0, 0), (0, ROWS - SEQ), (0, 0)))

    x = jnp.concatenate([images(tokens), images(cotangent)], axis=2)
    packs = [
        (
            jnp.concatenate([qkv_weight[l].T, out_weight[l]], axis=0),
            jnp.concatenate([fc1_weight[l].T, fc2_weight[l]], axis=0),
        )
        for l in range(LAYERS)
    ]
    zeros = jnp.zeros((32,), F32)
    small = jnp.stack(
        [
            jnp.concatenate([norm_gains.reshape(32).astype(F32), shifts.reshape(64).astype(F32), zeros]),
            jnp.concatenate([qv_bias.reshape(32).astype(F32), fc1_bias.reshape(64).astype(F32), zeros]),
        ]
    )
    small = jnp.pad(small, ((0, 6), (0, 0)))
    token_rows, gradient_full, wide_a, shared, vectors = open_call(x, packs[0][0], small)
    token_rows = token_rows.astype(F32)
    gradient_full = jnp.where(live, gradient_full, jnp.zeros((), BF16))

    def vector_set(part, count):
        part = part.reshape(4, 2, 8, 2, LAYERS, count, 8)
        return part.transpose(4, 5, 3, 0, 1, 2, 6).reshape(LAYERS, count, 1, D)

    gains = vector_set(vectors[..., :32], 2)
    biases = vector_set(vectors[..., 32:96], 4)
    qv = shared[:, 1, :32].reshape(8, 2, LAYERS, 16).transpose(2, 1, 0, 3).reshape(LAYERS, 2, 128)
    up_bias = shared[:, 1, 32:96].reshape(8, 2, LAYERS, 32).transpose(2, 1, 0, 3).reshape(LAYERS, 512)
    qkv_shift = jnp.concatenate([qv[:, :, :64], jnp.zeros((LAYERS, 2, 64), F32), qv[:, :, 64:]], axis=2)
    qkv_shift = qkv_shift.reshape(LAYERS, 384)

    state = lax.dynamic_slice(token_rows, (me.j * BLOCK, 0), (BLOCK, D))
    first_in = normed(token_rows, gains[0, 0], biases[0, 0])
    saved = []
    wides = []
    for l in range(LAYERS):
        proj_qkv = wide_a[:, :192].reshape(384, D)
        proj_out = wide_a[:, 192:].reshape(128, D)
        mixed = (inner_right(first_in, proj_qkv) + qkv_shift[l]).astype(BF16)
        mixed = mixed.reshape(ROWS, 2, 3, 64).transpose(2, 1, 0, 3)
        queries, key_rows, value_rows = mixed[0], mixed[1], mixed[2]
        attended, log_total = attend(queries, key_rows, value_rows)
        attended = heads_last(attended)
        part = matmul(attended, proj_out).astype(BF16)
        middle, second_in, wide_b = forward_call(
            1 + 2 * l, part, state, biases[l, 1], gains[l, 1], biases[l, 2], packs[l][1]
        )
        second_in = second_in.reshape(ROWS, D)
        proj_up = wide_b[:, :256].reshape(512, D)
        proj_down = wide_b[:, 256:].reshape(512, D)
        pre_act = inner_right(second_in, proj_up) + up_bias[l]
        activated = gelu(pre_act).astype(BF16)
        part = matmul(activated, proj_down).astype(BF16)
        saved.append((state, middle, first_in, queries, key_rows, value_rows, attended, log_total, second_in, pre_act, activated))
        wides.append((proj_qkv, proj_out, proj_up, proj_down))
        if l < LAYERS - 1:
            state, first_in, wide_a = forward_call(
                2 + 2 * l, part, middle, biases[l, 3], gains[l + 1, 0], biases[l + 1, 0], packs[l + 1][0]
            )
            first_in = first_in.reshape(ROWS, D)
        else:
            (state,) = forward_call(2 + 2 * l, part, middle, biases[l, 3], gains[0, 0], biases[0, 0], last=True)
    out_rows = jnp.where(live, state, 0.0).astype(BF16)

    gradient = lax.dynamic_slice(gradient_full, (me.j * BLOCK, 0), (BLOCK, D)).astype(F32)
    vector_sums = {(1, 3): jnp.sum(gradient, axis=0)}
    bias_sums = [None] * LAYERS
    owned = {}
    pending = None
    for l in reversed(range(LAYERS)):
        state, middle, first_in, queries, key_rows, value_rows, attended, log_total, second_in, pre_act, activated = saved[l]
        proj_qkv, proj_out, proj_up, proj_down = wides[l]
        d_pre = (inner_right(gradient_full, proj_down) * gelu_slope(pre_act)).astype(BF16)
        d_up_bias = jnp.sum(d_pre.astype(F32), axis=0)
        part = matmul(d_pre, proj_up).astype(BF16)
        base = 5 + 2 * (LAYERS - 1 - l)
        gradient, sums, weight_part, low, *landed = backward_call(
            base, part, middle, gradient, gains[l, 1], ((d_pre, second_in), (activated, gradient_full)), pending
        )
        if pending is not None:
            owned["a", l + 1] = landed[0]
        pending = weight_part
        vector_sums["g", l, 1] = sums[0]
        vector_sums[l, 2] = sums[1]
        vector_sums[l, 1] = sums[2]
        low = low.reshape(ROWS, D)
        d_attended = heads_first(inner_right(low, proj_out).astype(BF16))
        d_mixed = attend_back(queries, key_rows, value_rows, d_attended, log_total)
        d_mixed = jnp.stack(d_mixed).transpose(2, 1, 0, 3).reshape(ROWS, 384)
        part = matmul(d_mixed, proj_qkv).astype(BF16)
        mixed_sums = jnp.sum(d_mixed.astype(F32), axis=0).reshape(2, 3, 64)
        d_qv = jnp.concatenate([mixed_sums[:, 0], mixed_sums[:, 2]], axis=1)
        bias_sums[l] = (d_up_bias.reshape(4, 128), d_qv)
        gradient, sums, weight_part, *rest = backward_call(
            base + 1, part, state, gradient, gains[l, 0], ((d_mixed, first_in), (attended, low)), pending, last=l == 0
        )
        owned["b", l] = rest[-1]
        pending = weight_part
        if l > 0:
            gradient_full = rest[0].reshape(ROWS, D)
            vector_sums[l - 1, 3] = sums[2]
        vector_sums["g", l, 0] = sums[0]
        vector_sums[l, 0] = sums[1]
    rows = jnp.stack([out_rows, gradient.astype(BF16)])
    order = [("g", l, n) for l in range(LAYERS) for n in range(2)] + [(l, n) for l in range(LAYERS) for n in range(4)]
    vectors = jnp.pad(jnp.stack([vector_sums[key] for key in order]), ((0, 4), (0, 0)))
    vectors = vectors.reshape(16, 2, 512).transpose(1, 0, 2)
    bias_rows = jnp.concatenate([bias_sums[0][0], bias_sums[1][0], bias_sums[0][1], bias_sums[1][1], jnp.zeros((4, 128), F32)])
    landed, sums, owned["a", 0] = close_call(9, rows, vectors, bias_rows.reshape(2, 8, 128), pending)

    def side(v, width, at):
        return lax.dynamic_slice_in_dim(v, at * width, width, axis=-1)

    whole = side(landed, 64, me.c).transpose(2, 0, 1, 3, 4).reshape(2, 2, ROWS, 64)[:, :, :SEQ].reshape(2, 2 * SEQ, 64)
    vec = side(lax.dynamic_index_in_dim(sums, me.xl, keepdims=False)[:12], 8, me.c * 8 + me.d)
    bias_rows = sums[:, 16:].reshape(16, 128)
    d_fc1_bias = side(bias_rows[:8].reshape(LAYERS, 512), 32, me.xl * 8 + me.d).reshape(LAYERS, 1, 32)
    d_qv_bias = side(bias_rows[8:12].reshape(LAYERS, 256), 16, me.xl * 8 + me.d).reshape(LAYERS, 1, 16)
    return (
        whole[0],
        whole[1].astype(F32),
        jnp.stack([owned["a", l][:192].T for l in range(LAYERS)]),
        jnp.stack([owned["a", l][192:] for l in range(LAYERS)]),
        jnp.stack([owned["b", l][:256].T for l in range(LAYERS)]),
        jnp.stack([owned["b", l][256:] for l in range(LAYERS)]),
        vec[:4].reshape(LAYERS, 2, 1, 8),
        vec[4:].reshape(LAYERS, 4, 1, 8),
        d_qv_bias,
        d_fc1_bias,
    )


def solution(mesh):
    placed = (
        P("dp", "tensor"),
        P(),
        P("dp", "tensor"),
        P(None, "dp", "tensor"),
        P(None, "tensor", "dp"),
        P(None, "dp", "tensor"),
        P(None, "tensor", "dp"),
        P(None, None, "tensor", "dp"),
        P(None, None, "tensor", "dp"),
        P(None, "tensor", "dp"),
        P(None, "tensor", "dp"),
    )
    return jax.shard_map(
        local,
        mesh=mesh,
        in_specs=placed,
        out_specs=(
            P("dp", "tensor"),
            P("dp", "tensor"),
            P(None, "dp", "tensor"),
            P(None, "tensor", "dp"),
            P(None, "dp", "tensor"),
            P(None, "tensor", "dp"),
            P(None, None, "tensor", "dp"),
            P(None, None, "tensor", "dp"),
            P(None, "tensor", "dp"),
            P(None, "tensor", "dp"),
        ),
        check_vma=False,
    )
```

```python
import functools

import jax
import jax.numpy as jnp
from jax import lax
from jax.experimental import pallas as pl
from jax.experimental.pallas import tpu as pltpu
from jax.sharding import PartitionSpec as P

MESH = pl.DeviceIdType.MESH
F32 = jnp.float32
BF16 = jnp.bfloat16
SEQ = 577
LAYERS = 2
BLOCK = 80
ROWS = 8 * BLOCK
D = 1024
EPS = 1e-06
VMEM = pl.BlockSpec(memory_space=pltpu.VMEM)
ANY = pl.BlockSpec(memory_space=pl.ANY)


class Place:
    def __init__(self):
        self.t = lax.axis_index("tensor")
        self.d = lax.axis_index("dp")
        self.z = self.t // 4
        self.xl = (self.t // 2) % 2
        self.c = self.t % 2
        self.w = self.d * 2 + self.xl
        self.j = self.z * 2 + self.c
        self.y = self.d // 2
        self.x = (self.d % 2) * 2 + self.xl
        self.zf, self.zb, self.zo = self.around(self.z)
        self.xf, self.xb, self.xo = self.around(self.x)
        self.yf, self.yb, self.yo = self.around(self.y)

    def around(self, at):
        return (at + 5 - 2 * self.c) % 4, (at + 3 + 2 * self.c) % 4, (at + 2) % 4

    def member(self, z, c):
        return (self.d, z * 4 + self.xl * 2 + c)

    def member_at(self, k):
        j = (self.j + k) % 8
        return self.member(j // 2, j % 2)

    def sharer(self, k):
        w = (self.w + k) % 16
        return (w // 2, self.z * 4 + (w % 2) * 2 + self.c)

    def plane(self, y, x):
        return (y * 2 + x // 2, self.z * 4 + (x % 2) * 2 + self.c)


def remote(src, dst, sems, role, device):
    return pltpu.make_async_remote_copy(
        src_ref=src,
        dst_ref=dst,
        send_sem=sems[0].at[role],
        recv_sem=sems[1].at[role],
        device_id=device,
        device_id_type=MESH,
    )


def greet(devices):
    barrier = pltpu.get_barrier_semaphore()
    for device in devices:
        pl.semaphore_signal(barrier, inc=1, device_id=device, device_id_type=MESH)
    pl.semaphore_wait(barrier, len(devices))


def near(me):
    return [me.member(me.zf, me.c), me.member(me.zb, me.c), me.member(me.z, 1 - me.c)]


def cross(me):
    return [me.plane(me.y, me.xf), me.plane(me.y, me.xb), me.plane(me.yf, me.x), me.plane(me.yb, me.x)]


def nothing(point):
    pass


def gather(out, me, sems, beside=nothing):
    def pair(z, role, device):
        copy = remote(out.at[z, me.c], out.at[z, me.c], sems, role, device)
        copy.start()
        return copy

    ahead, back, other = near(me)
    first = pair(me.z, 0, ahead)
    second = pair(me.z, 1, back)
    over = [pair(me.z, 3, other)]
    beside(3)
    first.wait_recv()
    third = pair(me.zb, 2, ahead)
    over.append(pair(me.zb, 4, other))
    beside(4)
    second.wait_recv()
    over.append(pair(me.zf, 5, other))
    third.wait_recv()
    over.append(pair(me.zo, 6, other))
    beside(5)
    for copy in over:
        copy.wait_recv()
    for copy in [first, second, third] + over:
        copy.wait_send()


def reduce(part, crossed, held, landed, me, sems, beside=nothing):
    ahead, back, other = near(me)
    copies = []
    for role, z in enumerate((me.zo, me.zf, me.zb, me.z)):
        copies.append(remote(part.at[z, 1 - me.c], crossed.at[role], sems, role, other))
        copies[-1].start()
    beside(0)

    def both(role, z):
        copies[role].wait_recv()
        return part[z, me.c].astype(F32) + crossed[role].astype(F32)

    def send(slot, value, device):
        held[slot] = value.astype(BF16)
        copy = remote(held.at[slot], landed.at[slot], sems, 4 + slot, device)
        copy.start()
        copies.append(copy)
        return copy

    long = send(0, both(0, me.zo), ahead)
    short = send(1, both(1, me.zb), back)
    beside(1)
    long.wait_recv()
    last = send(2, both(2, me.zf) + landed[0].astype(F32), ahead)
    beside(2)
    total = both(3, me.z)
    short.wait_recv()
    total = total + landed[1].astype(F32)
    last.wait_recv()
    total = total + landed[2].astype(F32)
    return total, copies


def reduce_scratch():
    return [
        pltpu.VMEM((4, BLOCK, D), BF16),
        pltpu.VMEM((3, BLOCK, D), BF16),
        pltpu.VMEM((3, BLOCK, D), BF16),
        pltpu.SemaphoreType.DMA((7,)),
        pltpu.SemaphoreType.DMA((7,)),
    ]


def pair_sems(count):
    return [pltpu.SemaphoreType.DMA((count,)), pltpu.SemaphoreType.DMA((count,))]


def lanes(at, width):
    return pl.ds(pl.multiple_of(at * 128, 128), width)


class Spread:
    def __init__(self, src, dst, me, sems, local):
        self.src, self.dst, self.me, self.sems = src, dst, me, sems
        half = src.shape[0] // 2
        self.a, self.b = pl.ds(0, half), pl.ds(half, half)
        self.copies = {}
        self.keep = pltpu.make_async_copy(src, dst.at[me.xl, :, lanes((me.x // 2) * 4 + me.y, 128)], local)

    def send(self, role, src, dst, device):
        self.copies[role] = remote(src, dst, self.sems, role, device)
        self.copies[role].start()

    def arrived(self, *roles):
        for role in roles:
            self.copies[role].wait_recv()

    def block(self, y, x, rows):
        return self.dst.at[x % 2, rows, lanes((x // 2) * 4 + y, 128)]

    def row(self, role, y, device):
        for hi in range(2):
            part = self.dst.at[:, self.a, lanes(hi * 4 + y, 128)]
            self.send(role + hi, part, part, device)

    def column(self, role, x, device):
        part = self.dst.at[x % 2, self.b, lanes((x // 2) * 4, 512)]
        self.send(role, part, part, device)

    def step(self, number):
        me = self.me
        xf, xb, yf, yb = cross(me)
        if number == 0:
            self.keep.start()
            for role, rows, device in ((0, self.a, xf), (1, self.a, xb), (2, self.b, yf), (3, self.b, yb)):
                self.send(role, self.src.at[rows], self.block(me.y, me.x, rows), device)
        elif number == 1:
            self.arrived(0, 2)
            self.send(4, self.block(me.y, me.xb, self.a), self.block(me.y, me.xb, self.a), xf)
            self.send(5, self.block(me.yb, me.x, self.b), self.block(me.yb, me.x, self.b), yf)
        elif number == 2:
            self.keep.wait()
            self.arrived(1, 4)
            self.row(6, me.y, yf)
            self.row(8, me.y, yb)
            self.arrived(3, 5)
            self.column(10, me.x, xf)
            self.column(11, me.x, xb)
        elif number == 3:
            self.arrived(6, 7)
            self.row(12, me.yb, yf)
            self.arrived(10)
            self.column(14, me.xb, xf)
        else:
            self.arrived(8, 9, 11, 12, 13, 14)
            for copy in self.copies.values():
                copy.wait_send()


def spread_scratch():
    return pair_sems(15) + [pltpu.SemaphoreType.DMA((1,))]


class Collect:
    def __init__(self, src, out, me, bufs):
        self.src, self.out, self.me = src, out, me
        self.rows_in, self.rows_held, self.cols_in, self.cols_held, self.one_in, self.one_held, *self.sems = bufs
        half = src.shape[1] // 2
        self.a, self.b = pl.ds(0, half), pl.ds(half, half)
        self.half = half
        self.copies = {}

    def send(self, role, src, dst, device):
        self.copies[role] = remote(src, dst, self.sems, role, device)
        self.copies[role].start()

    def arrived(self, *roles):
        for role in roles:
            self.copies[role].wait_recv()

    def column(self, x):
        return self.src.at[x % 2, self.a, lanes((x // 2) * 4, 512)]

    def row(self, y, hi):
        return self.src.at[:, self.b, lanes(hi * 4 + y, 128)]

    def step(self, number):
        me = self.me
        xf, xb, yf, yb = cross(me)
        if number == 0:
            self.send(0, self.column(me.xo), self.cols_in.at[0], xf)
            self.send(1, self.column(me.xb), self.cols_in.at[1], xb)
            for hi in range(2):
                self.send(3 + hi, self.row(me.yo, hi), self.rows_in.at[0, hi], yf)
                self.send(5 + hi, self.row(me.yb, hi), self.rows_in.at[1, hi], yb)
        elif number == 1:
            self.arrived(0)
            self.cols_held[0] = (self.column(me.xf)[...].astype(F32) + self.cols_in[0].astype(F32)).astype(BF16)
            self.send(2, self.cols_held.at[0], self.cols_in.at[2], xf)
            self.arrived(3, 4)
            for hi in range(2):
                self.rows_held[0, hi] = (self.row(me.yf, hi)[...].astype(F32) + self.rows_in[0, hi].astype(F32)).astype(BF16)
                self.send(7 + hi, self.rows_held.at[0, hi], self.rows_in.at[2, hi], yf)
        elif number == 2:
            self.arrived(1, 2)
            self.cols_held[1] = (
                self.column(me.x)[...].astype(F32) + self.cols_in[1].astype(F32) + self.cols_in[2].astype(F32)
            ).astype(BF16)
            self.send(9, self.cols_held.at[1, :, lanes(me.yo, 128)], self.one_in.at[0], yf)
            self.send(10, self.cols_held.at[1, :, lanes(me.yb, 128)], self.one_in.at[1], yb)
            self.arrived(5, 6, 7, 8)
            for hi in range(2):
                self.rows_held[1, hi] = (
                    self.row(me.y, hi)[...].astype(F32)
                    + self.rows_in[1, hi].astype(F32)
                    + self.rows_in[2, hi].astype(F32)
                ).astype(BF16)
            self.send(12, self.rows_held.at[1, me.xo // 2, me.xo % 2], self.one_in.at[3], xf)
            self.send(13, self.rows_held.at[1, me.xb // 2, me.xb % 2], self.one_in.at[4], xb)
        elif number == 3:
            self.arrived(9)
            self.one_held[0] = (self.cols_held[1, :, lanes(me.yf, 128)].astype(F32) + self.one_in[0].astype(F32)).astype(BF16)
            self.send(11, self.one_held.at[0], self.one_in.at[2], yf)
            self.arrived(12)
            self.one_held[1] = (self.rows_held[1, me.xf // 2, me.xf % 2].astype(F32) + self.one_in[3].astype(F32)).astype(BF16)
            self.send(14, self.one_held.at[1], self.one_in.at[5], xf)
        else:
            self.arrived(10, 11)
            self.out[self.a, :] = (
                self.cols_held[1, :, lanes(me.y, 128)].astype(F32)
                + self.one_in[1].astype(F32)
                + self.one_in[2].astype(F32)
            )
            self.arrived(13, 14)
            self.out[self.b, :] = (
                self.rows_held[1, me.x // 2, me.x % 2].astype(F32)
                + self.one_in[4].astype(F32)
                + self.one_in[5].astype(F32)
            )
            for copy in self.copies.values():
                copy.wait_send()


def collect_scratch(n):
    half = n // 2
    return [
        pltpu.VMEM((3, 2, 2, half, 128), BF16),
        pltpu.VMEM((2, 2, 2, half, 128), BF16),
        pltpu.VMEM((3, half, 512), BF16),
        pltpu.VMEM((2, half, 512), BF16),
        pltpu.VMEM((6, half, 128), BF16),
        pltpu.VMEM((2, half, 128), BF16),
    ] + pair_sems(15)


def row_stats(v):
    mean = jnp.sum(v, axis=1, keepdims=True) / D
    square = jnp.sum(v * v, axis=1, keepdims=True) / D
    return mean, lax.rsqrt(square - mean * mean + EPS)


def normed(v, gain, bias):
    mean, inv = row_stats(v)
    return ((v - mean) * inv * gain + bias).astype(BF16)


def call(body, identity, inputs, in_specs, out_shape, out_specs, scratch):
    return pl.pallas_call(
        body,
        out_shape=out_shape,
        in_specs=in_specs,
        out_specs=out_specs,
        scratch_shapes=scratch,
        compiler_params=pltpu.CompilerParams(
            collective_id=identity, has_side_effects=True, vmem_limit_bytes=48 * 1024 * 1024
        ),
    )(*inputs)


def half_swap(left, right, low):
    return jnp.where(low, left, pltpu.roll(right, 64, 1)), jnp.where(low, pltpu.roll(left, 64, 1), right)


def open_kernel(
    counts_ref, x_ref, w_ref, s_ref, in_ref, state_ref, cot_ref, above_ref, wide_ref, vec_ref, qkv_ref, up_ref,
    y_ref, tok_ref, sw_ref, st_ref, comp, local, *sems
):
    me = Place()
    greet([me.sharer(k) for k in range(1, 16)] + [me.member_at(k) for k in range(1, 8)])
    mine = y_ref.at[me.z, me.c, me.xl]
    swap = remote(x_ref.at[1 - me.xl], mine, sems[0:2], 0, (me.d, me.z * 4 + (1 - me.xl) * 2 + me.c))
    swap.start()
    keep = pltpu.make_async_copy(x_ref.at[me.xl], mine, local.at[0])
    keep.start()
    small = [remote(s_ref, sw_ref.at[me.w], sems[2:4], k - 1, me.sharer(k)) for k in range(1, 16)]
    for copy in small:
        copy.start()
    wide = Spread(w_ref, wide_ref, me, sems[4:6], local.at[1])
    wide.step(0)
    sw_ref[me.w] = s_ref[...]
    keep.wait()
    swap.wait()
    spread = []
    low = lax.broadcasted_iota(jnp.int32, (16, 128), 1) < 64

    def beside(point):
        wide.step(point - 2)
        if point == 3:
            for copy in small:
                copy.wait()
            comp[...] = sum(pltpu.roll(sw_ref[w], (w % 2) * 64 + (w // 2) * 8, 1) for w in range(16))
            st_ref[me.z, me.c] = comp[...]
            for k in range(1, 8):
                spread.append(remote(comp, st_ref.at[me.z, me.c], sems[6:8], k - 1, me.member_at(k)))
                spread[-1].start()
            pair = []
            for p in range(2):
                pair.append(sum(pltpu.roll(sw_ref[2 * d + p], d * 16, 1) for d in range(8)))
                for k in range(2):
                    value = sum(pltpu.roll(sw_ref[2 * d + p], (d % 4) * 32, 1) for d in range(4 * k, 4 * k + 4))
                    up_ref[:, (p * 2 + k) * 128 : (p * 2 + k + 1) * 128] = value
            swapped = half_swap(*pair, low)
            qkv_ref[:, :128] = jnp.where(low, pair[0], 0.0)
            qkv_ref[:, 128:256] = jnp.where(low, pltpu.roll(pair[0], 64, 1), swapped[0])
            qkv_ref[:, 256:] = jnp.where(low, 0.0, pair[1])

    gather(y_ref, me, sems[8:10], beside)
    for copy in spread:
        copy.wait()
    for z in range(4):
        for p, value in enumerate(half_swap(st_ref[z, 0], st_ref[z, 1], low)):
            vec_ref[:, (p * 4 + z) * 128 : (p * 4 + z + 1) * 128] = value
    live = jnp.where(me.xl < counts_ref[me.d], 1.0, 0.0)
    low_rows = lax.broadcasted_iota(jnp.int32, (BLOCK, 128), 1) < 64

    def rows(index, carry):
        at = pl.ds(pl.multiple_of(index * BLOCK, BLOCK), BLOCK)
        for z in range(4):
            for p in range(2):
                token, cot = half_swap(y_ref[z, 0, p, at].astype(F32), y_ref[z, 1, p, at].astype(F32), low_rows)
                place = pl.ds((p * 4 + z) * 128, 128)
                tok_ref[at, place] = token
                cot_ref[at, place] = (cot * live).astype(BF16)
        in_ref[at, :] = normed(tok_ref[at, :], vec_ref[0:1, :], vec_ref[4:5, :])
        return carry

    lax.fori_loop(0, 8, rows, 0)
    at = pl.ds(pl.multiple_of(me.j * BLOCK, BLOCK), BLOCK)
    state_ref[...] = tok_ref[at, :]
    above_ref[...] = cot_ref[at, :].astype(F32)
    wide.step(4)


def open_call(counts, x, w, s):
    return call(
        open_kernel,
        0,
        (counts, x, w, s),
        [pl.BlockSpec(memory_space=pltpu.SMEM), VMEM, ANY, VMEM],
        [
            jax.ShapeDtypeStruct((ROWS, D), BF16),
            jax.ShapeDtypeStruct((BLOCK, D), F32),
            jax.ShapeDtypeStruct((ROWS, D), BF16),
            jax.ShapeDtypeStruct((BLOCK, D), F32),
            jax.ShapeDtypeStruct((2, w.shape[0], D), BF16),
            jax.ShapeDtypeStruct((16, D), F32),
            jax.ShapeDtypeStruct((16, 384), F32),
            jax.ShapeDtypeStruct((16, 512), F32),
        ],
        [VMEM] * 4 + [ANY] + [VMEM] * 3,
        [
            pltpu.VMEM((4, 2, 2, ROWS, 128), BF16),
            pltpu.VMEM((ROWS, D), F32),
            pltpu.VMEM((16, 16, 128), F32),
            pltpu.VMEM((4, 2, 16, 128), F32),
            pltpu.VMEM((16, 128), F32),
            pltpu.SemaphoreType.DMA((2,)),
        ]
        + pair_sems(1)
        + pair_sems(15)
        + pair_sems(15)
        + pair_sems(7)
        + pair_sems(7),
    )


def forward_kernel(spreads, last, part, state, shift, gain, bias, *refs):
    refs = list(refs)
    w_ref = refs.pop(0) if spreads else None
    new_ref = refs.pop(0)
    out_ref = None if last else refs.pop(0)
    wide_ref = refs.pop(0) if spreads else None
    crossed, held, landed, s0, s1, s2, s3, *rest = refs
    me = Place()
    greet(near(me) + (cross(me) if spreads else []))
    if spreads:
        wide = Spread(w_ref, wide_ref, me, rest[0:2], rest[2].at[0])

    def beside(point):
        if spreads and point in (0, 1, 2, 4):
            wide.step((0, 1, 2, None, 3)[point])

    total, copies = reduce(part, crossed, held, landed, me, (s0, s1), beside)
    value = state[...] + (total + shift[...])
    new_ref[...] = value
    if not last:
        out_ref[me.z, me.c] = normed(value, gain[...], bias[...])
        gather(out_ref, me, (s2, s3), beside)
    for copy in copies:
        copy.wait_send()
    if spreads:
        wide.step(4)


def forward_call(identity, part, state, shift, gain, bias, w=None, last=False):
    out_shape = [jax.ShapeDtypeStruct((BLOCK, D), F32)]
    out_specs = [VMEM]
    scratch = reduce_scratch() + pair_sems(7)
    if not last:
        out_shape.append(jax.ShapeDtypeStruct((4, 2, BLOCK, D), BF16))
        out_specs.append(VMEM)
    inputs = [part.reshape(4, 2, BLOCK, D), state, shift, gain, bias]
    in_specs = [VMEM] * 5
    if w is not None:
        inputs.append(w)
        in_specs.append(ANY)
        out_shape.append(jax.ShapeDtypeStruct((2, w.shape[0], D), BF16))
        out_specs.append(ANY)
        scratch += spread_scratch()
    return call(
        functools.partial(forward_kernel, w is not None, last), identity, inputs, in_specs, out_shape, out_specs, scratch
    )


def weight_product(left, right, out, heads):
    size = left.shape[1] // 2

    def tile(index, carry):
        at = lanes(index * 2, 256)
        value = lax.dot_general(left[...], right[:, at], (((0,), (0,)), ((), ())), preferred_element_type=F32).astype(BF16)
        for p in range(2):
            out[p, pl.ds(heads, size), at] = value[p * size : (p + 1) * size]
        return carry

    lax.fori_loop(0, 4, tile, 0)


def norm_back(total, base, above, gain):
    mean, inv = row_stats(base)
    hat = (base - mean) * inv
    weighted = total * gain
    first = jnp.sum(weighted, axis=1, keepdims=True) / D
    second = jnp.sum(weighted * hat, axis=1, keepdims=True) / D
    return above + inv * (weighted - first - hat * second), total * hat


def backward_kernel(collects, part, base, above, gain, left0, right0, left1, right1, *refs):
    refs = list(refs)
    w_ref = refs.pop(0) if collects else None
    new_ref, sums_ref, weight_ref, out_ref = refs[:4]
    refs = refs[4:]
    owned_ref = refs.pop(0) if collects else None
    crossed, held, landed, s0, s1, s2, s3, *rest = refs
    me = Place()
    greet(near(me) + (cross(me) if collects else []))
    if collects:
        slots = Collect(w_ref, owned_ref, me, rest)

    def beside(point):
        if point == 1:
            weight_product(left0, right0, weight_ref, 0)
        if point == 3:
            weight_product(left1, right1, weight_ref, left0.shape[1] // 2)
        if collects and point in (0, 2, 3, 4):
            slots.step((0, None, 1, 2, 3)[point])

    total, copies = reduce(part, crossed, held, landed, me, (s0, s1), beside)
    value, by_hat = norm_back(total, base[...], above[...], gain[...])
    new_ref[...] = value
    low = value.astype(BF16)
    out_ref[me.z, me.c] = low
    for row, each in enumerate((by_hat, total, low.astype(F32), above[...])):
        sums_ref[row : row + 1, :] = jnp.sum(each, axis=0, keepdims=True)
    sums_ref[4:8, :] = jnp.zeros((4, D), F32)
    gather(out_ref, me, (s2, s3), beside)
    for copy in copies:
        copy.wait_send()
    if collects:
        slots.step(4)


def backward_call(identity, part, base, above, gain, products, w=None):
    rows = sum(left.shape[1] // 2 for left, _ in products)
    out_shape = [
        jax.ShapeDtypeStruct((BLOCK, D), F32),
        jax.ShapeDtypeStruct((8, D), F32),
        jax.ShapeDtypeStruct((2, rows, D), BF16),
        jax.ShapeDtypeStruct((4, 2, BLOCK, D), BF16),
    ]
    scratch = reduce_scratch() + pair_sems(7)
    inputs = [part.reshape(4, 2, BLOCK, D), base, above, gain, *products[0], *products[1]]
    if w is not None:
        inputs.append(w)
        out_shape.append(jax.ShapeDtypeStruct((w.shape[1], 128), F32))
        scratch += collect_scratch(w.shape[1])
    return call(
        functools.partial(backward_kernel, w is not None),
        identity,
        inputs,
        [VMEM] * len(inputs),
        out_shape,
        [VMEM] * len(out_shape),
        scratch,
    )


def close_kernel(
    part, base, above, gain, left0, right0, left1, right1, w_ref, rows_ref, up_sums, mid_sums, down_sums, bias_ref,
    out_ref, grad_ref, vec_out, bias_out, owned_w, owned_p,
    product, low_ref, vec_ref, from_t, mine, from_w, from_b, local, *rest
):
    me = Place()
    crossed, held, landed, s0, s1 = rest[:5]
    sems, rest = rest[5:15], rest[15:]
    tensor = [(me.d, (me.t + k) % 16) for k in range(1, 16)]
    plane = [((me.d + k) % 8, me.z * 4 + xl * 2 + me.c) for k in range(1, 8) for xl in range(2)]
    greet(tensor + plane)
    slots_w = Collect(w_ref, owned_w, me, rest[:8])
    slots_p = Collect(product, owned_p, me, rest[8:])

    def scatter(source, target, sems, local):
        def features(t):
            return source.at[:, lanes(((t // 2) % 2) * 4 + t // 4, 128)]

        keep = pltpu.make_async_copy(features(me.t), target.at[me.xl, me.j], local)
        keep.start()
        copies = []
        for k in range(1, 16):
            t = (me.t + k) % 16
            copies.append(remote(features(t), target.at[me.xl, me.j], sems, k - 1, (me.d, t)))
            copies[-1].start()
        return keep, copies

    def share(source, target, sems, local):
        keep = pltpu.make_async_copy(source.at[me.xl], target.at[me.w], local)
        keep.start()
        copies = []
        for k in range(1, 16):
            xl = (me.w + k) % 2
            copies.append(remote(source.at[xl], target.at[me.w], sems, k - 1, me.sharer(k)))
            copies[-1].start()
        return keep, copies

    def finish(started):
        started[0].wait()
        for copy in started[1]:
            copy.wait()

    open_ends = []

    def beside(point):
        if point == 0:
            slots_w.step(0)
        elif point == 1:
            weight_product(left0, right0, product, 0)
            weight_product(left1, right1, product, left0.shape[1] // 2)
            slots_p.step(0)
        else:
            slots_w.step(1)
            open_ends.append(scatter(rows_ref, out_ref, sems[0:2], local.at[0]))
            open_ends.append(share(bias_ref, from_b, sems[2:4], local.at[1]))

    total, copies = reduce(part, crossed, held, landed, me, (s0, s1), beside)
    value, by_hat = norm_back(total, base[...], above[...], gain[...])
    low_ref[...] = value.astype(BF16)
    open_ends.append(scatter(low_ref, grad_ref, sems[4:6], local.at[2]))
    own = [jnp.sum(each, axis=0, keepdims=True) for each in (by_hat, total)]
    up, mid, down = ([ref[row : row + 1, :] for row in range(4)] for ref in (up_sums, mid_sums, down_sums))
    order = (own[0], down[0], mid[0], up[0], own[1], down[2], down[1], mid[2], mid[1], up[2], up[1], up[3])
    vec_ref[...] = jnp.zeros_like(vec_ref)
    for row, each in enumerate(order):
        for p in range(2):
            vec_ref[p, row : row + 1, :] = each[:, p * 512 : (p + 1) * 512]

    def vec(z):
        return vec_ref.at[:, :, lanes(z, 128)]

    keep = pltpu.make_async_copy(vec(me.z), from_t.at[me.j], local.at[3])
    keep.start()
    first = []
    for k in range(1, 8):
        j = (me.j + k) % 8
        first.append(remote(vec(j // 2), from_t.at[me.j], sems[6:8], k - 1, me.member(j // 2, j % 2)))
        first[-1].start()
    slots_w.step(2)
    slots_p.step(1)
    finish((keep, first))
    mine[...] = sum(from_t[j] for j in range(8))
    second = share(mine, from_w, sems[8:10], local.at[4])
    slots_w.step(3)
    slots_p.step(2)
    finish(second)
    vec_out[...] = sum(from_w[w] for w in range(16))
    slots_w.step(4)
    slots_p.step(3)
    for started in open_ends:
        finish(started)
    bias_out[...] = sum(from_b[w] for w in range(16))
    for copy in copies:
        copy.wait_send()
    slots_p.step(4)


def close_call(identity, part, base, above, gain, products, w, rows, sums, bias):
    size = sum(left.shape[1] // 2 for left, _ in products)
    inputs = [part.reshape(4, 2, BLOCK, D), base, above, gain, *products[0], *products[1], w, rows, *sums, bias]
    return call(
        close_kernel,
        identity,
        inputs,
        [VMEM] * len(inputs),
        [
            jax.ShapeDtypeStruct((2, 8, BLOCK, 128), BF16),
            jax.ShapeDtypeStruct((2, 8, BLOCK, 128), BF16),
            jax.ShapeDtypeStruct((16, 128), F32),
            jax.ShapeDtypeStruct((8, 128), F32),
            jax.ShapeDtypeStruct((w.shape[1], 128), F32),
            jax.ShapeDtypeStruct((size, 128), F32),
        ],
        [VMEM] * 6,
        [
            pltpu.VMEM((2, size, D), BF16),
            pltpu.VMEM((BLOCK, D), BF16),
            pltpu.VMEM((2, 16, 512), F32),
            pltpu.VMEM((8, 2, 16, 128), F32),
            pltpu.VMEM((2, 16, 128), F32),
            pltpu.VMEM((16, 16, 128), F32),
            pltpu.VMEM((16, 8, 128), F32),
            pltpu.SemaphoreType.DMA((5,)),
        ]
        + reduce_scratch()
        + pair_sems(15) * 3
        + pair_sems(7)
        + pair_sems(15)
        + collect_scratch(w.shape[1])
        + collect_scratch(size),
    )


def matmul(a, b):
    return jnp.dot(a, b, preferred_element_type=F32)


def inner_left(a, b):
    return lax.dot_general(a, b, (((0,), (0,)), ((), ())), preferred_element_type=F32)


def inner_right(a, b):
    return lax.dot_general(a, b, (((1,), (1,)), ((), ())), preferred_element_type=F32)


def scores_of(queries, key_rows):
    scores = 64 ** (-0.5) * jnp.einsum("hqc,hkc->hqk", queries, key_rows, preferred_element_type=F32)
    return jnp.where(lax.broadcasted_iota(jnp.int32, scores.shape, 2) < SEQ, scores, -1e30)


def attend(queries, key_rows, value_rows):
    scores = scores_of(queries, key_rows)
    row_max = jnp.max(scores, axis=-1, keepdims=True)
    shifted = jnp.exp(scores - row_max)
    row_total = jnp.sum(shifted, axis=-1, keepdims=True)
    soft = (shifted / row_total).astype(BF16)
    attended = jnp.einsum("hqk,hkc->hqc", soft, value_rows, preferred_element_type=F32)
    return attended.astype(BF16), row_max + jnp.log(row_total)


def attend_back(queries, key_rows, value_rows, d_attended, log_total):
    soft = jnp.exp(scores_of(queries, key_rows) - log_total)
    d_soft = jnp.einsum("hqc,hkc->hqk", d_attended, value_rows, preferred_element_type=F32)
    d_values = jnp.einsum("hqk,hqc->hkc", soft.astype(BF16), d_attended, preferred_element_type=F32)
    d_scores = (soft * (d_soft - jnp.sum(soft * d_soft, axis=-1, keepdims=True))).astype(BF16)
    d_queries = 64 ** (-0.5) * jnp.einsum("hqk,hkc->hqc", d_scores, key_rows, preferred_element_type=F32)
    d_keys = 64 ** (-0.5) * jnp.einsum("hqk,hqc->hkc", d_scores, queries, preferred_element_type=F32)
    return d_queries.astype(BF16), d_keys.astype(BF16), d_values.astype(BF16)


def gelu(v):
    return 0.5 * v * (1.0 + lax.erf(v * 0.5**0.5))


def gelu_slope(v):
    return 0.5 * (1.0 + lax.erf(v * 0.5**0.5)) + v * jnp.exp(-0.5 * v * v) * (0.5 / jnp.pi) ** 0.5


def heads_first(v):
    return v.reshape(ROWS, 2, -1).transpose(1, 0, 2)


def heads_last(v):
    return v.transpose(1, 0, 2).reshape(ROWS, -1)


def local(
    tokens,
    counts,
    cotangent,
    qkv_weight,
    out_weight,
    fc1_weight,
    fc2_weight,
    norm_gains,
    shifts,
    qv_bias,
    fc1_bias,
):
    me = Place()
    live = me.xl < lax.dynamic_index_in_dim(counts, me.d, keepdims=False)

    def images(v):
        return jnp.pad(v.reshape(2, SEQ, 64), ((0, 0), (0, ROWS - SEQ), (0, 0)))

    x = jnp.concatenate([images(tokens), images(cotangent)], axis=2)
    packs = [
        (
            jnp.concatenate([qkv_weight[l].T, out_weight[l]], axis=0),
            jnp.concatenate([fc1_weight[l].T, fc2_weight[l]], axis=0),
        )
        for l in range(LAYERS)
    ]
    def wide_rows(v, rows):
        v = v.reshape(rows, -1).astype(F32)
        return jnp.pad(v, ((0, 0), (0, 128 - v.shape[1])))

    small = jnp.concatenate(
        [wide_rows(norm_gains, 4), wide_rows(shifts, 8), wide_rows(qv_bias, 2), wide_rows(fc1_bias, 2)]
    )
    first_in, state, gradient_full, gradient, wide_a, vectors, qkv_shift, up_bias = open_call(counts, x, packs[0][0], small)
    gains = vectors[:4].reshape(LAYERS, 2, 1, D)
    biases = vectors[4:12].reshape(LAYERS, 4, 1, D)
    qkv_shift = qkv_shift[12:14]
    up_bias = up_bias[14:16]
    saved = []
    wides = []
    for l in range(LAYERS):
        proj_qkv = wide_a[:, :192].reshape(384, D)
        proj_out = wide_a[:, 192:].reshape(128, D)
        mixed = (inner_right(first_in, proj_qkv) + qkv_shift[l]).astype(BF16)
        mixed = mixed.reshape(ROWS, 2, 3, 64).transpose(2, 1, 0, 3)
        queries, key_rows, value_rows = mixed[0], mixed[1], mixed[2]
        attended, log_total = attend(queries, key_rows, value_rows)
        attended = heads_last(attended)
        part = matmul(attended, proj_out).astype(BF16)
        middle, second_in, wide_b = forward_call(
            1 + 2 * l, part, state, biases[l, 1], gains[l, 1], biases[l, 2], packs[l][1]
        )
        second_in = second_in.reshape(ROWS, D)
        proj_up = wide_b[:, :256].reshape(512, D)
        proj_down = wide_b[:, 256:].reshape(512, D)
        pre_act = inner_right(second_in, proj_up) + up_bias[l]
        activated = gelu(pre_act).astype(BF16)
        part = matmul(activated, proj_down).astype(BF16)
        saved.append((state, middle, first_in, queries, key_rows, value_rows, attended, log_total, second_in, pre_act, activated))
        wides.append((proj_qkv, proj_out, proj_up, proj_down))
        if l < LAYERS - 1:
            state, first_in, wide_a = forward_call(
                2 + 2 * l, part, middle, biases[l, 3], gains[l + 1, 0], biases[l + 1, 0], packs[l + 1][0]
            )
            first_in = first_in.reshape(ROWS, D)
        else:
            (state,) = forward_call(2 + 2 * l, part, middle, biases[l, 3], gains[0, 0], biases[0, 0], last=True)
    out_rows = jnp.where(live, state, 0.0).astype(BF16)

    all_sums = []
    bias_sums = [None] * LAYERS
    owned = {}
    pending = None
    for l in reversed(range(LAYERS)):
        state, middle, first_in, queries, key_rows, value_rows, attended, log_total, second_in, pre_act, activated = saved[l]
        proj_qkv, proj_out, proj_up, proj_down = wides[l]
        d_pre = (inner_right(gradient_full, proj_down) * gelu_slope(pre_act)).astype(BF16)
        d_up_bias = jnp.sum(d_pre.astype(F32), axis=0)
        part = matmul(d_pre, proj_up).astype(BF16)
        base = 5 + 2 * (LAYERS - 1 - l)
        gradient, sums, weight_part, low, *landed = backward_call(
            base, part, middle, gradient, gains[l, 1], ((d_pre, second_in), (activated, gradient_full)), pending
        )
        if pending is not None:
            owned["a", l + 1] = landed[0]
        pending = weight_part
        all_sums.append(sums)
        low = low.reshape(ROWS, D)
        d_attended = heads_first(inner_right(low, proj_out).astype(BF16))
        d_mixed = attend_back(queries, key_rows, value_rows, d_attended, log_total)
        d_mixed = jnp.stack(d_mixed).transpose(2, 1, 0, 3).reshape(ROWS, 384)
        part = matmul(d_mixed, proj_qkv).astype(BF16)
        mixed_sums = jnp.sum(d_mixed.astype(F32), axis=0).reshape(2, 3, 64)
        d_qv = jnp.concatenate([mixed_sums[:, 0], mixed_sums[:, 2]], axis=1)
        bias_sums[l] = (d_up_bias.reshape(2, 2, 128), d_qv.reshape(2, 1, 128))
        products = ((d_mixed, first_in), (attended, low))
        if l > 0:
            gradient, sums, weight_part, low, owned["b", l] = backward_call(
                base + 1, part, state, gradient, gains[l, 0], products, pending
            )
            all_sums.append(sums)
            pending = weight_part
            gradient_full = low.reshape(ROWS, D)
    bias = jnp.concatenate(
        [bias_sums[0][0], bias_sums[1][0], bias_sums[0][1], bias_sums[1][1], jnp.zeros((2, 2, 128), F32)], axis=1
    )
    out_landed, grad_landed, vec, bias, owned["b", 0], owned["a", 0] = close_call(
        9, part, state, gradient, gains[0, 0], products, pending, out_rows, all_sums, bias
    )

    def side(v, width, at):
        return lax.dynamic_slice_in_dim(v, at * width, width, axis=-1)

    def whole(v):
        return side(v, 64, me.c).reshape(2, ROWS, 64)[:, :SEQ].reshape(2 * SEQ, 64)

    vec = side(vec, 8, me.c * 8 + me.d)
    return (
        whole(out_landed),
        whole(grad_landed).astype(F32),
        jnp.stack([owned["a", l][:192].T for l in range(LAYERS)]),
        jnp.stack([owned["a", l][192:] for l in range(LAYERS)]),
        jnp.stack([owned["b", l][:256].T for l in range(LAYERS)]),
        jnp.stack([owned["b", l][256:] for l in range(LAYERS)]),
        vec[:4].reshape(LAYERS, 2, 1, 8),
        vec[4:12].reshape(LAYERS, 4, 1, 8),
        side(bias[4:6], 16, me.d).reshape(LAYERS, 1, 16),
        side(bias[:4].reshape(LAYERS, 256), 32, me.d).reshape(LAYERS, 1, 32),
    )


def solution(mesh):
    placed = (
        P("dp", "tensor"),
        P(),
        P("dp", "tensor"),
        P(None, "dp", "tensor"),
        P(None, "tensor", "dp"),
        P(None, "dp", "tensor"),
        P(None, "tensor", "dp"),
        P(None, None, "tensor", "dp"),
        P(None, None, "tensor", "dp"),
        P(None, "tensor", "dp"),
        P(None, "tensor", "dp"),
    )
    return jax.shard_map(
        local,
        mesh=mesh,
        in_specs=placed,
        out_specs=(
            P("dp", "tensor"),
            P("dp", "tensor"),
            P(None, "dp", "tensor"),
            P(None, "tensor", "dp"),
            P(None, "dp", "tensor"),
            P(None, "tensor", "dp"),
            P(None, None, "tensor", "dp"),
            P(None, None, "tensor", "dp"),
            P(None, "tensor", "dp"),
            P(None, "tensor", "dp"),
        ),
        check_vma=False,
    )
```

```python
import functools

import jax
import jax.numpy as jnp
from jax import lax
from jax.experimental import pallas as pl
from jax.experimental.pallas import tpu as pltpu
from jax.sharding import PartitionSpec as P

MESH = pl.DeviceIdType.MESH
F32 = jnp.float32
BF16 = jnp.bfloat16
SEQ = 577
LAYERS = 2
BLOCK = 80
ROWS = 8 * BLOCK
D = 1024
EPS = 1e-06
VMEM = pl.BlockSpec(memory_space=pltpu.VMEM)
ANY = pl.BlockSpec(memory_space=pl.ANY)


class Place:
    def __init__(self):
        self.t = lax.axis_index("tensor")
        self.d = lax.axis_index("dp")
        self.z = self.t // 4
        self.xl = (self.t // 2) % 2
        self.c = self.t % 2
        self.w = self.d * 2 + self.xl
        self.j = self.z * 2 + self.c
        self.y = self.d // 2
        self.x = (self.d % 2) * 2 + self.xl
        self.zf, self.zb, self.zo = self.around(self.z)
        self.xf, self.xb, self.xo = self.around(self.x)
        self.yf, self.yb, self.yo = self.around(self.y)

    def around(self, at):
        return (at + 5 - 2 * self.c) % 4, (at + 3 + 2 * self.c) % 4, (at + 2) % 4

    def member(self, z, c):
        return (self.d, z * 4 + self.xl * 2 + c)

    def member_at(self, k):
        j = (self.j + k) % 8
        return self.member(j // 2, j % 2)

    def sharer(self, k):
        w = (self.w + k) % 16
        return (w // 2, self.z * 4 + (w % 2) * 2 + self.c)

    def plane(self, y, x):
        return (y * 2 + x // 2, self.z * 4 + (x % 2) * 2 + self.c)


def remote(src, dst, sems, role, device):
    return pltpu.make_async_remote_copy(
        src_ref=src,
        dst_ref=dst,
        send_sem=sems[0].at[role],
        recv_sem=sems[1].at[role],
        device_id=device,
        device_id_type=MESH,
    )


def hello(devices):
    barrier = pltpu.get_barrier_semaphore()
    for device in devices:
        pl.semaphore_signal(barrier, inc=1, device_id=device, device_id_type=MESH)
    return len(devices)


def met(count):
    pl.semaphore_wait(pltpu.get_barrier_semaphore(), count)


def greet(devices):
    met(hello(devices))


class Moves:
    def __init__(self, sems):
        self.sems, self.copies = sems, []

    def start(self, source, target):
        copy = pltpu.make_async_copy(source, target, self.sems.at[len(self.copies)])
        copy.start()
        self.copies.append(copy)

    def wait(self, *which):
        for k in which:
            self.copies[k].wait()

    def wait_all(self):
        self.wait(*range(len(self.copies)))


BANK = jax.ShapeDtypeStruct((24, D, D), BF16)


def attention_places(bank):
    rows = pl.ds(0, ROWS)
    return [
        bank.at[1, rows, pl.ds(0, 384)],
        bank.at[0, rows],
        bank.at[1, rows, pl.ds(384, 128)],
        bank.at[2, pl.ds(0, 256)],
        bank.at[2, pl.ds(256, 256)],
    ]


def feed_places(bank):
    rows = pl.ds(0, ROWS)
    return [
        bank.at[1, rows, pl.ds(512, 512)],
        bank.at[0, rows],
        bank.at[1, rows, pl.ds(0, 512)],
        bank.at[2, pl.ds(0, 512)],
        bank.at[2, pl.ds(512, 512)],
    ]


class Row:
    def __init__(self, ref, row):
        self.ref, self.row = ref, row

    def __getitem__(self, index):
        lanes = slice(None) if index is Ellipsis else index[1]
        return self.ref[self.row : self.row + 1, lanes]


def gain_row(l, n):
    return 2 * l + n


def shift_row(l, n):
    return 4 + 4 * l + n


def near(me):
    return [me.member(me.zf, me.c), me.member(me.zb, me.c), me.member(me.z, 1 - me.c)]


def cross(me):
    return [me.plane(me.y, me.xf), me.plane(me.y, me.xb), me.plane(me.yf, me.x), me.plane(me.yb, me.x)]


def nothing(point):
    pass


def gather(out, me, sems, beside=nothing):
    def pair(z, role, device):
        copy = remote(out.at[z, me.c], out.at[z, me.c], sems, role, device)
        copy.start()
        return copy

    ahead, back, other = near(me)
    first = pair(me.z, 0, ahead)
    second = pair(me.z, 1, back)
    over = [pair(me.z, 3, other)]
    beside(3)
    first.wait_recv()
    third = pair(me.zb, 2, ahead)
    over.append(pair(me.zb, 4, other))
    beside(4)
    second.wait_recv()
    over.append(pair(me.zf, 5, other))
    third.wait_recv()
    over.append(pair(me.zo, 6, other))
    beside(5)
    for copy in over:
        copy.wait_recv()
    for copy in [first, second, third] + over:
        copy.wait_send()


def reduce(part, crossed, held, landed, me, sems, produce, begin, beside):
    ahead, back, other = near(me)
    copies = []

    def made(role, z):
        produce(z)
        if role == 0:
            begin()
        copies.append(remote(part.at[z, 1 - me.c], crossed.at[role], sems, role, other))
        copies[-1].start()

    def both(role, z):
        copies[role].wait_recv()
        return part[z, me.c].astype(F32) + crossed[role].astype(F32)

    def send(slot, value, device):
        held[slot] = value.astype(BF16)
        copy = remote(held.at[slot], landed.at[slot], sems, 4 + slot, device)
        copy.start()
        sent.append(copy)
        return copy

    sent = []
    made(0, me.zo)
    made(1, me.zf)
    beside(0)
    long = send(0, both(0, me.zo), ahead)
    made(2, me.zb)
    short = send(1, both(1, me.zb), back)
    made(3, me.z)
    beside(1)
    long.wait_recv()
    last = send(2, both(2, me.zf) + landed[0].astype(F32), ahead)
    beside(2)
    total = both(3, me.z)
    short.wait_recv()
    total = total + landed[1].astype(F32)
    last.wait_recv()
    total = total + landed[2].astype(F32)
    return total, copies + sent


def reduce_scratch():
    return [
        pltpu.VMEM((4, 2, BLOCK, D), BF16),
        pltpu.VMEM((4, BLOCK, D), BF16),
        pltpu.VMEM((3, BLOCK, D), BF16),
        pltpu.VMEM((3, BLOCK, D), BF16),
        pltpu.SemaphoreType.DMA((7,)),
        pltpu.SemaphoreType.DMA((7,)),
    ]


def pair_sems(count):
    return [pltpu.SemaphoreType.DMA((count,)), pltpu.SemaphoreType.DMA((count,))]


def lanes(at, width):
    return pl.ds(pl.multiple_of(at * 128, 128), width)


class Spread:
    def __init__(self, src, dst, me, sems, local):
        self.src, self.dst, self.me, self.sems = src, dst, me, sems
        half = src.shape[0] // 2
        self.a, self.b = pl.ds(0, half), pl.ds(half, half)
        self.copies = {}
        self.keep = pltpu.make_async_copy(src, dst.at[me.xl, :, lanes((me.x // 2) * 4 + me.y, 128)], local)

    def send(self, role, src, dst, device):
        self.copies[role] = remote(src, dst, self.sems, role, device)
        self.copies[role].start()

    def arrived(self, *roles):
        for role in roles:
            self.copies[role].wait_recv()

    def block(self, y, x, rows):
        return self.dst.at[x % 2, rows, lanes((x // 2) * 4 + y, 128)]

    def row(self, role, y, device):
        for hi in range(2):
            part = self.dst.at[:, self.a, lanes(hi * 4 + y, 128)]
            self.send(role + hi, part, part, device)

    def column(self, role, x, device):
        part = self.dst.at[x % 2, self.b, lanes((x // 2) * 4, 512)]
        self.send(role, part, part, device)

    def step(self, number):
        me = self.me
        xf, xb, yf, yb = cross(me)
        if number == 0:
            self.keep.start()
            for role, rows, device in ((0, self.a, xf), (1, self.a, xb), (2, self.b, yf), (3, self.b, yb)):
                self.send(role, self.src.at[rows], self.block(me.y, me.x, rows), device)
        elif number == 1:
            self.arrived(0, 2)
            self.send(4, self.block(me.y, me.xb, self.a), self.block(me.y, me.xb, self.a), xf)
            self.send(5, self.block(me.yb, me.x, self.b), self.block(me.yb, me.x, self.b), yf)
        elif number == 2:
            self.keep.wait()
            self.arrived(1, 4)
            self.row(6, me.y, yf)
            self.row(8, me.y, yb)
            self.arrived(3, 5)
            self.column(10, me.x, xf)
            self.column(11, me.x, xb)
        elif number == 3:
            self.arrived(6, 7)
            self.row(12, me.yb, yf)
            self.arrived(10)
            self.column(14, me.xb, xf)
        else:
            self.arrived(8, 9, 11, 12, 13, 14)
            for copy in self.copies.values():
                copy.wait_send()


def spread_scratch():
    return pair_sems(15) + [pltpu.SemaphoreType.DMA((1,))]


class Collect:
    def __init__(self, src, out, me, bufs):
        self.src, self.out, self.me = src, out, me
        self.rows_in, self.rows_held, self.cols_in, self.cols_held, self.one_in, self.one_held, *self.sems = bufs
        half = src.shape[1] // 2
        self.a, self.b = pl.ds(0, half), pl.ds(half, half)
        self.half = half
        self.copies = {}

    def send(self, role, src, dst, device):
        self.copies[role] = remote(src, dst, self.sems, role, device)
        self.copies[role].start()

    def arrived(self, *roles):
        for role in roles:
            self.copies[role].wait_recv()

    def column(self, x):
        return self.src.at[x % 2, self.a, lanes((x // 2) * 4, 512)]

    def row(self, y, hi):
        return self.src.at[:, self.b, lanes(hi * 4 + y, 128)]

    def step(self, number):
        me = self.me
        xf, xb, yf, yb = cross(me)
        if number == 0:
            self.send(0, self.column(me.xo), self.cols_in.at[0], xf)
            self.send(1, self.column(me.xb), self.cols_in.at[1], xb)
            for hi in range(2):
                self.send(3 + hi, self.row(me.yo, hi), self.rows_in.at[0, hi], yf)
                self.send(5 + hi, self.row(me.yb, hi), self.rows_in.at[1, hi], yb)
        elif number == 1:
            self.arrived(0)
            self.cols_held[0] = (self.column(me.xf)[...].astype(F32) + self.cols_in[0].astype(F32)).astype(BF16)
            self.send(2, self.cols_held.at[0], self.cols_in.at[2], xf)
            self.arrived(3, 4)
            for hi in range(2):
                self.rows_held[0, hi] = (self.row(me.yf, hi)[...].astype(F32) + self.rows_in[0, hi].astype(F32)).astype(BF16)
                self.send(7 + hi, self.rows_held.at[0, hi], self.rows_in.at[2, hi], yf)
        elif number == 2:
            self.arrived(1, 2)
            self.cols_held[1] = (
                self.column(me.x)[...].astype(F32) + self.cols_in[1].astype(F32) + self.cols_in[2].astype(F32)
            ).astype(BF16)
            self.send(9, self.cols_held.at[1, :, lanes(me.yo, 128)], self.one_in.at[0], yf)
            self.send(10, self.cols_held.at[1, :, lanes(me.yb, 128)], self.one_in.at[1], yb)
            self.arrived(5, 6, 7, 8)
            for hi in range(2):
                self.rows_held[1, hi] = (
                    self.row(me.y, hi)[...].astype(F32)
                    + self.rows_in[1, hi].astype(F32)
                    + self.rows_in[2, hi].astype(F32)
                ).astype(BF16)
            self.send(12, self.rows_held.at[1, me.xo // 2, me.xo % 2], self.one_in.at[3], xf)
            self.send(13, self.rows_held.at[1, me.xb // 2, me.xb % 2], self.one_in.at[4], xb)
        elif number == 3:
            self.arrived(9)
            self.one_held[0] = (self.cols_held[1, :, lanes(me.yf, 128)].astype(F32) + self.one_in[0].astype(F32)).astype(BF16)
            self.send(11, self.one_held.at[0], self.one_in.at[2], yf)
            self.arrived(12)
            self.one_held[1] = (self.rows_held[1, me.xf // 2, me.xf % 2].astype(F32) + self.one_in[3].astype(F32)).astype(BF16)
            self.send(14, self.one_held.at[1], self.one_in.at[5], xf)
        else:
            self.arrived(10, 11)
            self.out[self.a, :] = (
                self.cols_held[1, :, lanes(me.y, 128)].astype(F32)
                + self.one_in[1].astype(F32)
                + self.one_in[2].astype(F32)
            )
            self.arrived(13, 14)
            self.out[self.b, :] = (
                self.rows_held[1, me.x // 2, me.x % 2].astype(F32)
                + self.one_in[4].astype(F32)
                + self.one_in[5].astype(F32)
            )
            for copy in self.copies.values():
                copy.wait_send()


def collect_scratch(n):
    half = n // 2
    return [
        pltpu.VMEM((3, 2, 2, half, 128), BF16),
        pltpu.VMEM((2, 2, 2, half, 128), BF16),
        pltpu.VMEM((3, half, 512), BF16),
        pltpu.VMEM((2, half, 512), BF16),
        pltpu.VMEM((6, half, 128), BF16),
        pltpu.VMEM((2, half, 128), BF16),
    ] + pair_sems(15)


def row_stats(v):
    mean = jnp.sum(v, axis=1, keepdims=True) / D
    square = jnp.sum(v * v, axis=1, keepdims=True) / D
    return mean, lax.rsqrt(square - mean * mean + EPS)


def normed(v, gain, bias):
    mean, inv = row_stats(v)
    return ((v - mean) * inv * gain + bias).astype(BF16)


def call(body, identity, inputs, in_specs, out_shape, out_specs, scratch):
    return pl.pallas_call(
        body,
        out_shape=out_shape,
        in_specs=in_specs,
        out_specs=out_specs,
        scratch_shapes=scratch,
        cost_estimate=pl.CostEstimate(flops=20_000_000_000, bytes_accessed=40_000_000, transcendentals=0),
        compiler_params=pltpu.CompilerParams(
            collective_id=identity, has_side_effects=True, vmem_limit_bytes=24 * 1024 * 1024
        ),
    )(*inputs)


def half_swap(left, right, low):
    return jnp.where(low, left, pltpu.roll(right, 64, 1)), jnp.where(low, pltpu.roll(left, 64, 1), right)


def open_kernel(
    counts_ref, x_ref, w_ref, s_ref, in_ref, state_ref, cot_ref, above_ref, wide_ref, vec_ref, qkv_ref, up_ref,
    y_ref, tok_ref, sw_ref, st_ref, comp, local, *sems
):
    me = Place()
    greet([me.sharer(k) for k in range(1, 16)] + [me.member_at(k) for k in range(1, 8)])
    mine = y_ref.at[me.z, me.c, me.xl]
    swap = remote(x_ref.at[1 - me.xl], mine, sems[0:2], 0, (me.d, me.z * 4 + (1 - me.xl) * 2 + me.c))
    swap.start()
    keep = pltpu.make_async_copy(x_ref.at[me.xl], mine, local.at[0])
    keep.start()
    small = [remote(s_ref, sw_ref.at[me.w], sems[2:4], k - 1, me.sharer(k)) for k in range(1, 16)]
    for copy in small:
        copy.start()
    wide = Spread(w_ref, wide_ref, me, sems[4:6], local.at[1])
    wide.step(0)
    sw_ref[me.w] = s_ref[...]
    keep.wait()
    swap.wait()
    spread = []
    low = lax.broadcasted_iota(jnp.int32, (16, 128), 1) < 64

    def beside(point):
        wide.step(point - 2)
        if point == 3:
            for copy in small:
                copy.wait()
            comp[...] = sum(pltpu.roll(sw_ref[w], (w % 2) * 64 + (w // 2) * 8, 1) for w in range(16))
            st_ref[me.z, me.c] = comp[...]
            for k in range(1, 8):
                spread.append(remote(comp, st_ref.at[me.z, me.c], sems[6:8], k - 1, me.member_at(k)))
                spread[-1].start()
            pair = []
            for p in range(2):
                pair.append(sum(pltpu.roll(sw_ref[2 * d + p], d * 16, 1) for d in range(8)))
                for k in range(2):
                    value = sum(pltpu.roll(sw_ref[2 * d + p], (d % 4) * 32, 1) for d in range(4 * k, 4 * k + 4))
                    up_ref[:, (p * 2 + k) * 128 : (p * 2 + k + 1) * 128] = value
            swapped = half_swap(*pair, low)
            qkv_ref[:, :128] = jnp.where(low, pair[0], 0.0)
            qkv_ref[:, 128:256] = jnp.where(low, pltpu.roll(pair[0], 64, 1), swapped[0])
            qkv_ref[:, 256:] = jnp.where(low, 0.0, pair[1])

    gather(y_ref, me, sems[8:10], beside)
    for copy in spread:
        copy.wait()
    for z in range(4):
        for p, value in enumerate(half_swap(st_ref[z, 0], st_ref[z, 1], low)):
            vec_ref[:, (p * 4 + z) * 128 : (p * 4 + z + 1) * 128] = value
    live = jnp.where(me.xl < counts_ref[me.d], 1.0, 0.0)
    low_rows = lax.broadcasted_iota(jnp.int32, (BLOCK, 128), 1) < 64

    def rows(index, carry):
        at = pl.ds(pl.multiple_of(index * BLOCK, BLOCK), BLOCK)
        for z in range(4):
            for p in range(2):
                token, cot = half_swap(y_ref[z, 0, p, at].astype(F32), y_ref[z, 1, p, at].astype(F32), low_rows)
                place = pl.ds((p * 4 + z) * 128, 128)
                tok_ref[at, place] = token
                cot_ref[at, place] = (cot * live).astype(BF16)
        in_ref[at, :] = normed(tok_ref[at, :], vec_ref[0:1, :], vec_ref[4:5, :])
        return carry

    lax.fori_loop(0, 8, rows, 0)
    at = pl.ds(pl.multiple_of(me.j * BLOCK, BLOCK), BLOCK)
    state_ref[...] = tok_ref[at, :]
    above_ref[...] = cot_ref[at, :].astype(F32)
    wide.step(4)


def open_call(counts, x, w, s):
    return call(
        open_kernel,
        0,
        (counts, x, w, s),
        [pl.BlockSpec(memory_space=pltpu.SMEM), VMEM, ANY, VMEM],
        [
            jax.ShapeDtypeStruct((ROWS, D), BF16),
            jax.ShapeDtypeStruct((BLOCK, D), F32),
            jax.ShapeDtypeStruct((ROWS, D), BF16),
            jax.ShapeDtypeStruct((BLOCK, D), F32),
            jax.ShapeDtypeStruct((2, w.shape[0], D), BF16),
            jax.ShapeDtypeStruct((16, D), F32),
            jax.ShapeDtypeStruct((16, 384), F32),
            jax.ShapeDtypeStruct((16, 512), F32),
        ],
        [VMEM] * 4 + [ANY] + [VMEM] * 3,
        [
            pltpu.VMEM((4, 2, 2, ROWS, 128), BF16),
            pltpu.VMEM((ROWS, D), F32),
            pltpu.VMEM((16, 16, 128), F32),
            pltpu.VMEM((4, 2, 16, 128), F32),
            pltpu.VMEM((16, 128), F32),
            pltpu.SemaphoreType.DMA((2,)),
        ]
        + pair_sems(1)
        + pair_sems(15)
        + pair_sems(15)
        + pair_sems(7)
        + pair_sems(7),
    )


PAIR = 2 * BLOCK
QKV_SCRATCH = [pltpu.VMEM((384, D), BF16), pltpu.VMEM((128, D), BF16), pltpu.VMEM((6, ROWS, 128), BF16)]


def pair_rows(z):
    return pl.ds(pl.multiple_of(z * PAIR, PAIR), PAIR)


def dot(a, b, contract=(1, 0)):
    return lax.dot_general(a, b, (((contract[0],), (contract[1],)), ((), ())), preferred_element_type=F32)


def low_lanes(rows):
    return lax.broadcasted_iota(jnp.int32, (rows, 128), 1) < 64


def load_projections(wide, wq, wo):
    for p in range(2):
        wq[p * 192 : (p + 1) * 192, :] = wide[p, 0:192, :]
        wo[p * 64 : (p + 1) * 64, :] = wide[p, 192:256, :]


def turn(at, tiles, turned):
    low = low_lanes(PAIR)
    swapped = [pltpu.roll(tile, 64, 1) for tile in tiles]
    for index, tile in enumerate(swapped):
        turned[index, at, :] = tile.astype(BF16)
    turned[3, at, :] = jnp.where(low, tiles[0], 0.0).astype(BF16)
    turned[4, at, :] = jnp.where(low, swapped[1], 0.0).astype(BF16)


def score_rows(head, at, mixed, turned):
    keys = turned[0] if head == 0 else mixed[:, 256:384]
    scores = 64 ** (-0.5) * dot(turned[3 + head, at, :], keys, (1, 1))
    return jnp.where(lax.broadcasted_iota(jnp.int32, scores.shape, 1) < SEQ, scores, -1e30)


def store_part(part, z, value):
    part[z] = value.astype(BF16).reshape(2, BLOCK, D)


def forward_tail(me, refs, produce, begin, wide, state, shift, gain, bias, new_ref, out_ref, complete):
    part, crossed, held, landed, s0, s1, s2, s3 = refs

    def beside(point):
        if point == 1:
            complete()
        if wide is not None and point in (1, 2, 4):
            wide.step((None, 1, 2, None, 3)[point])

    total, copies = reduce(part, crossed, held, landed, me, (s0, s1), produce, begin, beside)
    value = state[...] + (total + shift[...])
    new_ref[...] = value
    if out_ref is not None:
        out_ref[me.z, me.c] = normed(value, gain[...], bias[...])
        gather(out_ref, me, (s2, s3), beside)
    for copy in copies:
        copy.wait_send()
    if wide is not None:
        wide.step(4)


def attention_kernel(
    banked, layer, in_ref, mine_ref, qkv_ref, state, vec_ref, w_ref, new_ref, out_ref, wide_ref, total_ref, *rest
):
    qkv_shift = Row(qkv_ref, 12 + layer)
    shift, gain, bias = (Row(vec_ref, r) for r in (shift_row(layer, 1), gain_row(layer, 1), shift_row(layer, 2)))
    if banked:
        bank, mixed, attended, wq, wo, turned, *rest = rest
        moves = Moves(rest[11])
        places = attention_places(bank)
        moves.start(in_ref, places[1])
        for p in range(2):
            moves.start(mine_ref.at[p], places[3 + p])
    else:
        mixed, attended, wq, wo, turned, *rest = rest
    me = Place()
    count = hello(near(me) + cross(me))
    wide = Spread(w_ref, wide_ref, me, rest[8:10], rest[10].at[0])
    load_projections(mine_ref, wq, wo)

    def project(index, carry):
        at = pair_rows(index)
        value = dot(in_ref[at, :], wq[...], (1, 1)) + qkv_shift[...]
        mixed[at, :] = value.astype(BF16)
        turn(at, [value[:, k * 128 : (k + 1) * 128] for k in range(3)], turned)
        return carry

    project(0, 0)
    met(count)
    wide.step(0)
    lax.fori_loop(1, 4, project, 0)

    def produce(z):
        at = pair_rows(z)
        parts = []
        for head in range(2):
            scores = score_rows(head, at, mixed, turned)
            row_max = jnp.max(scores, axis=1, keepdims=True)
            shifted = jnp.exp(scores - row_max)
            row_total = jnp.sum(shifted, axis=1, keepdims=True)
            soft = (shifted / row_total).astype(BF16)
            parts.append((dot(soft, mixed[:, 128 + head * 128 : 256 + head * 128]), row_max + jnp.log(row_total)))
        low = low_lanes(PAIR)
        value = jnp.where(low, parts[0][0], parts[1][0]).astype(BF16)
        attended[at, :] = value
        total_ref[at, :] = jnp.where(low, parts[0][1], parts[1][1])
        store_part(rest[0], z, dot(value, wo[...]))

    def complete():
        if banked:
            moves.start(mixed, places[0])
            moves.start(attended, places[2])

    forward_tail(me, rest[:8], produce, lambda: None, wide, state, shift, gain, bias, new_ref, out_ref, complete)
    if banked:
        moves.wait_all()


def attention_call(identity, banked, layer, first_in, mine, qkv_shift, state, vectors, w):
    kept = [jax.ShapeDtypeStruct((ROWS, 384), BF16), jax.ShapeDtypeStruct((ROWS, 128), BF16)]
    return call(
        functools.partial(attention_kernel, banked, layer),
        identity,
        (first_in, mine, qkv_shift, state, vectors, w),
        [VMEM] * 5 + [ANY],
        [
            jax.ShapeDtypeStruct((BLOCK, D), F32),
            jax.ShapeDtypeStruct((4, 2, BLOCK, D), BF16),
            jax.ShapeDtypeStruct((2, w.shape[0], D), BF16),
            jax.ShapeDtypeStruct((ROWS, 128), F32),
        ]
        + ([BANK] if banked else kept),
        [VMEM, VMEM, ANY, VMEM] + ([ANY] if banked else [VMEM] * 2),
        ([pltpu.VMEM(v.shape, v.dtype) for v in kept] if banked else [])
        + QKV_SCRATCH
        + reduce_scratch()
        + pair_sems(7)
        + spread_scratch()
        + ([pltpu.SemaphoreType.DMA((5,))] if banked else []),
    )


def feed_kernel(last, layer, in_ref, mine, up_ref, state, vec_ref, *refs):
    refs = list(refs)
    up_shift = Row(up_ref, 14 + layer)
    shift = Row(vec_ref, shift_row(layer, 3))
    gain, bias = (None, None) if last else (Row(vec_ref, gain_row(layer + 1, 0)), Row(vec_ref, shift_row(layer + 1, 0)))
    w_ref = None if last else refs.pop(0)
    new_ref = refs.pop(0)
    out_ref, wide_ref = (None, None) if last else (refs.pop(0), refs.pop(0))
    if not last:
        bank = refs.pop(0)
    activated, slope, *rest = refs
    if not last:
        moves = Moves(rest[11])
        places = feed_places(bank)
        moves.start(in_ref, places[1])
        for p in range(2):
            moves.start(mine.at[p], places[3 + p])
    me = Place()
    count = hello(near(me) + ([] if last else cross(me)))
    wide = None if last else Spread(w_ref, wide_ref, me, rest[8:10], rest[10].at[0])

    def begin():
        met(count)
        if not last:
            wide.step(0)

    def produce(z):
        at = pair_rows(z)
        rows = in_ref[at, :]
        total = 0.0
        for p in range(2):
            place = pl.ds(p * 256, 256)
            value = dot(rows, mine[p, 0:256, :], (1, 1)) + up_shift[:, place]
            normal = 0.5 * (1.0 + lax.erf(value * 0.5**0.5))
            active = (value * normal).astype(BF16)
            activated[at, place] = active
            slope[at, place] = (normal + value * jnp.exp(-0.5 * value * value) * (0.5 / jnp.pi) ** 0.5).astype(BF16)
            total = total + dot(active, mine[p, 256:512, :])
        store_part(rest[0], z, total)

    def complete():
        if not last:
            moves.start(slope, places[0])
            moves.start(activated, places[2])

    forward_tail(me, rest[:8], produce, begin, wide, state, shift, gain, bias, new_ref, out_ref, complete)
    if not last:
        moves.wait_all()


def feed_call(identity, layer, second_in, mine, up_shift, state, vectors, w=None):
    last = w is None
    out_shape = [jax.ShapeDtypeStruct((BLOCK, D), F32)]
    out_specs = [VMEM]
    inputs = [second_in, mine, up_shift, state, vectors]
    in_specs = [VMEM] * 5
    kept = [jax.ShapeDtypeStruct((ROWS, 512), BF16)] * 2
    scratch = reduce_scratch() + pair_sems(7)
    if not last:
        inputs.append(w)
        in_specs.append(ANY)
        out_shape += [jax.ShapeDtypeStruct((4, 2, BLOCK, D), BF16), jax.ShapeDtypeStruct((2, w.shape[0], D), BF16)]
        out_shape.append(BANK)
        out_specs += [VMEM, ANY, ANY]
        scratch = [pltpu.VMEM(v.shape, v.dtype) for v in kept] + scratch + spread_scratch()
        scratch.append(pltpu.SemaphoreType.DMA((5,)))
    else:
        out_shape += kept
        out_specs += [VMEM, VMEM]
    return call(functools.partial(feed_kernel, last, layer), identity, inputs, in_specs, out_shape, out_specs, scratch)


def weight_product(left, right, out, heads):
    size = left.shape[1] // 2

    def tile(index, carry):
        at = lanes(index * 2, 256)
        value = lax.dot_general(left[...], right[:, at], (((0,), (0,)), ((), ())), preferred_element_type=F32).astype(BF16)
        for p in range(2):
            out[p, pl.ds(heads, size), at] = value[p * size : (p + 1) * size]
        return carry

    lax.fori_loop(0, 4, tile, 0)


def norm_back(total, base, above, gain):
    mean, inv = row_stats(base)
    hat = (base - mean) * inv
    weighted = total * gain
    first = jnp.sum(weighted, axis=1, keepdims=True) / D
    second = jnp.sum(weighted * hat, axis=1, keepdims=True) / D
    return above + inv * (weighted - first - hat * second), total * hat


def backward_tail(me, refs, produce, begin, slots, products, weight_ref, base, above, gain, new_ref, sums_ref, out_ref):
    part, crossed, held, landed, s0, s1, s2, s3 = refs

    def beside(point):
        if point == 1:
            weight_product(*products[0], weight_ref, 0)
        if point == 3:
            weight_product(*products[1], weight_ref, products[0][0].shape[1] // 2)
        if slots is not None and point in (2, 3, 4):
            slots.step(point - 1)

    total, copies = reduce(part, crossed, held, landed, me, (s0, s1), produce, begin, beside)
    value, by_hat = norm_back(total, base[...], above[...], gain[...])
    new_ref[...] = value
    low = value.astype(BF16)
    out_ref[me.z, me.c] = low
    for row, each in enumerate((by_hat, total, low.astype(F32), above[...])):
        sums_ref[row : row + 1, :] = jnp.sum(each, axis=0, keepdims=True)
    sums_ref[4:8, :] = jnp.zeros((4, D), F32)
    gather(out_ref, me, (s2, s3), beside)
    for copy in copies:
        copy.wait_send()
    if slots is not None:
        slots.step(4)


def feed_back_kernel(collects, layer, grad_ref, *refs):
    refs = list(refs)
    base, above, gain = refs[0], refs[1], Row(refs[2], gain_row(layer, 1))
    kept, refs = (refs[3], refs[4:]) if collects else (refs[3:7], refs[7:])
    w_ref = refs.pop(0) if collects else None
    new_ref, sums_ref, weight_ref, out_ref, bias_ref = refs[:5]
    refs = refs[5:]
    owned_ref = refs.pop(0) if collects else None
    if collects:
        (slope, second_in, activated, mine, local), refs = refs[:5], refs[5:]
        moves = Moves(local)
        targets = (slope, second_in, activated, mine.at[0], mine.at[1])
        for source, target in zip(feed_places(kept), targets):
            moves.start(source, target)
    else:
        slope, second_in, activated, mine = kept
    d_pre, *rest = refs
    me = Place()
    count = hello(near(me) + (cross(me) if collects else []))
    if collects:
        moves.wait_all()
    slots = Collect(w_ref, owned_ref, me, rest[8:]) if collects else None

    def begin():
        met(count)
        if collects:
            slots.step(0)


    def produce(z):
        at = pair_rows(z)
        rows = grad_ref[at, :]
        total = 0.0
        for p in range(2):
            place = pl.ds(p * 256, 256)
            value = (dot(rows, mine[p, 256:512, :], (1, 1)) * slope[at, place]).astype(BF16)
            d_pre[at, place] = value
            total = total + dot(value, mine[p, 0:256, :])
        store_part(rest[0], z, total)

    products = ((d_pre, second_in), (activated, grad_ref))
    backward_tail(
        me, rest[:8], produce, begin, slots, products, weight_ref, base, above, gain, new_ref, sums_ref, out_ref
    )
    bias_ref[...] = jnp.sum(d_pre[...].astype(F32), axis=0, keepdims=True)


def backward_shapes(size):
    return [
        jax.ShapeDtypeStruct((BLOCK, D), F32),
        jax.ShapeDtypeStruct((8, D), F32),
        jax.ShapeDtypeStruct((2, size, D), BF16),
        jax.ShapeDtypeStruct((4, 2, BLOCK, D), BF16),
    ]


def feed_back_call(identity, layer, grad, base, above, vectors, kept, w=None):
    inputs = [grad, base, above, vectors, *kept]
    in_specs = [VMEM] * 4 + [VMEM if w is None else ANY] * len(kept)
    out_shape = backward_shapes(512) + [jax.ShapeDtypeStruct((1, 512), F32)]
    scratch = [pltpu.VMEM((ROWS, 512), BF16)] + reduce_scratch() + pair_sems(7)
    if w is not None:
        inputs.append(w)
        in_specs.append(VMEM)
        scratch = [
            pltpu.VMEM((ROWS, 512), BF16),
            pltpu.VMEM((ROWS, D), BF16),
            pltpu.VMEM((ROWS, 512), BF16),
            pltpu.VMEM((2, 512, D), BF16),
            pltpu.SemaphoreType.DMA((5,)),
        ] + scratch
        out_shape.append(jax.ShapeDtypeStruct((w.shape[1], 128), F32))
        scratch += collect_scratch(w.shape[1])
    body = functools.partial(feed_back_kernel, w is not None, layer)
    return call(body, identity, inputs, in_specs, out_shape, [VMEM] * len(out_shape), scratch)


BACK_SCRATCH = QKV_SCRATCH + [
    pltpu.VMEM((ROWS, 384), BF16),
    pltpu.VMEM((3, ROWS, 128), BF16),
    pltpu.VMEM((6, ROWS, 128), F32),
]


def attention_back(grad_ref, mine, mixed, total_ref, bufs, begin):
    wq, wo, turned, d_mixed, d_att, sums = bufs
    load_projections(mine, wq, wo)
    low = low_lanes(PAIR)

    def ready(index, carry):
        at = pair_rows(index)
        tiles = [mixed[at, k * 128 : (k + 1) * 128].astype(F32) for k in range(3)]
        turn(at, tiles, turned)
        value = dot(grad_ref[at, :], wo[...], (1, 1))
        d_att[0, at, :] = value.astype(BF16)
        d_att[1, at, :] = jnp.where(low, value, 0.0).astype(BF16)
        d_att[2, at, :] = jnp.where(low, 0.0, value).astype(BF16)
        return carry

    lax.fori_loop(0, 4, ready, 0)
    begin()
    for k in range(2, 6):
        sums[k] = jnp.zeros((ROWS, 128), F32)

    def chunk(index, carry):
        at = pair_rows(index)
        grads = d_att[0, at, :]
        for head in range(2):
            soft = jnp.exp(score_rows(head, at, mixed, turned) - total_ref[at, head * 64 : head * 64 + 1])
            d_soft = dot(d_att[1 + head, at, :], mixed[:, 128 + head * 128 : 256 + head * 128], (1, 1))
            sums[2 + head] += dot(soft.astype(BF16), grads, (0, 0))
            d_scores = (soft * (d_soft - jnp.sum(soft * d_soft, axis=1, keepdims=True))).astype(BF16)
            sums[head, at, :] = dot(d_scores, turned[2 * head])
            sums[4 + head] += dot(d_scores, turned[head, at, :], (0, 0))
        return carry

    lax.fori_loop(0, 4, chunk, 0)

    def join(index, carry):
        at = pair_rows(index)
        scale = 64 ** (-0.5)
        d_mixed[at, 0:128] = (scale * jnp.where(low, sums[0, at, :], sums[4, at, :])).astype(BF16)
        d_mixed[at, 128:256] = jnp.where(low, sums[2, at, :], scale * sums[1, at, :]).astype(BF16)
        d_mixed[at, 256:384] = jnp.where(low, scale * sums[5, at, :], sums[3, at, :]).astype(BF16)
        return carry

    lax.fori_loop(0, 4, join, 0)

    def produce(part, z):
        store_part(part, z, dot(d_mixed[pair_rows(z), :], wq[...]))

    return produce


def attention_back_kernel(layer, grad_ref, *refs):
    kept, (above, vec_ref, w_ref, new_ref, sums_ref, weight_ref, out_ref, bias_ref, owned_ref) = refs[:6], refs[6:15]
    bufs, rest = refs[15:21], refs[21:]
    gain = Row(vec_ref, gain_row(layer, 0))
    mine, mixed, total_ref, base, first_in, attended = kept
    me = Place()
    count = hello(near(me) + cross(me))
    slots = Collect(w_ref, owned_ref, me, rest[8:])

    def begin():
        met(count)
        slots.step(0)

    produce = attention_back(grad_ref, mine, mixed, total_ref, bufs, begin)
    produce = functools.partial(produce, rest[0])
    products = ((bufs[3], first_in), (attended, grad_ref))
    backward_tail(
        me, rest[:8], produce, lambda: None, slots, products, weight_ref, base, above, gain, new_ref, sums_ref, out_ref
    )
    bias_ref[...] = jnp.sum(bufs[3][...].astype(F32), axis=0, keepdims=True)


def attention_back_call(identity, layer, grad, mine, mixed, totals, base, first_in, attended, above, vectors, w):
    inputs = [grad, mine, mixed, totals, base, first_in, attended, above, vectors, w]
    in_specs = [VMEM] * 10
    out_shape = backward_shapes(256) + [
        jax.ShapeDtypeStruct((1, 384), F32),
        jax.ShapeDtypeStruct((w.shape[1], 128), F32),
    ]
    scratch = BACK_SCRATCH + reduce_scratch() + pair_sems(7) + collect_scratch(w.shape[1])
    body = functools.partial(attention_back_kernel, layer)
    return call(body, identity, inputs, in_specs, out_shape, [VMEM] * len(out_shape), scratch)


def close_kernel(
    counts_ref, grad_in, bank, total_ref, base, above, vec_in, w_ref, state_ref, up_sums, mid_sums, down_sums,
    up_bias, mid_bias, down_bias,
    out_ref, grad_ref, vec_out, bias_out, owned_w, owned_p,
    product, low_ref, vec_ref, from_t, mine, from_w, from_b, own_bias, rows_ref, local,
    mixed, first_in, attended, weights, fetched, *rest
):
    me = Place()
    bufs, rest = rest[:6], rest[6:]
    part, crossed, held, landed, s0, s1 = rest[:6]
    sems, rest = rest[6:16], rest[16:]
    tensor = [(me.d, (me.t + k) % 16) for k in range(1, 16)]
    plane = [((me.d + k) % 8, me.z * 4 + xl * 2 + me.c) for k in range(1, 8) for xl in range(2)]
    moves = Moves(fetched)
    targets = (mixed, first_in, attended, weights.at[0], weights.at[1])
    for source, target in zip(attention_places(bank), targets):
        moves.start(source, target)
    count = hello(tensor + plane)
    moves.wait_all()
    slots_w = Collect(w_ref, owned_w, me, rest[:8])
    slots_p = Collect(product, owned_p, me, rest[8:])

    def scatter(source, target, sems, local):
        def features(t):
            return source.at[:, lanes(((t // 2) % 2) * 4 + t // 4, 128)]

        keep = pltpu.make_async_copy(features(me.t), target.at[me.xl, me.j], local)
        keep.start()
        copies = []
        for k in range(1, 16):
            t = (me.t + k) % 16
            copies.append(remote(features(t), target.at[me.xl, me.j], sems, k - 1, (me.d, t)))
            copies[-1].start()
        return keep, copies

    def share(source, target, sems, local):
        keep = pltpu.make_async_copy(source.at[me.xl], target.at[me.w], local)
        keep.start()
        copies = []
        for k in range(1, 16):
            xl = (me.w + k) % 2
            copies.append(remote(source.at[xl], target.at[me.w], sems, k - 1, me.sharer(k)))
            copies[-1].start()
        return keep, copies

    def finish(started):
        started[0].wait()
        for copy in started[1]:
            copy.wait()

    open_ends = []

    def beside(point):
        if point == 1:
            weight_product(bufs[3], first_in, product, 0)
            weight_product(attended, grad_in, product, 192)
            slots_p.step(0)
            slots_w.step(1)
            live = jnp.where(me.xl < counts_ref[me.d], 1.0, 0.0)
            rows_ref[...] = (state_ref[...] * live).astype(BF16)
            low = low_lanes(8)
            own_bias[...] = jnp.zeros_like(own_bias)
            for l, each in enumerate((down_bias, up_bias)):
                for p in range(2):
                    for k in range(2):
                        at = (2 * p + k) * 128
                        own_bias[p, 2 * l + k : 2 * l + k + 1, :] = each[:, at : at + 128]
            for l, each in enumerate((jnp.sum(bufs[3][...].astype(F32), axis=0, keepdims=True), mid_bias[...])):
                tiles = [jnp.broadcast_to(each[:, k * 128 : (k + 1) * 128], (8, 128)) for k in range(3)]
                turned = pltpu.roll(tiles[1], 64, 1)
                own_bias[0, 4 + l : 5 + l, :] = jnp.where(low, tiles[0], turned)[0:1]
                own_bias[1, 4 + l : 5 + l, :] = jnp.where(low, turned, tiles[2])[0:1]
        elif point == 2:
            slots_p.step(1)
            open_ends.append(scatter(rows_ref, out_ref, sems[0:2], local.at[0]))
            open_ends.append(share(own_bias, from_b, sems[2:4], local.at[1]))

    def begin():
        met(count)
        slots_w.step(0)

    produce = attention_back(grad_in, weights, mixed, total_ref, bufs, begin)
    produce = functools.partial(produce, part)
    total, copies = reduce(part, crossed, held, landed, me, (s0, s1), produce, lambda: None, beside)
    value, by_hat = norm_back(total, base[...], above[...], vec_in[0:1, :])
    low_ref[...] = value.astype(BF16)
    open_ends.append(scatter(low_ref, grad_ref, sems[4:6], local.at[2]))
    own = [jnp.sum(each, axis=0, keepdims=True) for each in (by_hat, total)]
    up, mid, down = ([ref[row : row + 1, :] for row in range(4)] for ref in (up_sums, mid_sums, down_sums))
    order = (own[0], down[0], mid[0], up[0], own[1], down[2], down[1], mid[2], mid[1], up[2], up[1], up[3])
    vec_ref[...] = jnp.zeros_like(vec_ref)
    for row, each in enumerate(order):
        for p in range(2):
            vec_ref[p, row : row + 1, :] = each[:, p * 512 : (p + 1) * 512]

    def vec(z):
        return vec_ref.at[:, :, lanes(z, 128)]

    keep = pltpu.make_async_copy(vec(me.z), from_t.at[me.j], local.at[3])
    keep.start()
    first = []
    for k in range(1, 8):
        j = (me.j + k) % 8
        first.append(remote(vec(j // 2), from_t.at[me.j], sems[6:8], k - 1, me.member(j // 2, j % 2)))
        first[-1].start()
    slots_w.step(2)
    finish((keep, first))
    mine[...] = sum(from_t[j] for j in range(8))
    second = share(mine, from_w, sems[8:10], local.at[4])
    slots_w.step(3)
    slots_p.step(2)
    slots_w.step(4)
    slots_p.step(3)
    finish(second)
    at_lane = 128 - (me.c * 64 + me.d * 8)
    vec_out[...] = pltpu.roll(sum(from_w[w] for w in range(16)), at_lane % 128, 1)
    for started in open_ends:
        finish(started)
    bias = sum(from_b[w] for w in range(16))
    for l in range(LAYERS):
        fc1 = jnp.where(me.d < 4, bias[2 * l : 2 * l + 1], bias[2 * l + 1 : 2 * l + 2])
        bias_out[l : l + 1, :] = pltpu.roll(fc1, (128 - (me.d % 4) * 32) % 128, 1)
    bias_out[4:8, :] = pltpu.roll(bias[4:8], (128 - me.d * 16) % 128, 1)
    bias_out[2:4, :] = jnp.zeros((2, 128), F32)
    for copy in copies:
        copy.wait_send()
    slots_p.step(4)


def close_call(identity, counts, grad, bank, totals, base, above, vectors, w, rows, sums, bias_sums):
    inputs = [counts, grad, bank, totals, base, above, vectors, w, rows, *sums, *bias_sums]
    return call(
        close_kernel,
        identity,
        inputs,
        [pl.BlockSpec(memory_space=pltpu.SMEM), VMEM, ANY] + [VMEM] * (len(inputs) - 3),
        [
            jax.ShapeDtypeStruct((2, 8, BLOCK, 128), BF16),
            jax.ShapeDtypeStruct((2, 8, BLOCK, 128), BF16),
            jax.ShapeDtypeStruct((16, 128), F32),
            jax.ShapeDtypeStruct((8, 128), F32),
            jax.ShapeDtypeStruct((w.shape[1], 128), F32),
            jax.ShapeDtypeStruct((256, 128), F32),
        ],
        [VMEM] * 6,
        [
            pltpu.VMEM((2, 256, D), BF16),
            pltpu.VMEM((BLOCK, D), BF16),
            pltpu.VMEM((2, 16, 512), F32),
            pltpu.VMEM((8, 2, 16, 128), F32),
            pltpu.VMEM((2, 16, 128), F32),
            pltpu.VMEM((16, 16, 128), F32),
            pltpu.VMEM((16, 8, 128), F32),
            pltpu.VMEM((2, 8, 128), F32),
            pltpu.VMEM((BLOCK, D), BF16),
            pltpu.SemaphoreType.DMA((5,)),
            pltpu.VMEM((ROWS, 384), BF16),
            pltpu.VMEM((ROWS, D), BF16),
            pltpu.VMEM((ROWS, 128), BF16),
            pltpu.VMEM((2, 256, D), BF16),
            pltpu.SemaphoreType.DMA((5,)),
        ]
        + BACK_SCRATCH
        + reduce_scratch()
        + pair_sems(15) * 3
        + pair_sems(7)
        + pair_sems(15)
        + collect_scratch(w.shape[1])
        + collect_scratch(256),
    )


def local(
    tokens,
    counts,
    cotangent,
    qkv_weight,
    out_weight,
    fc1_weight,
    fc2_weight,
    norm_gains,
    shifts,
    qv_bias,
    fc1_bias,
):
    me = Place()

    def images(v):
        return jnp.pad(v.reshape(2, SEQ, 64), ((0, 0), (0, ROWS - SEQ), (0, 0)))

    x = jnp.concatenate([images(tokens), images(cotangent)], axis=2)
    packs = [
        (
            jnp.concatenate([qkv_weight[l].T, out_weight[l]], axis=0),
            jnp.concatenate([fc1_weight[l].T, fc2_weight[l]], axis=0),
        )
        for l in range(LAYERS)
    ]
    def wide_rows(v, rows):
        v = v.reshape(rows, -1).astype(F32)
        return jnp.pad(v, ((0, 0), (0, 128 - v.shape[1])))

    small = jnp.concatenate(
        [wide_rows(norm_gains, 4), wide_rows(shifts, 8), wide_rows(qv_bias, 2), wide_rows(fc1_bias, 2)]
    )
    first_in, state, gradient_full, gradient, wide_a, vectors, qkv_shift, up_bias = open_call(counts, x, packs[0][0], small)
    saved = []
    for l in range(LAYERS):
        middle, second_in, wide_b, totals, *attention_kept = attention_call(
            1 + 2 * l, l == 0, l, first_in, wide_a, qkv_shift, state, vectors, packs[l][1]
        )
        second_in = second_in.reshape(ROWS, D)
        inputs = (l, second_in, wide_b, up_bias, middle, vectors)
        if l > 0:
            mixed, attended = attention_kept
            attention_kept = (wide_a, mixed, totals, state, first_in, attended)
        kept = (state, middle, totals, attention_kept)
        if l < LAYERS - 1:
            state, first_in, wide_a, bank = feed_call(2 + 2 * l, *inputs, packs[l + 1][0])
            first_in = first_in.reshape(ROWS, D)
            feed_kept = (bank,)
        else:
            state, activated, slope = feed_call(2 + 2 * l, *inputs)
            feed_kept = (slope, second_in, activated, wide_b)
        saved.append(kept + (feed_kept,))
    out_rows = state

    all_sums = []
    bias_sums = []
    owned = {}
    pending = None
    for l in reversed(range(LAYERS)):
        state, middle, totals, attention_kept, feed_kept = saved[l]
        base = 5 + 2 * (LAYERS - 1 - l)
        gradient, sums, weight_part, low, up_sums, *landed = feed_back_call(
            base, l, gradient_full, middle, gradient, vectors, feed_kept, pending
        )
        if pending is not None:
            owned["a", l + 1] = landed[0]
        pending = weight_part
        all_sums.append(sums)
        bias_sums.append(up_sums)
        low = low.reshape(ROWS, D)
        if l > 0:
            gradient, sums, weight_part, low, mixed_sums, owned["b", l] = attention_back_call(
                base + 1, l, low, *attention_kept, gradient, vectors, pending
            )
            all_sums.append(sums)
            pending = weight_part
            gradient_full = low.reshape(ROWS, D)
            bias_sums.append(mixed_sums)
    out_landed, grad_landed, vec, bias, owned["b", 0], owned["a", 0] = close_call(
        base + 1, counts, low, *attention_kept, totals, state, gradient, vectors, pending, out_rows, all_sums, bias_sums
    )

    def side(v, width, at):
        return lax.dynamic_slice_in_dim(v, at * width, width, axis=-1)

    def whole(v):
        return side(v, 64, me.c).reshape(2, ROWS, 64)[:, :SEQ].reshape(2 * SEQ, 64)

    vec = vec[:, :8]
    return (
        whole(out_landed),
        whole(grad_landed).astype(F32),
        jnp.stack([owned["a", l][:192].T for l in range(LAYERS)]),
        jnp.stack([owned["a", l][192:] for l in range(LAYERS)]),
        jnp.stack([owned["b", l][:256].T for l in range(LAYERS)]),
        jnp.stack([owned["b", l][256:] for l in range(LAYERS)]),
        vec[:4].reshape(LAYERS, 2, 1, 8),
        vec[4:12].reshape(LAYERS, 4, 1, 8),
        bias[4:6, :16].reshape(LAYERS, 1, 16),
        bias[:2, :32].reshape(LAYERS, 1, 32),
    )


def solution(mesh):
    placed = (
        P("dp", "tensor"),
        P(),
        P("dp", "tensor"),
        P(None, "dp", "tensor"),
        P(None, "tensor", "dp"),
        P(None, "dp", "tensor"),
        P(None, "tensor", "dp"),
        P(None, None, "tensor", "dp"),
        P(None, None, "tensor", "dp"),
        P(None, "tensor", "dp"),
        P(None, "tensor", "dp"),
    )
    return jax.shard_map(
        local,
        mesh=mesh,
        in_specs=placed,
        out_specs=(
            P("dp", "tensor"),
            P("dp", "tensor"),
            P(None, "dp", "tensor"),
            P(None, "tensor", "dp"),
            P(None, "dp", "tensor"),
            P(None, "tensor", "dp"),
            P(None, None, "tensor", "dp"),
            P(None, None, "tensor", "dp"),
            P(None, "tensor", "dp"),
            P(None, "tensor", "dp"),
        ),
        check_vma=False,
    )
```

```python
import functools

import jax
import jax.numpy as jnp
from jax import lax
from jax.experimental import pallas as pl
from jax.experimental.pallas import tpu as pltpu
from jax.sharding import PartitionSpec as P

MESH = pl.DeviceIdType.MESH
F32 = jnp.float32
BF16 = jnp.bfloat16
SEQ = 577
LAYERS = 2
BLOCK = 80
ROWS = 8 * BLOCK
D = 1024
EPS = 1e-06
VMEM = pl.BlockSpec(memory_space=pltpu.VMEM)
ANY = pl.BlockSpec(memory_space=pl.ANY)


class Place:
    def __init__(self):
        self.t = lax.axis_index("tensor")
        self.d = lax.axis_index("dp")
        self.z = self.t // 4
        self.xl = (self.t // 2) % 2
        self.c = self.t % 2
        self.w = self.d * 2 + self.xl
        self.j = self.z * 2 + self.c
        self.y = self.d // 2
        self.x = (self.d % 2) * 2 + self.xl
        self.zf, self.zb, self.zo = self.around(self.z)
        self.xf, self.xb, self.xo = self.around(self.x)
        self.yf, self.yb, self.yo = self.around(self.y)

    def around(self, at):
        return (at + 5 - 2 * self.c) % 4, (at + 3 + 2 * self.c) % 4, (at + 2) % 4

    def member(self, z, c):
        return (self.d, z * 4 + self.xl * 2 + c)

    def member_at(self, k):
        j = (self.j + k) % 8
        return self.member(j // 2, j % 2)

    def sharer(self, k):
        w = (self.w + k) % 16
        return (w // 2, self.z * 4 + (w % 2) * 2 + self.c)

    def plane(self, y, x):
        return (y * 2 + x // 2, self.z * 4 + (x % 2) * 2 + self.c)


def remote(src, dst, sems, role, device):
    return pltpu.make_async_remote_copy(
        src_ref=src,
        dst_ref=dst,
        send_sem=sems[0].at[role],
        recv_sem=sems[1].at[role],
        device_id=device,
        device_id_type=MESH,
    )


def hello(devices):
    barrier = pltpu.get_barrier_semaphore()
    for device in devices:
        pl.semaphore_signal(barrier, inc=1, device_id=device, device_id_type=MESH)
    return len(devices)


def met(count):
    pl.semaphore_wait(pltpu.get_barrier_semaphore(), count)


def greet(devices):
    met(hello(devices))


class Moves:
    def __init__(self, sems):
        self.sems, self.copies = sems, []

    def start(self, source, target):
        copy = pltpu.make_async_copy(source, target, self.sems.at[len(self.copies)])
        copy.start()
        self.copies.append(copy)

    def wait(self, *which):
        for k in which:
            self.copies[k].wait()

    def wait_all(self):
        self.wait(*range(len(self.copies)))


BANK = jax.ShapeDtypeStruct((24, D, D), BF16)


def attention_places(bank):
    rows = pl.ds(0, ROWS)
    return [
        bank.at[1, rows, pl.ds(0, 384)],
        bank.at[0, rows],
        bank.at[1, rows, pl.ds(384, 128)],
        bank.at[2, pl.ds(0, 256)],
        bank.at[2, pl.ds(256, 256)],
    ]


def feed_places(bank):
    rows = pl.ds(0, ROWS)
    return [
        bank.at[1, rows, pl.ds(512, 512)],
        bank.at[0, rows],
        bank.at[1, rows, pl.ds(0, 512)],
        bank.at[2, pl.ds(0, 512)],
        bank.at[2, pl.ds(512, 512)],
    ]


class Row:
    def __init__(self, ref, row):
        self.ref, self.row = ref, row

    def __getitem__(self, index):
        lanes = slice(None) if index is Ellipsis else index[1]
        return self.ref[self.row : self.row + 1, lanes]


def gain_row(l, n):
    return 2 * l + n


def shift_row(l, n):
    return 4 + 4 * l + n


def near(me):
    return [me.member(me.zf, me.c), me.member(me.zb, me.c), me.member(me.z, 1 - me.c)]


def cross(me):
    return [me.plane(me.y, me.xf), me.plane(me.y, me.xb), me.plane(me.yf, me.x), me.plane(me.yb, me.x)]


def nothing(point):
    pass


def gather_steps(out, me, sems):
    def pair(z, role, device):
        copy = remote(out.at[z, me.c], out.at[z, me.c], sems, role, device)
        copy.start()
        return copy

    ahead, back, other = near(me)
    first = pair(me.z, 0, ahead)
    second = pair(me.z, 1, back)
    over = [pair(me.z, 3, other)]
    yield
    first.wait_recv()
    third = pair(me.zb, 2, ahead)
    over.append(pair(me.zb, 4, other))
    yield
    second.wait_recv()
    over.append(pair(me.zf, 5, other))
    third.wait_recv()
    over.append(pair(me.zo, 6, other))
    yield
    for copy in over:
        copy.wait_recv()
    for copy in [first, second, third] + over:
        copy.wait_send()


def gather(out, me, sems, beside=nothing):
    for point, _ in enumerate(gather_steps(out, me, sems)):
        beside(3 + point)


def reduce(part, crossed, held, landed, me, sems, produce, begin, beside):
    ahead, back, other = near(me)
    copies = []

    def made(role, z):
        produce(z)
        if role == 0:
            begin()
        copies.append(remote(part.at[z, 1 - me.c], crossed.at[role], sems, role, other))
        copies[-1].start()

    def both(role, z):
        copies[role].wait_recv()
        return part[z, me.c].astype(F32) + crossed[role].astype(F32)

    def send(slot, value, device):
        held[slot] = value.astype(BF16)
        copy = remote(held.at[slot], landed.at[slot], sems, 4 + slot, device)
        copy.start()
        sent.append(copy)
        return copy

    sent = []
    made(0, me.zo)
    made(1, me.zf)
    beside(0)
    long = send(0, both(0, me.zo), ahead)
    made(2, me.zb)
    short = send(1, both(1, me.zb), back)
    made(3, me.z)
    beside(1)
    long.wait_recv()
    last = send(2, both(2, me.zf) + landed[0].astype(F32), ahead)
    beside(2)
    total = both(3, me.z)
    short.wait_recv()
    total = total + landed[1].astype(F32)
    last.wait_recv()
    total = total + landed[2].astype(F32)
    return total, copies + sent


def reduce_steps(part, crossed, held, landed, me, sems, finish):
    ahead, back, other = near(me)
    copies = []

    def send(source, target, role, device):
        copies.append(remote(source, target, sems, role, device))
        copies[-1].start()

    def both(role, z):
        copies[role].wait_recv()
        return part[z, me.c].astype(F32) + crossed[role].astype(F32)

    for role, z in enumerate((me.zo, me.zf, me.zb, me.z)):
        send(part.at[z, 1 - me.c], crossed.at[role], role, other)
    yield
    for slot, (z, device) in enumerate(((me.zo, ahead), (me.zb, back))):
        held[slot] = both(slot, z).astype(BF16)
        send(held.at[slot], landed.at[slot], 4 + slot, device)
    yield
    copies[4].wait_recv()
    held[2] = (both(2, me.zf) + landed[0].astype(F32)).astype(BF16)
    send(held.at[2], landed.at[2], 6, ahead)
    yield
    total = both(3, me.z)
    for slot in (1, 2):
        copies[4 + slot].wait_recv()
        total = total + landed[slot].astype(F32)
    finish(total)
    for copy in copies:
        copy.wait_send()


def reduce_scratch():
    return [
        pltpu.VMEM((4, 2, BLOCK, D), BF16),
        pltpu.VMEM((4, BLOCK, D), BF16),
        pltpu.VMEM((3, BLOCK, D), BF16),
        pltpu.VMEM((3, BLOCK, D), BF16),
        pltpu.SemaphoreType.DMA((7,)),
        pltpu.SemaphoreType.DMA((7,)),
    ]


def pair_sems(count):
    return [pltpu.SemaphoreType.DMA((count,)), pltpu.SemaphoreType.DMA((count,))]


def lanes(at, width):
    return pl.ds(pl.multiple_of(at * 128, 128), width)


class Spread:
    def __init__(self, src, dst, me, sems, local):
        self.src, self.dst, self.me, self.sems = src, dst, me, sems
        half = src.shape[0] // 2
        self.a, self.b = pl.ds(0, half), pl.ds(half, half)
        self.copies = {}
        self.keep = pltpu.make_async_copy(src, dst.at[me.xl, :, lanes((me.x // 2) * 4 + me.y, 128)], local)

    def send(self, role, src, dst, device):
        self.copies[role] = remote(src, dst, self.sems, role, device)
        self.copies[role].start()

    def arrived(self, *roles):
        for role in roles:
            self.copies[role].wait_recv()

    def block(self, y, x, rows):
        return self.dst.at[x % 2, rows, lanes((x // 2) * 4 + y, 128)]

    def row(self, role, y, device):
        for hi in range(2):
            part = self.dst.at[:, self.a, lanes(hi * 4 + y, 128)]
            self.send(role + hi, part, part, device)

    def column(self, role, x, device):
        part = self.dst.at[x % 2, self.b, lanes((x // 2) * 4, 512)]
        self.send(role, part, part, device)

    def step(self, number):
        me = self.me
        xf, xb, yf, yb = cross(me)
        if number == 0:
            self.keep.start()
            for role, rows, device in ((0, self.a, xf), (1, self.a, xb), (2, self.b, yf), (3, self.b, yb)):
                self.send(role, self.src.at[rows], self.block(me.y, me.x, rows), device)
        elif number == 1:
            self.arrived(0, 2)
            self.send(4, self.block(me.y, me.xb, self.a), self.block(me.y, me.xb, self.a), xf)
            self.send(5, self.block(me.yb, me.x, self.b), self.block(me.yb, me.x, self.b), yf)
        elif number == 2:
            self.keep.wait()
            self.arrived(1, 4)
            self.row(6, me.y, yf)
            self.row(8, me.y, yb)
            self.arrived(3, 5)
            self.column(10, me.x, xf)
            self.column(11, me.x, xb)
        elif number == 3:
            self.arrived(6, 7)
            self.row(12, me.yb, yf)
            self.arrived(10)
            self.column(14, me.xb, xf)
        else:
            self.arrived(8, 9, 11, 12, 13, 14)
            for copy in self.copies.values():
                copy.wait_send()


def spread_scratch():
    return pair_sems(15) + [pltpu.SemaphoreType.DMA((1,))]


class Collect:
    def __init__(self, src, out, me, bufs):
        self.src, self.out, self.me = src, out, me
        self.rows_in, self.rows_held, self.cols_in, self.cols_held, self.one_in, self.one_held, *self.sems = bufs
        half = src.shape[1] // 2
        self.a, self.b = pl.ds(0, half), pl.ds(half, half)
        self.half = half
        self.copies = {}

    def send(self, role, src, dst, device):
        self.copies[role] = remote(src, dst, self.sems, role, device)
        self.copies[role].start()

    def arrived(self, *roles):
        for role in roles:
            self.copies[role].wait_recv()

    def column(self, x):
        return self.src.at[x % 2, self.a, lanes((x // 2) * 4, 512)]

    def row(self, y, hi):
        return self.src.at[:, self.b, lanes(hi * 4 + y, 128)]

    def step(self, number):
        me = self.me
        xf, xb, yf, yb = cross(me)
        if number == 0:
            self.send(0, self.column(me.xo), self.cols_in.at[0], xf)
            self.send(1, self.column(me.xb), self.cols_in.at[1], xb)
            for hi in range(2):
                self.send(3 + hi, self.row(me.yo, hi), self.rows_in.at[0, hi], yf)
                self.send(5 + hi, self.row(me.yb, hi), self.rows_in.at[1, hi], yb)
        elif number == 1:
            self.arrived(0)
            self.cols_held[0] = (self.column(me.xf)[...].astype(F32) + self.cols_in[0].astype(F32)).astype(BF16)
            self.send(2, self.cols_held.at[0], self.cols_in.at[2], xf)
            self.arrived(3, 4)
            for hi in range(2):
                self.rows_held[0, hi] = (self.row(me.yf, hi)[...].astype(F32) + self.rows_in[0, hi].astype(F32)).astype(BF16)
                self.send(7 + hi, self.rows_held.at[0, hi], self.rows_in.at[2, hi], yf)
        elif number == 2:
            self.arrived(1, 2)
            self.cols_held[1] = (
                self.column(me.x)[...].astype(F32) + self.cols_in[1].astype(F32) + self.cols_in[2].astype(F32)
            ).astype(BF16)
            self.send(9, self.cols_held.at[1, :, lanes(me.yo, 128)], self.one_in.at[0], yf)
            self.send(10, self.cols_held.at[1, :, lanes(me.yb, 128)], self.one_in.at[1], yb)
            self.arrived(5, 6, 7, 8)
            for hi in range(2):
                self.rows_held[1, hi] = (
                    self.row(me.y, hi)[...].astype(F32)
                    + self.rows_in[1, hi].astype(F32)
                    + self.rows_in[2, hi].astype(F32)
                ).astype(BF16)
            self.send(12, self.rows_held.at[1, me.xo // 2, me.xo % 2], self.one_in.at[3], xf)
            self.send(13, self.rows_held.at[1, me.xb // 2, me.xb % 2], self.one_in.at[4], xb)
        elif number == 3:
            self.arrived(9)
            self.one_held[0] = (self.cols_held[1, :, lanes(me.yf, 128)].astype(F32) + self.one_in[0].astype(F32)).astype(BF16)
            self.send(11, self.one_held.at[0], self.one_in.at[2], yf)
            self.arrived(12)
            self.one_held[1] = (self.rows_held[1, me.xf // 2, me.xf % 2].astype(F32) + self.one_in[3].astype(F32)).astype(BF16)
            self.send(14, self.one_held.at[1], self.one_in.at[5], xf)
        else:
            self.arrived(10, 11)
            self.out[self.a, :] = (
                self.cols_held[1, :, lanes(me.y, 128)].astype(F32)
                + self.one_in[1].astype(F32)
                + self.one_in[2].astype(F32)
            )
            self.arrived(13, 14)
            self.out[self.b, :] = (
                self.rows_held[1, me.x // 2, me.x % 2].astype(F32)
                + self.one_in[4].astype(F32)
                + self.one_in[5].astype(F32)
            )
            for copy in self.copies.values():
                copy.wait_send()


def collect_scratch(n):
    half = n // 2
    return [
        pltpu.VMEM((3, 2, 2, half, 128), BF16),
        pltpu.VMEM((2, 2, 2, half, 128), BF16),
        pltpu.VMEM((3, half, 512), BF16),
        pltpu.VMEM((2, half, 512), BF16),
        pltpu.VMEM((6, half, 128), BF16),
        pltpu.VMEM((2, half, 128), BF16),
    ] + pair_sems(15)


def row_stats(v):
    mean = jnp.sum(v, axis=1, keepdims=True) / D
    square = jnp.sum(v * v, axis=1, keepdims=True) / D
    return mean, lax.rsqrt(square - mean * mean + EPS)


def normed(v, gain, bias):
    mean, inv = row_stats(v)
    return ((v - mean) * inv * gain + bias).astype(BF16)


def call(body, identity, inputs, in_specs, out_shape, out_specs, scratch):
    return pl.pallas_call(
        body,
        out_shape=out_shape,
        in_specs=in_specs,
        out_specs=out_specs,
        scratch_shapes=scratch,
        cost_estimate=pl.CostEstimate(flops=20_000_000_000, bytes_accessed=40_000_000, transcendentals=0),
        compiler_params=pltpu.CompilerParams(
            collective_id=identity, has_side_effects=True, vmem_limit_bytes=24 * 1024 * 1024
        ),
    )(*inputs)


def half_swap(left, right, low):
    return jnp.where(low, left, pltpu.roll(right, 64, 1)), jnp.where(low, pltpu.roll(left, 64, 1), right)


def unfold(blocks, out, change):
    low = low_lanes(BLOCK)

    def rows(index, carry):
        start = pl.multiple_of(index * BLOCK, BLOCK)
        for z in range(4):
            for p in range(2):
                left, right = (blocks[z, c, p, pl.ds(start, BLOCK)].astype(F32) for c in range(2))
                for half, value in enumerate(half_swap(left, right, low)):
                    at = pl.ds(pl.multiple_of(half * (ROWS // 2) + start, BLOCK), BLOCK)
                    out[at, pl.ds((p * 4 + z) * 128, 128)] = change(value).astype(out.dtype)
        return carry

    lax.fori_loop(0, 4, rows, 0)


def open_kernel(
    x_ref, x2_ref, w_ref, s_ref, in_ref, state_ref, wide_ref, vec_ref, qkv_ref, up_ref, cot_ref,
    y_ref, tok_ref, sw_ref, st_ref, comp, local, *sems
):
    me = Place()
    greet([me.sharer(k) for k in range(1, 16)] + [me.member_at(k) for k in range(1, 8)])
    mine = y_ref.at[me.z, me.c, me.xl]
    neighbour = (me.d, me.z * 4 + (1 - me.xl) * 2 + me.c)
    swap = remote(x_ref.at[1 - me.xl], mine, sems[0:2], 0, neighbour)
    swap.start()
    keep = pltpu.make_async_copy(x_ref.at[me.xl], mine, local.at[0])
    keep.start()
    cot_ref[me.xl] = x2_ref[me.xl]
    small = [remote(s_ref, sw_ref.at[me.w], sems[2:4], k - 1, me.sharer(k)) for k in range(1, 16)]
    for copy in small:
        copy.start()
    wide = Spread(w_ref, wide_ref, me, sems[4:6], local.at[1])
    wide.step(0)
    swap_cot = remote(x2_ref.at[1 - me.xl], cot_ref.at[me.xl], sems[0:2], 1, neighbour)
    swap_cot.start()
    sw_ref[me.w] = s_ref[...]
    keep.wait()
    swap.wait()
    spread = []
    low = lax.broadcasted_iota(jnp.int32, (16, 128), 1) < 64

    def beside(point):
        wide.step(point - 2)
        if point == 3:
            for copy in small:
                copy.wait()
            comp[...] = sum(pltpu.roll(sw_ref[w], (w % 2) * 64 + (w // 2) * 8, 1) for w in range(16))
            st_ref[me.z, me.c] = comp[...]
            for k in range(1, 8):
                spread.append(remote(comp, st_ref.at[me.z, me.c], sems[6:8], k - 1, me.member_at(k)))
                spread[-1].start()
            pair = []
            for p in range(2):
                pair.append(sum(pltpu.roll(sw_ref[2 * d + p], d * 16, 1) for d in range(8)))
                for k in range(2):
                    value = sum(pltpu.roll(sw_ref[2 * d + p], (d % 4) * 32, 1) for d in range(4 * k, 4 * k + 4))
                    up_ref[:, (p * 2 + k) * 128 : (p * 2 + k + 1) * 128] = value
            swapped = half_swap(*pair, low)
            qkv_ref[:, :128] = jnp.where(low, pair[0], 0.0)
            qkv_ref[:, 128:256] = jnp.where(low, pltpu.roll(pair[0], 64, 1), swapped[0])
            qkv_ref[:, 256:] = jnp.where(low, 0.0, pair[1])

    gather(y_ref, me, sems[8:10], beside)
    for copy in spread:
        copy.wait()
    for z in range(4):
        for p, value in enumerate(half_swap(st_ref[z, 0], st_ref[z, 1], low)):
            vec_ref[:, (p * 4 + z) * 128 : (p * 4 + z + 1) * 128] = value
    unfold(y_ref, tok_ref, lambda v: v)

    def rows(index, carry):
        at = pl.ds(pl.multiple_of(index * BLOCK, BLOCK), BLOCK)
        in_ref[at, :] = normed(tok_ref[at, :], vec_ref[0:1, :], vec_ref[4:5, :])
        return carry

    lax.fori_loop(0, 8, rows, 0)
    state_ref[...] = tok_ref[pl.ds(pl.multiple_of(me.j * BLOCK, BLOCK), BLOCK), :]
    swap_cot.wait()
    wide.step(4)


FOLDED = (4, 2, 2, ROWS // 2, 128)


def open_call(x, x2, w, s):
    return call(
        open_kernel,
        0,
        (x, x2, w, s),
        [VMEM, VMEM, ANY, VMEM],
        [
            jax.ShapeDtypeStruct((ROWS, D), BF16),
            jax.ShapeDtypeStruct((BLOCK, D), F32),
            jax.ShapeDtypeStruct((2, w.shape[0], D), BF16),
            jax.ShapeDtypeStruct((16, D), F32),
            jax.ShapeDtypeStruct((16, 384), F32),
            jax.ShapeDtypeStruct((16, 512), F32),
            jax.ShapeDtypeStruct((2, ROWS // 2, 128), BF16),
        ],
        [VMEM] * 2 + [ANY] + [VMEM] * 4,
        [
            pltpu.VMEM(FOLDED, BF16),
            pltpu.VMEM((ROWS, D), F32),
            pltpu.VMEM((16, 16, 128), F32),
            pltpu.VMEM((4, 2, 16, 128), F32),
            pltpu.VMEM((16, 128), F32),
            pltpu.SemaphoreType.DMA((2,)),
        ]
        + pair_sems(2)
        + pair_sems(15)
        + pair_sems(15)
        + pair_sems(7)
        + pair_sems(7),
    )


PAIR = 2 * BLOCK
QKV_SCRATCH = [pltpu.VMEM((384, D), BF16), pltpu.VMEM((128, D), BF16), pltpu.VMEM((6, ROWS, 128), BF16)]


def pair_rows(z):
    return pl.ds(pl.multiple_of(z * PAIR, PAIR), PAIR)


def dot(a, b, contract=(1, 0)):
    return lax.dot_general(a, b, (((contract[0],), (contract[1],)), ((), ())), preferred_element_type=F32)


def low_lanes(rows):
    return lax.broadcasted_iota(jnp.int32, (rows, 128), 1) < 64


def load_projections(wide, wq, wo):
    for p in range(2):
        wq[p * 192 : (p + 1) * 192, :] = wide[p, 0:192, :]
        wo[p * 64 : (p + 1) * 64, :] = wide[p, 192:256, :]


def turn(at, tiles, turned):
    low = low_lanes(PAIR)
    swapped = [pltpu.roll(tile, 64, 1) for tile in tiles]
    for index, tile in enumerate(swapped):
        turned[index, at, :] = tile.astype(BF16)
    turned[3, at, :] = jnp.where(low, tiles[0], 0.0).astype(BF16)
    turned[4, at, :] = jnp.where(low, swapped[1], 0.0).astype(BF16)


def score_rows(head, at, mixed, turned):
    keys = turned[0] if head == 0 else mixed[:, 256:384]
    scores = 64 ** (-0.5) * dot(turned[3 + head, at, :], keys, (1, 1))
    return jnp.where(lax.broadcasted_iota(jnp.int32, scores.shape, 1) < SEQ, scores, -1e30)


def store_part(part, z, value):
    part[z] = value.astype(BF16).reshape(2, BLOCK, D)


def forward_tail(me, refs, produce, begin, wide, state, shift, gain, bias, new_ref, out_ref, complete):
    part, crossed, held, landed, s0, s1, s2, s3 = refs

    def beside(point):
        complete(point)
        if wide is not None and point in (1, 2, 4):
            wide.step((None, 1, 2, None, 3)[point])

    total, copies = reduce(part, crossed, held, landed, me, (s0, s1), produce, begin, beside)
    value = state[...] + (total + shift[...])
    new_ref[...] = value
    if out_ref is not None:
        out_ref[me.z, me.c] = normed(value, gain[...], bias[...])
        gather(out_ref, me, (s2, s3), beside)
    for copy in copies:
        copy.wait_send()
    if wide is not None:
        wide.step(4)


def attention_kernel(
    banked, layer, in_ref, mine_ref, qkv_ref, state, vec_ref, w_ref, *rest
):
    qkv_shift = Row(qkv_ref, 12 + layer)
    shift, gain, bias = (Row(vec_ref, r) for r in (shift_row(layer, 1), gain_row(layer, 1), shift_row(layer, 2)))
    if banked:
        counts_ref, x_ref, *rest = rest
    new_ref, out_ref, wide_ref, total_ref, *rest = rest
    if banked:
        bank, cot_ref, above_ref, mixed, attended, wq, wo, turned, *rest = rest
        moves = Moves(rest[11])
        places = attention_places(bank)
        moves.start(in_ref, places[1])
        for p in range(2):
            moves.start(mine_ref.at[p], places[3 + p])
    else:
        mixed, attended, wq, wo, turned, *rest = rest
    me = Place()
    count = hello(near(me) + cross(me))
    wide = Spread(w_ref, wide_ref, me, rest[8:10], rest[10].at[0])
    load_projections(mine_ref, wq, wo)

    def project(index, carry):
        at = pair_rows(index)
        value = dot(in_ref[at, :], wq[...], (1, 1)) + qkv_shift[...]
        mixed[at, :] = value.astype(BF16)
        turn(at, [value[:, k * 128 : (k + 1) * 128] for k in range(3)], turned)
        return carry

    project(0, 0)
    met(count)
    wide.step(0)
    if banked:
        folded, cot_sems = rest[12], rest[13:15]
        folded[me.z, me.c] = x_ref[...]
        cot_steps = gather_steps(folded, me, cot_sems)
        next(cot_steps)
    lax.fori_loop(1, 4, project, 0)

    def produce(z):
        at = pair_rows(z)
        parts = []
        for head in range(2):
            scores = score_rows(head, at, mixed, turned)
            row_max = jnp.max(scores, axis=1, keepdims=True)
            shifted = jnp.exp(scores - row_max)
            row_total = jnp.sum(shifted, axis=1, keepdims=True)
            soft = (shifted / row_total).astype(BF16)
            parts.append((dot(soft, mixed[:, 128 + head * 128 : 256 + head * 128]), row_max + jnp.log(row_total)))
        low = low_lanes(PAIR)
        value = jnp.where(low, parts[0][0], parts[1][0]).astype(BF16)
        attended[at, :] = value
        total_ref[at, :] = jnp.where(low, parts[0][1], parts[1][1])
        store_part(rest[0], z, dot(value, wo[...]))

    def complete(point):
        if banked and point == 1:
            moves.start(mixed, places[0])
            moves.start(attended, places[2])
        if banked and point in (1, 3, 5):
            next(cot_steps, None)

    forward_tail(me, rest[:8], produce, lambda: None, wide, state, shift, gain, bias, new_ref, out_ref, complete)
    if banked:
        live = jnp.where(me.xl < counts_ref[me.d], 1.0, 0.0)
        unfold(folded, cot_ref, lambda v: v * live)
        above_ref[...] = cot_ref[pl.ds(pl.multiple_of(me.j * BLOCK, BLOCK), BLOCK), :].astype(F32)
        moves.wait_all()


def attention_call(identity, layer, first_in, mine, qkv_shift, state, vectors, w, counts=None, x=None):
    banked = x is not None
    kept = [jax.ShapeDtypeStruct((ROWS, 384), BF16), jax.ShapeDtypeStruct((ROWS, 128), BF16)]
    return call(
        functools.partial(attention_kernel, banked, layer),
        identity,
        (first_in, mine, qkv_shift, state, vectors, w) + ((counts, x) if banked else ()),
        [VMEM] * 5 + [ANY] + ([pl.BlockSpec(memory_space=pltpu.SMEM), VMEM] if banked else []),
        [
            jax.ShapeDtypeStruct((BLOCK, D), F32),
            jax.ShapeDtypeStruct((4, 2, BLOCK, D), BF16),
            jax.ShapeDtypeStruct((2, w.shape[0], D), BF16),
            jax.ShapeDtypeStruct((ROWS, 128), F32),
        ]
        + ([BANK, jax.ShapeDtypeStruct((ROWS, D), BF16), jax.ShapeDtypeStruct((BLOCK, D), F32)] if banked else kept),
        [VMEM, VMEM, ANY, VMEM] + ([ANY, VMEM, VMEM] if banked else [VMEM] * 2),
        ([pltpu.VMEM(v.shape, v.dtype) for v in kept] if banked else [])
        + QKV_SCRATCH
        + reduce_scratch()
        + pair_sems(7)
        + spread_scratch()
        + (
            [pltpu.SemaphoreType.DMA((5,)), pltpu.VMEM(FOLDED, BF16)] + pair_sems(7)
            if banked
            else []
        ),
    )


def feed_rows(at, in_ref, mine, up_shift, activated, slope):
    rows = in_ref[at, :]
    total = 0.0
    for p in range(2):
        place = pl.ds(p * 256, 256)
        value = dot(rows, mine[p, 0:256, :], (1, 1)) + up_shift[:, place]
        normal = 0.5 * (1.0 + lax.erf(value * 0.5**0.5))
        active = (value * normal).astype(BF16)
        activated[at, place] = active
        slope[at, place] = (normal + value * jnp.exp(-0.5 * value * value) * (0.5 / jnp.pi) ** 0.5).astype(BF16)
        total = total + dot(active, mine[p, 256:512, :])
    return total


def feed_back_rows(at, grad_ref, mine, slope, d_pre):
    rows = grad_ref[at, :]
    total = 0.0
    for p in range(2):
        place = pl.ds(p * 256, 256)
        value = (dot(rows, mine[p, 256:512, :], (1, 1)) * slope[at, place]).astype(BF16)
        d_pre[at, place] = value
        total = total + dot(value, mine[p, 0:256, :])
    return total


def feed_kernel(
    layer, in_ref, mine, up_ref, state, vec_ref, w_ref, new_ref, out_ref, wide_ref, bank, activated, slope, *rest
):
    up_shift = Row(up_ref, 14 + layer)
    shift, gain, bias = (Row(vec_ref, r) for r in (shift_row(layer, 3), gain_row(layer + 1, 0), shift_row(layer + 1, 0)))
    moves = Moves(rest[11])
    places = feed_places(bank)
    moves.start(in_ref, places[1])
    for p in range(2):
        moves.start(mine.at[p], places[3 + p])
    me = Place()
    count = hello(near(me) + cross(me))
    wide = Spread(w_ref, wide_ref, me, rest[8:10], rest[10].at[0])

    def begin():
        met(count)
        wide.step(0)

    def produce(z):
        store_part(rest[0], z, feed_rows(pair_rows(z), in_ref, mine, up_shift, activated, slope))

    def complete(point):
        if point == 1:
            moves.start(slope, places[0])
            moves.start(activated, places[2])

    forward_tail(me, rest[:8], produce, begin, wide, state, shift, gain, bias, new_ref, out_ref, complete)
    moves.wait_all()


def feed_call(identity, layer, second_in, mine, up_shift, state, vectors, w):
    kept = [pltpu.VMEM((ROWS, 512), BF16)] * 2
    return call(
        functools.partial(feed_kernel, layer),
        identity,
        [second_in, mine, up_shift, state, vectors, w],
        [VMEM] * 5 + [ANY],
        [
            jax.ShapeDtypeStruct((BLOCK, D), F32),
            jax.ShapeDtypeStruct((4, 2, BLOCK, D), BF16),
            jax.ShapeDtypeStruct((2, w.shape[0], D), BF16),
            BANK,
        ],
        [VMEM, VMEM, ANY, ANY],
        kept + reduce_scratch() + pair_sems(7) + spread_scratch() + [pltpu.SemaphoreType.DMA((5,))],
    )


def weight_product(left, right, out, heads):
    size = left.shape[1] // 2

    def tile(index, carry):
        at = lanes(index * 2, 256)
        value = lax.dot_general(left[...], right[:, at], (((0,), (0,)), ((), ())), preferred_element_type=F32).astype(BF16)
        for p in range(2):
            out[p, pl.ds(heads, size), at] = value[p * size : (p + 1) * size]
        return carry

    lax.fori_loop(0, 4, tile, 0)


def norm_back(total, base, above, gain):
    mean, inv = row_stats(base)
    hat = (base - mean) * inv
    weighted = total * gain
    first = jnp.sum(weighted, axis=1, keepdims=True) / D
    second = jnp.sum(weighted * hat, axis=1, keepdims=True) / D
    return above + inv * (weighted - first - hat * second), total * hat


def backward_tail(
    me, refs, produce, begin, slots, products, weight_ref, base, above, gain, new_ref, sums_ref, out_ref, also=nothing
):
    part, crossed, held, landed, s0, s1, s2, s3 = refs

    def beside(point):
        also(point)
        if point == 1:
            weight_product(*products[0], weight_ref, 0)
        if point == 3:
            weight_product(*products[1], weight_ref, products[0][0].shape[1] // 2)
        if slots is not None and point in (2, 3, 4):
            slots.step(point - 1)

    total, copies = reduce(part, crossed, held, landed, me, (s0, s1), produce, begin, beside)
    value, by_hat = norm_back(total, base[...], above[...], gain[...])
    new_ref[...] = value
    low = value.astype(BF16)
    out_ref[me.z, me.c] = low
    for row, each in enumerate((by_hat, total, low.astype(F32), above[...])):
        sums_ref[row : row + 1, :] = jnp.sum(each, axis=0, keepdims=True)
    sums_ref[4:8, :] = jnp.zeros((4, D), F32)
    gather(out_ref, me, (s2, s3), beside)
    for copy in copies:
        copy.wait_send()
    if slots is not None:
        slots.step(4)


def feed_back_kernel(
    layer, grad_ref, base, above, vec_ref, bank, w_ref, new_ref, sums_ref, weight_ref, out_ref, bias_ref, owned_ref,
    slope, second_in, activated, mine, fetched, d_pre, *rest
):
    moves = Moves(fetched)
    for source, target in zip(feed_places(bank), (slope, second_in, activated, mine.at[0], mine.at[1])):
        moves.start(source, target)
    me = Place()
    count = hello(near(me) + cross(me))
    moves.wait_all()
    slots = Collect(w_ref, owned_ref, me, rest[8:])

    def begin():
        met(count)
        slots.step(0)

    def produce(z):
        store_part(rest[0], z, feed_back_rows(pair_rows(z), grad_ref, mine, slope, d_pre))

    products = ((d_pre, second_in), (activated, grad_ref))
    gain = Row(vec_ref, gain_row(layer, 1))
    backward_tail(
        me, rest[:8], produce, begin, slots, products, weight_ref, base, above, gain, new_ref, sums_ref, out_ref
    )
    bias_ref[...] = jnp.sum(d_pre[...].astype(F32), axis=0, keepdims=True)


def turn_kernel(
    layer, in_ref, mine, up_ref, state, vec_ref, grad_ref, above, last_ref, new_ref, sums_ref, weight_ref, out_ref,
    bias_ref, activated, slope, d_pre, *rest
):
    up_shift, shift, gain = Row(up_ref, 14 + layer), Row(vec_ref, shift_row(layer, 3)), Row(vec_ref, gain_row(layer, 1))
    me = Place()
    count = hello(near(me))
    second, s0, s1 = rest[8:12], rest[12], rest[13]

    def produce(z):
        at = pair_rows(z)
        store_part(second[0], z, feed_rows(at, in_ref, mine, up_shift, activated, slope))
        store_part(rest[0], z, feed_back_rows(at, grad_ref, mine, slope, d_pre))

    def finish(total):
        last_ref[...] = state[...] + (total + shift[...])

    steps = reduce_steps(*second, me, (s0, s1), finish)

    def also(point):
        if point in (1, 2, 3, 5):
            next(steps, None)

    products = ((d_pre, in_ref), (activated, grad_ref))
    begin = functools.partial(met, count)
    backward_tail(
        me, rest[:8], produce, begin, None, products, weight_ref, state, above, gain, new_ref, sums_ref, out_ref, also
    )
    bias_ref[...] = jnp.sum(d_pre[...].astype(F32), axis=0, keepdims=True)


def backward_shapes(size):
    return [
        jax.ShapeDtypeStruct((BLOCK, D), F32),
        jax.ShapeDtypeStruct((8, D), F32),
        jax.ShapeDtypeStruct((2, size, D), BF16),
        jax.ShapeDtypeStruct((4, 2, BLOCK, D), BF16),
    ]


def feed_back_call(identity, layer, grad, base, above, vectors, bank, w):
    out_shape = backward_shapes(512) + [
        jax.ShapeDtypeStruct((1, 512), F32),
        jax.ShapeDtypeStruct((w.shape[1], 128), F32),
    ]
    scratch = [
        pltpu.VMEM((ROWS, 512), BF16),
        pltpu.VMEM((ROWS, D), BF16),
        pltpu.VMEM((ROWS, 512), BF16),
        pltpu.VMEM((2, 512, D), BF16),
        pltpu.SemaphoreType.DMA((5,)),
        pltpu.VMEM((ROWS, 512), BF16),
    ]
    scratch += reduce_scratch() + pair_sems(7) + collect_scratch(w.shape[1])
    inputs = [grad, base, above, vectors, bank, w]
    in_specs = [VMEM] * 4 + [ANY, VMEM]
    body = functools.partial(feed_back_kernel, layer)
    return call(body, identity, inputs, in_specs, out_shape, [VMEM] * len(out_shape), scratch)


def turn_call(identity, layer, second_in, mine, up_shift, state, vectors, grad, above):
    out_shape = [jax.ShapeDtypeStruct((BLOCK, D), F32)] + backward_shapes(512) + [jax.ShapeDtypeStruct((1, 512), F32)]
    scratch = [pltpu.VMEM((ROWS, 512), BF16)] * 3 + reduce_scratch() + pair_sems(7) + reduce_scratch()
    inputs = [second_in, mine, up_shift, state, vectors, grad, above]
    body = functools.partial(turn_kernel, layer)
    return call(body, identity, inputs, [VMEM] * len(inputs), out_shape, [VMEM] * len(out_shape), scratch)


BACK_SCRATCH = QKV_SCRATCH + [
    pltpu.VMEM((ROWS, 384), BF16),
    pltpu.VMEM((3, ROWS, 128), BF16),
    pltpu.VMEM((6, ROWS, 128), F32),
]


def attention_back(grad_ref, mine, mixed, total_ref, bufs, begin, between=None):
    wq, wo, turned, d_mixed, d_att, sums = bufs
    load_projections(mine, wq, wo)
    low = low_lanes(PAIR)

    def ready(index, carry):
        at = pair_rows(index)
        tiles = [mixed[at, k * 128 : (k + 1) * 128].astype(F32) for k in range(3)]
        turn(at, tiles, turned)
        value = dot(grad_ref[at, :], wo[...], (1, 1))
        d_att[0, at, :] = value.astype(BF16)
        d_att[1, at, :] = jnp.where(low, value, 0.0).astype(BF16)
        d_att[2, at, :] = jnp.where(low, 0.0, value).astype(BF16)
        return carry

    lax.fori_loop(0, 4, ready, 0)
    begin()
    for k in range(2, 6):
        sums[k] = jnp.zeros((ROWS, 128), F32)

    def chunk(index, carry):
        at = pair_rows(index)
        grads = d_att[0, at, :]
        for head in range(2):
            soft = jnp.exp(score_rows(head, at, mixed, turned) - total_ref[at, head * 64 : head * 64 + 1])
            d_soft = dot(d_att[1 + head, at, :], mixed[:, 128 + head * 128 : 256 + head * 128], (1, 1))
            sums[2 + head] += dot(soft.astype(BF16), grads, (0, 0))
            d_scores = (soft * (d_soft - jnp.sum(soft * d_soft, axis=1, keepdims=True))).astype(BF16)
            sums[head, at, :] = dot(d_scores, turned[2 * head])
            sums[4 + head] += dot(d_scores, turned[head, at, :], (0, 0))
        return carry

    lax.fori_loop(0, 4, chunk, 0)
    if between is not None:
        between()

    def join(index, carry):
        at = pair_rows(index)
        scale = 64 ** (-0.5)
        d_mixed[at, 0:128] = (scale * jnp.where(low, sums[0, at, :], sums[4, at, :])).astype(BF16)
        d_mixed[at, 128:256] = jnp.where(low, sums[2, at, :], scale * sums[1, at, :]).astype(BF16)
        d_mixed[at, 256:384] = jnp.where(low, scale * sums[5, at, :], sums[3, at, :]).astype(BF16)
        return carry

    lax.fori_loop(0, 4, join, 0)

    def produce(part, z):
        store_part(part, z, dot(d_mixed[pair_rows(z), :], wq[...]))

    return produce


def attention_back_kernel(layer, grad_ref, *refs):
    kept, (above, vec_ref, w_ref, new_ref, sums_ref, weight_ref, out_ref, bias_ref, owned_ref) = refs[:6], refs[6:15]
    bufs, rest = refs[15:21], refs[21:]
    gain = Row(vec_ref, gain_row(layer, 0))
    mine, mixed, total_ref, base, first_in, attended = kept
    me = Place()
    count = hello(near(me) + cross(me))
    slots = Collect(w_ref, owned_ref, me, rest[8:])

    def begin():
        met(count)
        slots.step(0)

    produce = attention_back(grad_ref, mine, mixed, total_ref, bufs, begin)
    produce = functools.partial(produce, rest[0])
    products = ((bufs[3], first_in), (attended, grad_ref))
    backward_tail(
        me, rest[:8], produce, lambda: None, slots, products, weight_ref, base, above, gain, new_ref, sums_ref, out_ref
    )
    bias_ref[...] = jnp.sum(bufs[3][...].astype(F32), axis=0, keepdims=True)


def attention_back_call(identity, layer, grad, mine, mixed, totals, base, first_in, attended, above, vectors, w):
    inputs = [grad, mine, mixed, totals, base, first_in, attended, above, vectors, w]
    in_specs = [VMEM] * 10
    out_shape = backward_shapes(256) + [
        jax.ShapeDtypeStruct((1, 384), F32),
        jax.ShapeDtypeStruct((w.shape[1], 128), F32),
    ]
    scratch = BACK_SCRATCH + reduce_scratch() + pair_sems(7) + collect_scratch(w.shape[1])
    body = functools.partial(attention_back_kernel, layer)
    return call(body, identity, inputs, in_specs, out_shape, [VMEM] * len(out_shape), scratch)


def close_kernel(
    counts_ref, grad_in, bank, total_ref, base, above, vec_in, w_ref, state_ref, up_sums, mid_sums, down_sums,
    up_bias, mid_bias, down_bias,
    out_ref, grad_ref, vec_out, bias_out, owned_w, owned_p,
    product, low_ref, vec_ref, from_t, mine, from_w, own_bias, rows_ref, local,
    mixed, first_in, attended, weights, fetched, *rest
):
    me = Place()
    bufs, rest = rest[:6], rest[6:]
    part, crossed, held, landed, s0, s1 = rest[:6]
    sems, rest = rest[6:14], rest[14:]
    tensor = [(me.d, (me.t + k) % 16) for k in range(1, 16)]
    plane = [((me.d + k) % 8, me.z * 4 + xl * 2 + me.c) for k in range(1, 8) for xl in range(2)]
    moves = Moves(fetched)
    targets = (mixed, first_in, attended, weights.at[0], weights.at[1])
    for source, target in zip(attention_places(bank), targets):
        moves.start(source, target)
    count = hello(tensor + plane)
    moves.wait_all()
    slots_w = Collect(w_ref, owned_w, me, rest[:8])
    slots_p = Collect(product, owned_p, me, rest[8:])

    def scatter(source, target, sems, local):
        def features(t):
            return source.at[:, lanes(((t // 2) % 2) * 4 + t // 4, 128)]

        keep = pltpu.make_async_copy(features(me.t), target.at[me.xl, me.j], local)
        keep.start()
        copies = []
        for k in range(1, 16):
            t = (me.t + k) % 16
            copies.append(remote(features(t), target.at[me.xl, me.j], sems, k - 1, (me.d, t)))
            copies[-1].start()
        return keep, copies

    def share(source, target, sems, local):
        keep = pltpu.make_async_copy(source.at[me.xl], target.at[me.w], local)
        keep.start()
        copies = []
        for k in range(1, 16):
            xl = (me.w + k) % 2
            copies.append(remote(source.at[xl], target.at[me.w], sems, k - 1, me.sharer(k)))
            copies[-1].start()
        return keep, copies

    def finish(started):
        started[0].wait()
        for copy in started[1]:
            copy.wait()

    open_ends = []

    def beside(point):
        if point == 1:
            weight_product(bufs[3], first_in, product, 0)
            weight_product(attended, grad_in, product, 192)
            slots_p.step(0)
            slots_w.step(2)
            low = low_lanes(8)
            own_bias[...] = jnp.zeros_like(own_bias)
            for l, each in enumerate((down_bias, up_bias)):
                for p in range(2):
                    for k in range(2):
                        at = (2 * p + k) * 128
                        own_bias[p, 2 * l + k : 2 * l + k + 1, :] = each[:, at : at + 128]
            for l, each in enumerate((jnp.sum(bufs[3][...].astype(F32), axis=0, keepdims=True), mid_bias[...])):
                tiles = [jnp.broadcast_to(each[:, k * 128 : (k + 1) * 128], (8, 128)) for k in range(3)]
                turned = pltpu.roll(tiles[1], 64, 1)
                own_bias[0, 4 + l : 5 + l, :] = jnp.where(low, tiles[0], turned)[0:1]
                own_bias[1, 4 + l : 5 + l, :] = jnp.where(low, turned, tiles[2])[0:1]
        elif point == 2:
            slots_p.step(1)
            slots_w.step(3)

    def begin():
        met(count)
        slots_w.step(0)
        live = jnp.where(me.xl < counts_ref[me.d], 1.0, 0.0)
        rows_ref[...] = (state_ref[...] * live).astype(BF16)
        open_ends.append(scatter(rows_ref, out_ref, sems[0:2], local.at[0]))

    produce = attention_back(grad_in, weights, mixed, total_ref, bufs, begin, lambda: slots_w.step(1))
    produce = functools.partial(produce, part)
    total, copies = reduce(part, crossed, held, landed, me, (s0, s1), produce, lambda: None, beside)
    value, by_hat = norm_back(total, base[...], above[...], vec_in[0:1, :])
    low_ref[...] = value.astype(BF16)
    own = [jnp.sum(each, axis=0, keepdims=True) for each in (by_hat, total)]
    up, mid, down = ([ref[row : row + 1, :] for row in range(4)] for ref in (up_sums, mid_sums, down_sums))
    order = (own[0], down[0], mid[0], up[0], own[1], down[2], down[1], mid[2], mid[1], up[2], up[1], up[3])
    vec_ref[...] = jnp.zeros_like(vec_ref)
    for row, each in enumerate(order):
        for p in range(2):
            vec_ref[p, row : row + 1, :] = each[:, p * 512 : (p + 1) * 512]

    def vec(z):
        return vec_ref.at[:, :, lanes(z, 128)]

    keep = pltpu.make_async_copy(vec(me.z), from_t.at[me.j], local.at[3])
    keep.start()
    first = []
    for k in range(1, 8):
        j = (me.j + k) % 8
        first.append(remote(vec(j // 2), from_t.at[me.j], sems[4:6], k - 1, me.member(j // 2, j % 2)))
        first[-1].start()
    open_ends.append(scatter(low_ref, grad_ref, sems[2:4], local.at[1]))
    finish((keep, first))
    mine[:, 0:16, :] = sum(from_t[j] for j in range(8))
    mine[:, 16:24, :] = own_bias[...]
    second = share(mine, from_w, sems[6:8], local.at[2])
    slots_p.step(2)
    slots_w.step(4)
    slots_p.step(3)
    finish(second)
    total = sum(from_w[w] for w in range(16))
    at_lane = 128 - (me.c * 64 + me.d * 8)
    vec_out[...] = pltpu.roll(total[0:16], at_lane % 128, 1)
    for started in open_ends:
        finish(started)
    bias = total[16:24]
    for l in range(LAYERS):
        fc1 = jnp.where(me.d < 4, bias[2 * l : 2 * l + 1], bias[2 * l + 1 : 2 * l + 2])
        bias_out[l : l + 1, :] = pltpu.roll(fc1, (128 - (me.d % 4) * 32) % 128, 1)
    bias_out[4:8, :] = pltpu.roll(bias[4:8], (128 - me.d * 16) % 128, 1)
    bias_out[2:4, :] = jnp.zeros((2, 128), F32)
    for copy in copies:
        copy.wait_send()
    slots_p.step(4)


def close_call(identity, counts, grad, bank, totals, base, above, vectors, w, rows, sums, bias_sums):
    inputs = [counts, grad, bank, totals, base, above, vectors, w, rows, *sums, *bias_sums]
    return call(
        close_kernel,
        identity,
        inputs,
        [pl.BlockSpec(memory_space=pltpu.SMEM), VMEM, ANY] + [VMEM] * (len(inputs) - 3),
        [
            jax.ShapeDtypeStruct((2, 8, BLOCK, 128), BF16),
            jax.ShapeDtypeStruct((2, 8, BLOCK, 128), BF16),
            jax.ShapeDtypeStruct((16, 128), F32),
            jax.ShapeDtypeStruct((8, 128), F32),
            jax.ShapeDtypeStruct((w.shape[1], 128), F32),
            jax.ShapeDtypeStruct((256, 128), F32),
        ],
        [VMEM] * 6,
        [
            pltpu.VMEM((2, 256, D), BF16),
            pltpu.VMEM((BLOCK, D), BF16),
            pltpu.VMEM((2, 16, 512), F32),
            pltpu.VMEM((8, 2, 16, 128), F32),
            pltpu.VMEM((2, 24, 128), F32),
            pltpu.VMEM((16, 24, 128), F32),
            pltpu.VMEM((2, 8, 128), F32),
            pltpu.VMEM((BLOCK, D), BF16),
            pltpu.SemaphoreType.DMA((5,)),
            pltpu.VMEM((ROWS, 384), BF16),
            pltpu.VMEM((ROWS, D), BF16),
            pltpu.VMEM((ROWS, 128), BF16),
            pltpu.VMEM((2, 256, D), BF16),
            pltpu.SemaphoreType.DMA((5,)),
        ]
        + BACK_SCRATCH
        + reduce_scratch()
        + pair_sems(15) * 2
        + pair_sems(7)
        + pair_sems(15)
        + collect_scratch(w.shape[1])
        + collect_scratch(256),
    )


def local(
    tokens,
    counts,
    cotangent,
    qkv_weight,
    out_weight,
    fc1_weight,
    fc2_weight,
    norm_gains,
    shifts,
    qv_bias,
    fc1_bias,
):
    me = Place()

    def images(v):
        v = jnp.pad(v.reshape(2, SEQ, 64), ((0, 0), (0, ROWS - SEQ), (0, 0)))
        return jnp.concatenate([v[:, : ROWS // 2], v[:, ROWS // 2 :]], axis=2)

    packs = [
        (
            jnp.concatenate([qkv_weight[l].T, out_weight[l]], axis=0),
            jnp.concatenate([fc1_weight[l].T, fc2_weight[l]], axis=0),
        )
        for l in range(LAYERS)
    ]
    def wide_rows(v, rows):
        v = v.reshape(rows, -1).astype(F32)
        return jnp.pad(v, ((0, 0), (0, 128 - v.shape[1])))

    small = jnp.concatenate(
        [wide_rows(norm_gains, 4), wide_rows(shifts, 8), wide_rows(qv_bias, 2), wide_rows(fc1_bias, 2)]
    )
    x, cot, packs, small = lax.optimization_barrier((images(tokens), images(cotangent), packs, small))
    first_in, state, wide_a, vectors, qkv_shift, up_bias, cot = open_call(x, cot, packs[0][0], small)
    first_state = state
    middle, second_in, wide_b, first_totals, first_bank, gradient_full, gradient = attention_call(
        1, 0, first_in, wide_a, qkv_shift, state, vectors, packs[0][1], counts, cot
    )
    first_middle = middle
    state, first_in, wide_a, feed_bank = feed_call(
        2, 0, second_in.reshape(ROWS, D), wide_b, up_bias, middle, vectors, packs[1][0]
    )
    first_in = first_in.reshape(ROWS, D)
    middle, second_in, wide_b, totals, mixed, attended = attention_call(
        3, 1, first_in, wide_a, qkv_shift, state, vectors, packs[1][1]
    )
    last_rows, gradient, up_sums, pending, low, up_bias_sums = turn_call(
        4, 1, second_in.reshape(ROWS, D), wide_b, up_bias, middle, vectors, gradient_full, gradient
    )
    owned = {}
    gradient, mid_sums, pending, low, mid_bias_sums, owned["b", 1] = attention_back_call(
        5, 1, low.reshape(ROWS, D), wide_a, mixed, totals, state, first_in, attended, gradient, vectors, pending
    )
    gradient, down_sums, pending, low, down_bias_sums, owned["a", 1] = feed_back_call(
        6, 0, low.reshape(ROWS, D), first_middle, gradient, vectors, feed_bank, pending
    )
    all_sums = [up_sums, mid_sums, down_sums]
    bias_sums = [up_bias_sums, mid_bias_sums, down_bias_sums]
    out_landed, grad_landed, vec, bias, owned["b", 0], owned["a", 0] = close_call(
        7, counts, low.reshape(ROWS, D), first_bank, first_totals, first_state, gradient, vectors, pending,
        last_rows, all_sums, bias_sums
    )

    def side(v, width, at):
        return lax.dynamic_slice_in_dim(v, at * width, width, axis=-1)

    def whole(v):
        return side(v, 64, me.c).reshape(2, ROWS, 64)[:, :SEQ].reshape(2 * SEQ, 64)

    vec = vec[:, :8]
    return (
        whole(out_landed),
        whole(grad_landed).astype(F32),
        jnp.stack([owned["a", l][:192].T for l in range(LAYERS)]),
        jnp.stack([owned["a", l][192:] for l in range(LAYERS)]),
        jnp.stack([owned["b", l][:256].T for l in range(LAYERS)]),
        jnp.stack([owned["b", l][256:] for l in range(LAYERS)]),
        vec[:4].reshape(LAYERS, 2, 1, 8),
        vec[4:12].reshape(LAYERS, 4, 1, 8),
        bias[4:6, :16].reshape(LAYERS, 1, 16),
        bias[:2, :32].reshape(LAYERS, 1, 32),
    )


def solution(mesh):
    placed = (
        P("dp", "tensor"),
        P(),
        P("dp", "tensor"),
        P(None, "dp", "tensor"),
        P(None, "tensor", "dp"),
        P(None, "dp", "tensor"),
        P(None, "tensor", "dp"),
        P(None, None, "tensor", "dp"),
        P(None, None, "tensor", "dp"),
        P(None, "tensor", "dp"),
        P(None, "tensor", "dp"),
    )
    return jax.shard_map(
        local,
        mesh=mesh,
        in_specs=placed,
        out_specs=(
            P("dp", "tensor"),
            P("dp", "tensor"),
            P(None, "dp", "tensor"),
            P(None, "tensor", "dp"),
            P(None, "dp", "tensor"),
            P(None, "tensor", "dp"),
            P(None, None, "tensor", "dp"),
            P(None, None, "tensor", "dp"),
            P(None, "tensor", "dp"),
            P(None, "tensor", "dp"),
        ),
        check_vma=False,
    )
```

```python
import functools

import jax
import jax.numpy as jnp
from jax import lax
from jax.experimental import pallas as pl
from jax.experimental.pallas import tpu as pltpu
from jax.sharding import PartitionSpec as P

MESH = pl.DeviceIdType.MESH
F32 = jnp.float32
BF16 = jnp.bfloat16
SEQ = 577
LAYERS = 2
BLOCK = 80
ROWS = 8 * BLOCK
D = 1024
EPS = 1e-06
VMEM = pl.BlockSpec(memory_space=pltpu.VMEM)
ANY = pl.BlockSpec(memory_space=pl.ANY)


class Place:
    def __init__(self):
        self.t = lax.axis_index("tensor")
        self.d = lax.axis_index("dp")
        self.z = self.t // 4
        self.xl = (self.t // 2) % 2
        self.c = self.t % 2
        self.w = self.d * 2 + self.xl
        self.j = self.z * 2 + self.c
        self.y = self.d // 2
        self.x = (self.d % 2) * 2 + self.xl
        self.zf, self.zb, self.zo = self.around(self.z)
        self.xf, self.xb, self.xo = self.around(self.x)
        self.yf, self.yb, self.yo = self.around(self.y)

    def around(self, at):
        return (at + 5 - 2 * self.c) % 4, (at + 3 + 2 * self.c) % 4, (at + 2) % 4

    def member(self, z, c):
        return (self.d, z * 4 + self.xl * 2 + c)

    def member_at(self, k):
        j = (self.j + k) % 8
        return self.member(j // 2, j % 2)

    def sharer(self, k):
        w = (self.w + k) % 16
        return (w // 2, self.z * 4 + (w % 2) * 2 + self.c)

    def plane(self, y, x):
        return (y * 2 + x // 2, self.z * 4 + (x % 2) * 2 + self.c)


def remote(src, dst, sems, role, device):
    return pltpu.make_async_remote_copy(
        src_ref=src,
        dst_ref=dst,
        send_sem=sems[0].at[role],
        recv_sem=sems[1].at[role],
        device_id=device,
        device_id_type=MESH,
    )


def hello(devices):
    barrier = pltpu.get_barrier_semaphore()
    for device in devices:
        pl.semaphore_signal(barrier, inc=1, device_id=device, device_id_type=MESH)
    return len(devices)


def met(count):
    pl.semaphore_wait(pltpu.get_barrier_semaphore(), count)


def greet(devices):
    met(hello(devices))


class Moves:
    def __init__(self, sems):
        self.sems, self.copies = sems, []

    def start(self, source, target):
        copy = pltpu.make_async_copy(source, target, self.sems.at[len(self.copies)])
        copy.start()
        self.copies.append(copy)

    def wait(self, *which):
        for k in which:
            self.copies[k].wait()

    def wait_all(self):
        self.wait(*range(len(self.copies)))


BANK = jax.ShapeDtypeStruct((24, D, D), BF16)


def attention_places(bank):
    rows = pl.ds(0, ROWS)
    return [
        bank.at[1, rows, pl.ds(0, 384)],
        bank.at[0, rows],
        bank.at[1, rows, pl.ds(384, 128)],
        bank.at[2, pl.ds(0, 256)],
        bank.at[2, pl.ds(256, 256)],
    ]


def feed_places(bank):
    rows = pl.ds(0, ROWS)
    return [
        bank.at[1, rows, pl.ds(512, 512)],
        bank.at[0, rows],
        bank.at[1, rows, pl.ds(0, 512)],
        bank.at[2, pl.ds(0, 512)],
        bank.at[2, pl.ds(512, 512)],
    ]


class Row:
    def __init__(self, ref, row):
        self.ref, self.row = ref, row

    def __getitem__(self, index):
        lanes = slice(None) if index is Ellipsis else index[1]
        return self.ref[self.row : self.row + 1, lanes]


def gain_row(l, n):
    return 2 * l + n


def shift_row(l, n):
    return 4 + 4 * l + n


def near(me):
    return [me.member(me.zf, me.c), me.member(me.zb, me.c), me.member(me.z, 1 - me.c)]


def cross(me):
    return [me.plane(me.y, me.xf), me.plane(me.y, me.xb), me.plane(me.yf, me.x), me.plane(me.yb, me.x)]


def nothing(point):
    pass


def gather_steps(out, me, sems):
    ahead, back, other = near(me)
    copies = []

    def send(z, role, device, half=None):
        part = out.at[z, me.c]
        if half is not None:
            part = part.at[half] if len(out.shape) == 5 else part.at[:, pl.ds(half * (D // 2), D // 2)]
        copies.append(remote(part, part, sems, role, device))
        copies[-1].start()
        return copies[-1]

    first, second = [], []
    for half in range(2):
        first.append(send(me.z, half, ahead, half))
        second.append(send(me.z, 2 + half, back, half))
    over = [send(me.z, 6, other)]
    yield
    third = []
    for half in range(2):
        first[half].wait_recv()
        third.append(send(me.zb, 4 + half, ahead, half))
    over.append(send(me.zb, 7, other))
    yield
    for half in range(2):
        second[half].wait_recv()
    over.append(send(me.zf, 8, other))
    for half in range(2):
        third[half].wait_recv()
        over.append(send(me.zo, 9 + half, other, half))
    yield
    for copy in over:
        copy.wait_recv()
    for copy in copies:
        copy.wait_send()


def gather(out, me, sems, beside=nothing):
    for point, _ in enumerate(gather_steps(out, me, sems)):
        beside(3 + point)


def reduce(part, crossed, held, landed, me, sems, produce, begin, beside):
    ahead, back, other = near(me)
    copies = []

    def made(role, z):
        produce(z)
        if role == 0:
            begin()
        copies.append(remote(part.at[z, 1 - me.c], crossed.at[role], sems, role, other))
        copies[-1].start()

    def both(role, z):
        copies[role].wait_recv()
        return part[z, me.c].astype(F32) + crossed[role].astype(F32)

    sent = []

    def send(slot, value, role, device, place=slice(None)):
        held[slot, :, place] = value.astype(BF16)
        copy = remote(held.at[slot, :, place], landed.at[slot, :, place], sems, role, device)
        copy.start()
        sent.append(copy)
        return copy

    halves = (slice(0, D // 2), slice(D // 2, D))
    made(0, me.zo)
    made(1, me.zf)
    beside(0)
    value = both(0, me.zo)
    long = [send(0, value[:, place], 4 + k, ahead, place) for k, place in enumerate(halves)]
    made(2, me.zb)
    short = send(1, both(1, me.zb), 6, back)
    made(3, me.z)
    beside(1)
    value = both(2, me.zf)
    last = []
    for k, place in enumerate(halves):
        long[k].wait_recv()
        last.append(send(2, value[:, place] + landed[0, :, place].astype(F32), 7 + k, ahead, place))
    beside(2)
    total = both(3, me.z)
    short.wait_recv()
    total = total + landed[1].astype(F32)
    for copy in last:
        copy.wait_recv()
    total = total + landed[2].astype(F32)
    return total, copies + sent


def reduce_steps(part, crossed, held, landed, me, sems, finish):
    ahead, back, other = near(me)
    copies = []

    def send(source, target, role, device):
        copies.append(remote(source, target, sems, role, device))
        copies[-1].start()

    def both(role, z):
        copies[role].wait_recv()
        return part[z, me.c].astype(F32) + crossed[role].astype(F32)

    for role, z in enumerate((me.zo, me.zf, me.zb, me.z)):
        send(part.at[z, 1 - me.c], crossed.at[role], role, other)
    yield
    for slot, (z, device) in enumerate(((me.zo, ahead), (me.zb, back))):
        held[slot] = both(slot, z).astype(BF16)
        send(held.at[slot], landed.at[slot], 4 + slot, device)
    yield
    copies[4].wait_recv()
    held[2] = (both(2, me.zf) + landed[0].astype(F32)).astype(BF16)
    send(held.at[2], landed.at[2], 6, ahead)
    yield
    total = both(3, me.z)
    for slot in (1, 2):
        copies[4 + slot].wait_recv()
        total = total + landed[slot].astype(F32)
    finish(total)
    for copy in copies:
        copy.wait_send()


def reduce_scratch():
    return [
        pltpu.VMEM((4, 2, BLOCK, D), BF16),
        pltpu.VMEM((4, BLOCK, D), BF16),
        pltpu.VMEM((3, BLOCK, D), BF16),
        pltpu.VMEM((3, BLOCK, D), BF16),
        pltpu.SemaphoreType.DMA((9,)),
        pltpu.SemaphoreType.DMA((9,)),
    ]


def pair_sems(count):
    return [pltpu.SemaphoreType.DMA((count,)), pltpu.SemaphoreType.DMA((count,))]


def lanes(at, width):
    return pl.ds(pl.multiple_of(at * 128, 128), width)


class Spread:
    def __init__(self, src, dst, me, sems, local):
        self.src, self.dst, self.me, self.sems = src, dst, me, sems
        half = src.shape[0] // 2
        self.a, self.b = pl.ds(0, half), pl.ds(half, half)
        self.copies = {}
        self.keep = pltpu.make_async_copy(src, dst.at[me.xl, :, lanes((me.x // 2) * 4 + me.y, 128)], local)

    def send(self, role, src, dst, device):
        self.copies[role] = remote(src, dst, self.sems, role, device)
        self.copies[role].start()

    def arrived(self, *roles):
        for role in roles:
            self.copies[role].wait_recv()

    def block(self, y, x, rows):
        return self.dst.at[x % 2, rows, lanes((x // 2) * 4 + y, 128)]

    def row(self, role, y, device):
        for hi in range(2):
            part = self.dst.at[:, self.a, lanes(hi * 4 + y, 128)]
            self.send(role + hi, part, part, device)

    def column(self, role, x, device):
        part = self.dst.at[x % 2, self.b, lanes((x // 2) * 4, 512)]
        self.send(role, part, part, device)

    def step(self, number):
        me = self.me
        xf, xb, yf, yb = cross(me)
        if number == 0:
            self.keep.start()
            for role, rows, device in ((0, self.a, xf), (1, self.a, xb), (2, self.b, yf), (3, self.b, yb)):
                self.send(role, self.src.at[rows], self.block(me.y, me.x, rows), device)
        elif number == 1:
            self.arrived(0, 2)
            self.send(4, self.block(me.y, me.xb, self.a), self.block(me.y, me.xb, self.a), xf)
            self.send(5, self.block(me.yb, me.x, self.b), self.block(me.yb, me.x, self.b), yf)
        elif number == 2:
            self.keep.wait()
            self.arrived(1, 4)
            self.row(6, me.y, yf)
            self.row(8, me.y, yb)
            self.arrived(3, 5)
            self.column(10, me.x, xf)
            self.column(11, me.x, xb)
        elif number == 3:
            self.arrived(6, 7)
            self.row(12, me.yb, yf)
            self.arrived(10)
            self.column(14, me.xb, xf)
        else:
            self.arrived(8, 9, 11, 12, 13, 14)
            for copy in self.copies.values():
                copy.wait_send()


def spread_scratch():
    return pair_sems(15) + [pltpu.SemaphoreType.DMA((1,))]


class Collect:
    def __init__(self, src, out, me, bufs):
        self.src, self.out, self.me = src, out, me
        self.rows_in, self.rows_held, self.cols_in, self.cols_held, self.one_in, self.one_held, *self.sems = bufs
        half = src.shape[1] // 2
        self.a, self.b = pl.ds(0, half), pl.ds(half, half)
        self.half = half
        self.copies = {}

    def send(self, role, src, dst, device):
        self.copies[role] = remote(src, dst, self.sems, role, device)
        self.copies[role].start()

    def arrived(self, *roles):
        for role in roles:
            self.copies[role].wait_recv()

    def column(self, x):
        return self.src.at[x % 2, self.a, lanes((x // 2) * 4, 512)]

    def row(self, y, hi):
        return self.src.at[:, self.b, lanes(hi * 4 + y, 128)]

    def step(self, number):
        me = self.me
        xf, xb, yf, yb = cross(me)
        if number == 0:
            self.send(0, self.column(me.xo), self.cols_in.at[0], xf)
            self.send(1, self.column(me.xb), self.cols_in.at[1], xb)
            for hi in range(2):
                self.send(3 + hi, self.row(me.yo, hi), self.rows_in.at[0, hi], yf)
                self.send(5 + hi, self.row(me.yb, hi), self.rows_in.at[1, hi], yb)
        elif number == 1:
            self.arrived(0)
            self.cols_held[0] = (self.column(me.xf)[...].astype(F32) + self.cols_in[0].astype(F32)).astype(BF16)
            self.send(2, self.cols_held.at[0], self.cols_in.at[2], xf)
            self.arrived(3, 4)
            for hi in range(2):
                self.rows_held[0, hi] = (self.row(me.yf, hi)[...].astype(F32) + self.rows_in[0, hi].astype(F32)).astype(BF16)
                self.send(7 + hi, self.rows_held.at[0, hi], self.rows_in.at[2, hi], yf)
        elif number == 2:
            self.arrived(1, 2)
            self.cols_held[1] = (
                self.column(me.x)[...].astype(F32) + self.cols_in[1].astype(F32) + self.cols_in[2].astype(F32)
            ).astype(BF16)
            self.send(9, self.cols_held.at[1, :, lanes(me.yo, 128)], self.one_in.at[0], yf)
            self.send(10, self.cols_held.at[1, :, lanes(me.yb, 128)], self.one_in.at[1], yb)
            self.arrived(5, 6, 7, 8)
            for hi in range(2):
                self.rows_held[1, hi] = (
                    self.row(me.y, hi)[...].astype(F32)
                    + self.rows_in[1, hi].astype(F32)
                    + self.rows_in[2, hi].astype(F32)
                ).astype(BF16)
            self.send(12, self.rows_held.at[1, me.xo // 2, me.xo % 2], self.one_in.at[3], xf)
            self.send(13, self.rows_held.at[1, me.xb // 2, me.xb % 2], self.one_in.at[4], xb)
        elif number == 3:
            self.arrived(9)
            self.one_held[0] = (self.cols_held[1, :, lanes(me.yf, 128)].astype(F32) + self.one_in[0].astype(F32)).astype(BF16)
            self.send(11, self.one_held.at[0], self.one_in.at[2], yf)
            self.arrived(12)
            self.one_held[1] = (self.rows_held[1, me.xf // 2, me.xf % 2].astype(F32) + self.one_in[3].astype(F32)).astype(BF16)
            self.send(14, self.one_held.at[1], self.one_in.at[5], xf)
        else:
            self.arrived(10, 11)
            self.out[self.a, :] = (
                self.cols_held[1, :, lanes(me.y, 128)].astype(F32)
                + self.one_in[1].astype(F32)
                + self.one_in[2].astype(F32)
            )
            self.arrived(13, 14)
            self.out[self.b, :] = (
                self.rows_held[1, me.x // 2, me.x % 2].astype(F32)
                + self.one_in[4].astype(F32)
                + self.one_in[5].astype(F32)
            )
            for copy in self.copies.values():
                copy.wait_send()


def collect_scratch(n):
    half = n // 2
    return [
        pltpu.VMEM((3, 2, 2, half, 128), BF16),
        pltpu.VMEM((2, 2, 2, half, 128), BF16),
        pltpu.VMEM((3, half, 512), BF16),
        pltpu.VMEM((2, half, 512), BF16),
        pltpu.VMEM((6, half, 128), BF16),
        pltpu.VMEM((2, half, 128), BF16),
    ] + pair_sems(15)


def row_stats(v):
    mean = jnp.sum(v, axis=1, keepdims=True) / D
    square = jnp.sum(v * v, axis=1, keepdims=True) / D
    return mean, lax.rsqrt(square - mean * mean + EPS)


def normed(v, gain, bias):
    mean, inv = row_stats(v)
    return ((v - mean) * inv * gain + bias).astype(BF16)


def call(body, identity, inputs, in_specs, out_shape, out_specs, scratch):
    return pl.pallas_call(
        body,
        out_shape=out_shape,
        in_specs=in_specs,
        out_specs=out_specs,
        scratch_shapes=scratch,
        cost_estimate=pl.CostEstimate(flops=20_000_000_000, bytes_accessed=40_000_000, transcendentals=0),
        compiler_params=pltpu.CompilerParams(
            collective_id=identity, has_side_effects=True, vmem_limit_bytes=24 * 1024 * 1024
        ),
    )(*inputs)


def half_swap(left, right, low):
    return jnp.where(low, left, pltpu.roll(right, 64, 1)), jnp.where(low, pltpu.roll(left, 64, 1), right)


def unfold(blocks, out, change):
    low = low_lanes(BLOCK)

    def rows(index, carry):
        start = pl.multiple_of(index * BLOCK, BLOCK)
        for z in range(4):
            for p in range(2):
                left, right = (blocks[z, c, p, pl.ds(start, BLOCK)].astype(F32) for c in range(2))
                for half, value in enumerate(half_swap(left, right, low)):
                    at = pl.ds(pl.multiple_of(half * (ROWS // 2) + start, BLOCK), BLOCK)
                    out[at, pl.ds((p * 4 + z) * 128, 128)] = change(value).astype(out.dtype)
        return carry

    lax.fori_loop(0, 4, rows, 0)


def open_kernel(
    x_ref, x2_ref, w_ref, s_ref, in_ref, state_ref, wide_ref, vec_ref, qkv_ref, up_ref, cot_ref,
    y_ref, tok_ref, sw_ref, st_ref, comp, local, *sems
):
    me = Place()
    greet([me.sharer(k) for k in range(1, 16)] + [me.member_at(k) for k in range(1, 8)])
    mine = y_ref.at[me.z, me.c, me.xl]
    neighbour = (me.d, me.z * 4 + (1 - me.xl) * 2 + me.c)
    swap = remote(x_ref.at[1 - me.xl], mine, sems[0:2], 0, neighbour)
    swap.start()
    keep = pltpu.make_async_copy(x_ref.at[me.xl], mine, local.at[0])
    keep.start()
    cot_ref[me.xl] = x2_ref[me.xl]
    small = [remote(s_ref, sw_ref.at[me.w], sems[2:4], k - 1, me.sharer(k)) for k in range(1, 16)]
    for copy in small:
        copy.start()
    wide = Spread(w_ref, wide_ref, me, sems[4:6], local.at[1])
    wide.step(0)
    swap_cot = remote(x2_ref.at[1 - me.xl], cot_ref.at[me.xl], sems[0:2], 1, neighbour)
    swap_cot.start()
    sw_ref[me.w] = s_ref[...]
    keep.wait()
    swap.wait()
    spread = []
    low = lax.broadcasted_iota(jnp.int32, (16, 128), 1) < 64

    def beside(point):
        wide.step(point - 2)
        if point == 3:
            for copy in small:
                copy.wait()
            comp[...] = sum(pltpu.roll(sw_ref[w], (w % 2) * 64 + (w // 2) * 8, 1) for w in range(16))
            st_ref[me.z, me.c] = comp[...]
            for k in range(1, 8):
                spread.append(remote(comp, st_ref.at[me.z, me.c], sems[6:8], k - 1, me.member_at(k)))
                spread[-1].start()
            pair = []
            for p in range(2):
                pair.append(sum(pltpu.roll(sw_ref[2 * d + p], d * 16, 1) for d in range(8)))
                for k in range(2):
                    value = sum(pltpu.roll(sw_ref[2 * d + p], (d % 4) * 32, 1) for d in range(4 * k, 4 * k + 4))
                    up_ref[:, (p * 2 + k) * 128 : (p * 2 + k + 1) * 128] = value
            swapped = half_swap(*pair, low)
            qkv_ref[:, :128] = jnp.where(low, pair[0], 0.0)
            qkv_ref[:, 128:256] = jnp.where(low, pltpu.roll(pair[0], 64, 1), swapped[0])
            qkv_ref[:, 256:] = jnp.where(low, 0.0, pair[1])

    gather(y_ref, me, sems[8:10], beside)
    for copy in spread:
        copy.wait()
    for z in range(4):
        for p, value in enumerate(half_swap(st_ref[z, 0], st_ref[z, 1], low)):
            vec_ref[:, (p * 4 + z) * 128 : (p * 4 + z + 1) * 128] = value
    unfold(y_ref, tok_ref, lambda v: v)

    def rows(index, carry):
        at = pl.ds(pl.multiple_of(index * BLOCK, BLOCK), BLOCK)
        in_ref[at, :] = normed(tok_ref[at, :], vec_ref[0:1, :], vec_ref[4:5, :])
        return carry

    lax.fori_loop(0, 8, rows, 0)
    state_ref[...] = tok_ref[pl.ds(pl.multiple_of(me.j * BLOCK, BLOCK), BLOCK), :]
    swap_cot.wait()
    wide.step(4)


FOLDED = (4, 2, 2, ROWS // 2, 128)


def open_call(x, x2, w, s):
    return call(
        open_kernel,
        0,
        (x, x2, w, s),
        [VMEM, VMEM, ANY, VMEM],
        [
            jax.ShapeDtypeStruct((ROWS, D), BF16),
            jax.ShapeDtypeStruct((BLOCK, D), F32),
            jax.ShapeDtypeStruct((2, w.shape[0], D), BF16),
            jax.ShapeDtypeStruct((16, D), F32),
            jax.ShapeDtypeStruct((16, 384), F32),
            jax.ShapeDtypeStruct((16, 512), F32),
            jax.ShapeDtypeStruct((2, ROWS // 2, 128), BF16),
        ],
        [VMEM] * 2 + [ANY] + [VMEM] * 4,
        [
            pltpu.VMEM(FOLDED, BF16),
            pltpu.VMEM((ROWS, D), F32),
            pltpu.VMEM((16, 16, 128), F32),
            pltpu.VMEM((4, 2, 16, 128), F32),
            pltpu.VMEM((16, 128), F32),
            pltpu.SemaphoreType.DMA((2,)),
        ]
        + pair_sems(2)
        + pair_sems(15)
        + pair_sems(15)
        + pair_sems(7)
        + pair_sems(11),
    )


PAIR = 2 * BLOCK
QKV_SCRATCH = [pltpu.VMEM((384, D), BF16), pltpu.VMEM((128, D), BF16), pltpu.VMEM((6, ROWS, 128), BF16)]


def pair_rows(z):
    return pl.ds(pl.multiple_of(z * PAIR, PAIR), PAIR)


def dot(a, b, contract=(1, 0)):
    return lax.dot_general(a, b, (((contract[0],), (contract[1],)), ((), ())), preferred_element_type=F32)


def low_lanes(rows):
    return lax.broadcasted_iota(jnp.int32, (rows, 128), 1) < 64


def load_projections(wide, wq, wo):
    for p in range(2):
        wq[p * 192 : (p + 1) * 192, :] = wide[p, 0:192, :]
        wo[p * 64 : (p + 1) * 64, :] = wide[p, 192:256, :]


def turn(at, tiles, turned):
    low = low_lanes(PAIR)
    swapped = [pltpu.roll(tile, 64, 1) for tile in tiles]
    for index, tile in enumerate(swapped):
        turned[index, at, :] = tile.astype(BF16)
    turned[3, at, :] = jnp.where(low, tiles[0], 0.0).astype(BF16)
    turned[4, at, :] = jnp.where(low, swapped[1], 0.0).astype(BF16)


def score_rows(head, at, mixed, turned):
    keys = turned[0] if head == 0 else mixed[:, 256:384]
    scores = 64 ** (-0.5) * dot(turned[3 + head, at, :], keys, (1, 1))
    return jnp.where(lax.broadcasted_iota(jnp.int32, scores.shape, 1) < SEQ, scores, -1e30)


def store_part(part, z, value):
    part[z] = value.astype(BF16).reshape(2, BLOCK, D)


def forward_tail(me, refs, produce, begin, wide, state, shift, gain, bias, new_ref, out_ref, complete):
    part, crossed, held, landed, s0, s1, s2, s3 = refs

    def beside(point):
        complete(point)
        if wide is not None and point in (1, 2, 4):
            wide.step((None, 1, 2, None, 3)[point])

    total, copies = reduce(part, crossed, held, landed, me, (s0, s1), produce, begin, beside)
    value = state[...] + (total + shift[...])
    new_ref[...] = value
    if out_ref is not None:
        out_ref[me.z, me.c] = normed(value, gain[...], bias[...])
        gather(out_ref, me, (s2, s3), beside)
    for copy in copies:
        copy.wait_send()
    if wide is not None:
        wide.step(4)


def attention_kernel(
    banked, layer, in_ref, mine_ref, qkv_ref, state, vec_ref, w_ref, *rest
):
    qkv_shift = Row(qkv_ref, 12 + layer)
    shift, gain, bias = (Row(vec_ref, r) for r in (shift_row(layer, 1), gain_row(layer, 1), shift_row(layer, 2)))
    if banked:
        counts_ref, x_ref, *rest = rest
    new_ref, out_ref, wide_ref, total_ref, *rest = rest
    if banked:
        bank, cot_ref, above_ref, mixed, attended, wq, wo, turned, *rest = rest
        moves = Moves(rest[11])
        places = attention_places(bank)
        moves.start(in_ref, places[1])
        for p in range(2):
            moves.start(mine_ref.at[p], places[3 + p])
    else:
        mixed, attended, wq, wo, turned, *rest = rest
    me = Place()
    count = hello(near(me) + cross(me))
    wide = Spread(w_ref, wide_ref, me, rest[8:10], rest[10].at[0])
    load_projections(mine_ref, wq, wo)

    def project(index, carry):
        at = pair_rows(index)
        value = dot(in_ref[at, :], wq[...], (1, 1)) + qkv_shift[...]
        mixed[at, :] = value.astype(BF16)
        turn(at, [value[:, k * 128 : (k + 1) * 128] for k in range(3)], turned)
        return carry

    project(0, 0)
    met(count)
    wide.step(0)
    if banked:
        folded, cot_sems = rest[12], rest[13:15]
        folded[me.z, me.c] = x_ref[...]
        cot_steps = gather_steps(folded, me, cot_sems)
        next(cot_steps)
    lax.fori_loop(1, 4, project, 0)

    def produce(z):
        at = pair_rows(z)
        parts = []
        for head in range(2):
            scores = score_rows(head, at, mixed, turned)
            row_max = jnp.max(scores, axis=1, keepdims=True)
            shifted = jnp.exp(scores - row_max)
            row_total = jnp.sum(shifted, axis=1, keepdims=True)
            soft = (shifted / row_total).astype(BF16)
            parts.append((dot(soft, mixed[:, 128 + head * 128 : 256 + head * 128]), row_max + jnp.log(row_total)))
        low = low_lanes(PAIR)
        value = jnp.where(low, parts[0][0], parts[1][0]).astype(BF16)
        attended[at, :] = value
        total_ref[at, :] = jnp.where(low, parts[0][1], parts[1][1])
        store_part(rest[0], z, dot(value, wo[...]))

    def complete(point):
        if banked and point == 1:
            moves.start(mixed, places[0])
            moves.start(attended, places[2])
        if banked and point in (1, 3, 5):
            next(cot_steps, None)

    forward_tail(me, rest[:8], produce, lambda: None, wide, state, shift, gain, bias, new_ref, out_ref, complete)
    if banked:
        live = jnp.where(me.xl < counts_ref[me.d], 1.0, 0.0)
        unfold(folded, cot_ref, lambda v: v * live)
        above_ref[...] = cot_ref[pl.ds(pl.multiple_of(me.j * BLOCK, BLOCK), BLOCK), :].astype(F32)
        moves.wait_all()


def attention_call(identity, layer, first_in, mine, qkv_shift, state, vectors, w, counts=None, x=None):
    banked = x is not None
    kept = [jax.ShapeDtypeStruct((ROWS, 384), BF16), jax.ShapeDtypeStruct((ROWS, 128), BF16)]
    return call(
        functools.partial(attention_kernel, banked, layer),
        identity,
        (first_in, mine, qkv_shift, state, vectors, w) + ((counts, x) if banked else ()),
        [VMEM] * 5 + [ANY] + ([pl.BlockSpec(memory_space=pltpu.SMEM), VMEM] if banked else []),
        [
            jax.ShapeDtypeStruct((BLOCK, D), F32),
            jax.ShapeDtypeStruct((4, 2, BLOCK, D), BF16),
            jax.ShapeDtypeStruct((2, w.shape[0], D), BF16),
            jax.ShapeDtypeStruct((ROWS, 128), F32),
        ]
        + ([BANK, jax.ShapeDtypeStruct((ROWS, D), BF16), jax.ShapeDtypeStruct((BLOCK, D), F32)] if banked else kept),
        [VMEM, VMEM, ANY, VMEM] + ([ANY, VMEM, VMEM] if banked else [VMEM] * 2),
        ([pltpu.VMEM(v.shape, v.dtype) for v in kept] if banked else [])
        + QKV_SCRATCH
        + reduce_scratch()
        + pair_sems(11)
        + spread_scratch()
        + (
            [pltpu.SemaphoreType.DMA((5,)), pltpu.VMEM(FOLDED, BF16)] + pair_sems(11)
            if banked
            else []
        ),
    )


def feed_rows(at, in_ref, mine, up_shift, activated, slope):
    rows = in_ref[at, :]
    total = 0.0
    for p in range(2):
        place = pl.ds(p * 256, 256)
        value = dot(rows, mine[p, 0:256, :], (1, 1)) + up_shift[:, place]
        normal = 0.5 * (1.0 + lax.erf(value * 0.5**0.5))
        active = (value * normal).astype(BF16)
        activated[at, place] = active
        slope[at, place] = (normal + value * jnp.exp(-0.5 * value * value) * (0.5 / jnp.pi) ** 0.5).astype(BF16)
        total = total + dot(active, mine[p, 256:512, :])
    return total


def feed_back_rows(at, grad_ref, mine, slope, d_pre):
    rows = grad_ref[at, :]
    total = 0.0
    for p in range(2):
        place = pl.ds(p * 256, 256)
        value = (dot(rows, mine[p, 256:512, :], (1, 1)) * slope[at, place]).astype(BF16)
        d_pre[at, place] = value
        total = total + dot(value, mine[p, 0:256, :])
    return total


def feed_kernel(
    layer, in_ref, mine, up_ref, state, vec_ref, w_ref, new_ref, out_ref, wide_ref, bank, activated, slope, *rest
):
    up_shift = Row(up_ref, 14 + layer)
    shift, gain, bias = (Row(vec_ref, r) for r in (shift_row(layer, 3), gain_row(layer + 1, 0), shift_row(layer + 1, 0)))
    moves = Moves(rest[11])
    places = feed_places(bank)
    moves.start(in_ref, places[1])
    for p in range(2):
        moves.start(mine.at[p], places[3 + p])
    me = Place()
    count = hello(near(me) + cross(me))
    wide = Spread(w_ref, wide_ref, me, rest[8:10], rest[10].at[0])

    def begin():
        met(count)
        wide.step(0)

    def produce(z):
        store_part(rest[0], z, feed_rows(pair_rows(z), in_ref, mine, up_shift, activated, slope))

    def complete(point):
        if point == 1:
            moves.start(slope, places[0])
            moves.start(activated, places[2])

    forward_tail(me, rest[:8], produce, begin, wide, state, shift, gain, bias, new_ref, out_ref, complete)
    moves.wait_all()


def feed_call(identity, layer, second_in, mine, up_shift, state, vectors, w):
    kept = [pltpu.VMEM((ROWS, 512), BF16)] * 2
    return call(
        functools.partial(feed_kernel, layer),
        identity,
        [second_in, mine, up_shift, state, vectors, w],
        [VMEM] * 5 + [ANY],
        [
            jax.ShapeDtypeStruct((BLOCK, D), F32),
            jax.ShapeDtypeStruct((4, 2, BLOCK, D), BF16),
            jax.ShapeDtypeStruct((2, w.shape[0], D), BF16),
            BANK,
        ],
        [VMEM, VMEM, ANY, ANY],
        kept + reduce_scratch() + pair_sems(11) + spread_scratch() + [pltpu.SemaphoreType.DMA((5,))],
    )


def weight_product(left, right, out, heads):
    size = left.shape[1] // 2

    def tile(index, carry):
        at = lanes(index * 2, 256)
        value = lax.dot_general(left[...], right[:, at], (((0,), (0,)), ((), ())), preferred_element_type=F32).astype(BF16)
        for p in range(2):
            out[p, pl.ds(heads, size), at] = value[p * size : (p + 1) * size]
        return carry

    lax.fori_loop(0, 4, tile, 0)


def norm_back(total, base, above, gain):
    mean, inv = row_stats(base)
    hat = (base - mean) * inv
    weighted = total * gain
    first = jnp.sum(weighted, axis=1, keepdims=True) / D
    second = jnp.sum(weighted * hat, axis=1, keepdims=True) / D
    return above + inv * (weighted - first - hat * second), total * hat


def backward_tail(
    me, refs, produce, begin, slots, products, weight_ref, base, above, gain, new_ref, sums_ref, out_ref, also=nothing
):
    part, crossed, held, landed, s0, s1, s2, s3 = refs

    def beside(point):
        also(point)
        if point == 1:
            weight_product(*products[0], weight_ref, 0)
        if point == 3:
            weight_product(*products[1], weight_ref, products[0][0].shape[1] // 2)
        if slots is not None and point in (2, 3, 4):
            slots.step(point - 1)

    total, copies = reduce(part, crossed, held, landed, me, (s0, s1), produce, begin, beside)
    value, by_hat = norm_back(total, base[...], above[...], gain[...])
    new_ref[...] = value
    low = value.astype(BF16)
    out_ref[me.z, me.c] = low
    for row, each in enumerate((by_hat, total, low.astype(F32), above[...])):
        sums_ref[row : row + 1, :] = jnp.sum(each, axis=0, keepdims=True)
    sums_ref[4:8, :] = jnp.zeros((4, D), F32)
    gather(out_ref, me, (s2, s3), beside)
    for copy in copies:
        copy.wait_send()
    if slots is not None:
        slots.step(4)


def feed_back_kernel(
    layer, grad_ref, base, above, vec_ref, bank, w_ref, new_ref, sums_ref, weight_ref, out_ref, bias_ref, owned_ref,
    slope, second_in, activated, mine, fetched, d_pre, *rest
):
    moves = Moves(fetched)
    for source, target in zip(feed_places(bank), (slope, second_in, activated, mine.at[0], mine.at[1])):
        moves.start(source, target)
    me = Place()
    count = hello(near(me) + cross(me))
    moves.wait_all()
    slots = Collect(w_ref, owned_ref, me, rest[8:])

    def begin():
        met(count)
        slots.step(0)

    def produce(z):
        store_part(rest[0], z, feed_back_rows(pair_rows(z), grad_ref, mine, slope, d_pre))

    products = ((d_pre, second_in), (activated, grad_ref))
    gain = Row(vec_ref, gain_row(layer, 1))
    backward_tail(
        me, rest[:8], produce, begin, slots, products, weight_ref, base, above, gain, new_ref, sums_ref, out_ref
    )
    bias_ref[...] = jnp.sum(d_pre[...].astype(F32), axis=0, keepdims=True)


def turn_kernel(
    layer, in_ref, mine, up_ref, state, vec_ref, grad_ref, above, last_ref, new_ref, sums_ref, weight_ref, out_ref,
    bias_ref, activated, slope, d_pre, *rest
):
    up_shift, shift, gain = Row(up_ref, 14 + layer), Row(vec_ref, shift_row(layer, 3)), Row(vec_ref, gain_row(layer, 1))
    me = Place()
    count = hello(near(me))
    second, s0, s1 = rest[8:12], rest[12], rest[13]

    def produce(z):
        at = pair_rows(z)
        store_part(second[0], z, feed_rows(at, in_ref, mine, up_shift, activated, slope))
        store_part(rest[0], z, feed_back_rows(at, grad_ref, mine, slope, d_pre))

    def finish(total):
        last_ref[...] = state[...] + (total + shift[...])

    steps = reduce_steps(*second, me, (s0, s1), finish)

    def also(point):
        if point in (1, 2, 3, 5):
            next(steps, None)

    products = ((d_pre, in_ref), (activated, grad_ref))
    begin = functools.partial(met, count)
    backward_tail(
        me, rest[:8], produce, begin, None, products, weight_ref, state, above, gain, new_ref, sums_ref, out_ref, also
    )
    bias_ref[...] = jnp.sum(d_pre[...].astype(F32), axis=0, keepdims=True)


def backward_shapes(size):
    return [
        jax.ShapeDtypeStruct((BLOCK, D), F32),
        jax.ShapeDtypeStruct((8, D), F32),
        jax.ShapeDtypeStruct((2, size, D), BF16),
        jax.ShapeDtypeStruct((4, 2, BLOCK, D), BF16),
    ]


def feed_back_call(identity, layer, grad, base, above, vectors, bank, w):
    out_shape = backward_shapes(512) + [
        jax.ShapeDtypeStruct((1, 512), F32),
        jax.ShapeDtypeStruct((w.shape[1], 128), F32),
    ]
    scratch = [
        pltpu.VMEM((ROWS, 512), BF16),
        pltpu.VMEM((ROWS, D), BF16),
        pltpu.VMEM((ROWS, 512), BF16),
        pltpu.VMEM((2, 512, D), BF16),
        pltpu.SemaphoreType.DMA((5,)),
        pltpu.VMEM((ROWS, 512), BF16),
    ]
    scratch += reduce_scratch() + pair_sems(11) + collect_scratch(w.shape[1])
    inputs = [grad, base, above, vectors, bank, w]
    in_specs = [VMEM] * 4 + [ANY, VMEM]
    body = functools.partial(feed_back_kernel, layer)
    return call(body, identity, inputs, in_specs, out_shape, [VMEM] * len(out_shape), scratch)


def turn_call(identity, layer, second_in, mine, up_shift, state, vectors, grad, above):
    out_shape = [jax.ShapeDtypeStruct((BLOCK, D), F32)] + backward_shapes(512) + [jax.ShapeDtypeStruct((1, 512), F32)]
    scratch = [pltpu.VMEM((ROWS, 512), BF16)] * 3 + reduce_scratch() + pair_sems(11) + reduce_scratch()
    inputs = [second_in, mine, up_shift, state, vectors, grad, above]
    body = functools.partial(turn_kernel, layer)
    return call(body, identity, inputs, [VMEM] * len(inputs), out_shape, [VMEM] * len(out_shape), scratch)


BACK_SCRATCH = QKV_SCRATCH + [
    pltpu.VMEM((ROWS, 384), BF16),
    pltpu.VMEM((3, ROWS, 128), BF16),
    pltpu.VMEM((6, ROWS, 128), F32),
]


def attention_back(grad_ref, mine, mixed, total_ref, bufs, begin, between=None):
    wq, wo, turned, d_mixed, d_att, sums = bufs
    load_projections(mine, wq, wo)
    low = low_lanes(PAIR)

    def ready(index, carry):
        at = pair_rows(index)
        tiles = [mixed[at, k * 128 : (k + 1) * 128].astype(F32) for k in range(3)]
        turn(at, tiles, turned)
        value = dot(grad_ref[at, :], wo[...], (1, 1))
        d_att[0, at, :] = value.astype(BF16)
        d_att[1, at, :] = jnp.where(low, value, 0.0).astype(BF16)
        d_att[2, at, :] = jnp.where(low, 0.0, value).astype(BF16)
        return carry

    lax.fori_loop(0, 4, ready, 0)
    begin()
    for k in range(2, 6):
        sums[k] = jnp.zeros((ROWS, 128), F32)

    def chunk(index, carry):
        at = pair_rows(index)
        grads = d_att[0, at, :]
        for head in range(2):
            soft = jnp.exp(score_rows(head, at, mixed, turned) - total_ref[at, head * 64 : head * 64 + 1])
            d_soft = dot(d_att[1 + head, at, :], mixed[:, 128 + head * 128 : 256 + head * 128], (1, 1))
            sums[2 + head] += dot(soft.astype(BF16), grads, (0, 0))
            d_scores = (soft * (d_soft - jnp.sum(soft * d_soft, axis=1, keepdims=True))).astype(BF16)
            sums[head, at, :] = dot(d_scores, turned[2 * head])
            sums[4 + head] += dot(d_scores, turned[head, at, :], (0, 0))
        return carry

    lax.fori_loop(0, 4, chunk, 0)
    if between is not None:
        between()

    def join(index, carry):
        at = pair_rows(index)
        scale = 64 ** (-0.5)
        d_mixed[at, 0:128] = (scale * jnp.where(low, sums[0, at, :], sums[4, at, :])).astype(BF16)
        d_mixed[at, 128:256] = jnp.where(low, sums[2, at, :], scale * sums[1, at, :]).astype(BF16)
        d_mixed[at, 256:384] = jnp.where(low, scale * sums[5, at, :], sums[3, at, :]).astype(BF16)
        return carry

    lax.fori_loop(0, 4, join, 0)

    def produce(part, z):
        store_part(part, z, dot(d_mixed[pair_rows(z), :], wq[...]))

    return produce


def attention_back_kernel(layer, grad_ref, *refs):
    kept, (above, vec_ref, w_ref, new_ref, sums_ref, weight_ref, out_ref, bias_ref, owned_ref) = refs[:6], refs[6:15]
    bufs, rest = refs[15:21], refs[21:]
    gain = Row(vec_ref, gain_row(layer, 0))
    mine, mixed, total_ref, base, first_in, attended = kept
    me = Place()
    count = hello(near(me) + cross(me))
    slots = Collect(w_ref, owned_ref, me, rest[8:])

    def begin():
        met(count)
        slots.step(0)

    produce = attention_back(grad_ref, mine, mixed, total_ref, bufs, begin)
    produce = functools.partial(produce, rest[0])
    products = ((bufs[3], first_in), (attended, grad_ref))
    backward_tail(
        me, rest[:8], produce, lambda: None, slots, products, weight_ref, base, above, gain, new_ref, sums_ref, out_ref
    )
    bias_ref[...] = jnp.sum(bufs[3][...].astype(F32), axis=0, keepdims=True)


def attention_back_call(identity, layer, grad, mine, mixed, totals, base, first_in, attended, above, vectors, w):
    inputs = [grad, mine, mixed, totals, base, first_in, attended, above, vectors, w]
    in_specs = [VMEM] * 10
    out_shape = backward_shapes(256) + [
        jax.ShapeDtypeStruct((1, 384), F32),
        jax.ShapeDtypeStruct((w.shape[1], 128), F32),
    ]
    scratch = BACK_SCRATCH + reduce_scratch() + pair_sems(11) + collect_scratch(w.shape[1])
    body = functools.partial(attention_back_kernel, layer)
    return call(body, identity, inputs, in_specs, out_shape, [VMEM] * len(out_shape), scratch)


def close_kernel(
    counts_ref, grad_in, bank, total_ref, base, above, vec_in, w_ref, state_ref, up_sums, mid_sums, down_sums,
    up_bias, mid_bias, down_bias,
    out_ref, grad_ref, vec_out, bias_out, owned_w, owned_p,
    product, low_ref, vec_ref, from_t, mine, from_w, own_bias, rows_ref, local,
    mixed, first_in, attended, weights, fetched, *rest
):
    me = Place()
    bufs, rest = rest[:6], rest[6:]
    part, crossed, held, landed, s0, s1 = rest[:6]
    sems, rest = rest[6:14], rest[14:]
    tensor = [(me.d, (me.t + k) % 16) for k in range(1, 16)]
    plane = [((me.d + k) % 8, me.z * 4 + xl * 2 + me.c) for k in range(1, 8) for xl in range(2)]
    moves = Moves(fetched)
    targets = (mixed, first_in, attended, weights.at[0], weights.at[1])
    for source, target in zip(attention_places(bank), targets):
        moves.start(source, target)
    count = hello(tensor + plane)
    moves.wait_all()
    slots_w = Collect(w_ref, owned_w, me, rest[:8])
    slots_p = Collect(product, owned_p, me, rest[8:])

    def scatter(source, target, sems, local):
        def features(t):
            return source.at[:, lanes(((t // 2) % 2) * 4 + t // 4, 128)]

        keep = pltpu.make_async_copy(features(me.t), target.at[me.xl, me.j], local)
        keep.start()
        copies = []
        for k in range(1, 16):
            t = (me.t + k) % 16
            copies.append(remote(features(t), target.at[me.xl, me.j], sems, k - 1, (me.d, t)))
            copies[-1].start()
        return keep, copies

    def share(source, target, sems, local):
        keep = pltpu.make_async_copy(source.at[me.xl], target.at[me.w], local)
        keep.start()
        copies = []
        for k in range(1, 16):
            xl = (me.w + k) % 2
            copies.append(remote(source.at[xl], target.at[me.w], sems, k - 1, me.sharer(k)))
            copies[-1].start()
        return keep, copies

    def finish(started):
        started[0].wait()
        for copy in started[1]:
            copy.wait()

    open_ends = []

    def beside(point):
        if point == 1:
            weight_product(bufs[3], first_in, product, 0)
            weight_product(attended, grad_in, product, 192)
            slots_p.step(0)
            slots_w.step(2)
            low = low_lanes(8)
            own_bias[...] = jnp.zeros_like(own_bias)
            for l, each in enumerate((down_bias, up_bias)):
                for p in range(2):
                    for k in range(2):
                        at = (2 * p + k) * 128
                        own_bias[p, 2 * l + k : 2 * l + k + 1, :] = each[:, at : at + 128]
            for l, each in enumerate((jnp.sum(bufs[3][...].astype(F32), axis=0, keepdims=True), mid_bias[...])):
                tiles = [jnp.broadcast_to(each[:, k * 128 : (k + 1) * 128], (8, 128)) for k in range(3)]
                turned = pltpu.roll(tiles[1], 64, 1)
                own_bias[0, 4 + l : 5 + l, :] = jnp.where(low, tiles[0], turned)[0:1]
                own_bias[1, 4 + l : 5 + l, :] = jnp.where(low, turned, tiles[2])[0:1]
        elif point == 2:
            slots_p.step(1)
            slots_w.step(3)

    def begin():
        met(count)
        slots_w.step(0)
        live = jnp.where(me.xl < counts_ref[me.d], 1.0, 0.0)
        rows_ref[...] = (state_ref[...] * live).astype(BF16)
        open_ends.append(scatter(rows_ref, out_ref, sems[0:2], local.at[0]))

    produce = attention_back(grad_in, weights, mixed, total_ref, bufs, begin, lambda: slots_w.step(1))
    produce = functools.partial(produce, part)
    total, copies = reduce(part, crossed, held, landed, me, (s0, s1), produce, lambda: None, beside)
    value, by_hat = norm_back(total, base[...], above[...], vec_in[0:1, :])
    low_ref[...] = value.astype(BF16)
    own = [jnp.sum(each, axis=0, keepdims=True) for each in (by_hat, total)]
    up, mid, down = ([ref[row : row + 1, :] for row in range(4)] for ref in (up_sums, mid_sums, down_sums))
    order = (own[0], down[0], mid[0], up[0], own[1], down[2], down[1], mid[2], mid[1], up[2], up[1], up[3])
    vec_ref[...] = jnp.zeros_like(vec_ref)
    for row, each in enumerate(order):
        for p in range(2):
            vec_ref[p, row : row + 1, :] = each[:, p * 512 : (p + 1) * 512]

    def vec(z):
        return vec_ref.at[:, :, lanes(z, 128)]

    keep = pltpu.make_async_copy(vec(me.z), from_t.at[me.j], local.at[3])
    keep.start()
    first = []
    for k in range(1, 8):
        j = (me.j + k) % 8
        first.append(remote(vec(j // 2), from_t.at[me.j], sems[4:6], k - 1, me.member(j // 2, j % 2)))
        first[-1].start()
    open_ends.append(scatter(low_ref, grad_ref, sems[2:4], local.at[1]))
    finish((keep, first))
    mine[:, 0:16, :] = sum(from_t[j] for j in range(8))
    mine[:, 16:24, :] = own_bias[...]
    second = share(mine, from_w, sems[6:8], local.at[2])
    slots_p.step(2)
    slots_w.step(4)
    slots_p.step(3)
    finish(second)
    total = sum(from_w[w] for w in range(16))
    at_lane = 128 - (me.c * 64 + me.d * 8)
    vec_out[...] = pltpu.roll(total[0:16], at_lane % 128, 1)
    for started in open_ends:
        finish(started)
    bias = total[16:24]
    for l in range(LAYERS):
        fc1 = jnp.where(me.d < 4, bias[2 * l : 2 * l + 1], bias[2 * l + 1 : 2 * l + 2])
        bias_out[l : l + 1, :] = pltpu.roll(fc1, (128 - (me.d % 4) * 32) % 128, 1)
    bias_out[4:8, :] = pltpu.roll(bias[4:8], (128 - me.d * 16) % 128, 1)
    bias_out[2:4, :] = jnp.zeros((2, 128), F32)
    for copy in copies:
        copy.wait_send()
    slots_p.step(4)


def close_call(identity, counts, grad, bank, totals, base, above, vectors, w, rows, sums, bias_sums):
    inputs = [counts, grad, bank, totals, base, above, vectors, w, rows, *sums, *bias_sums]
    return call(
        close_kernel,
        identity,
        inputs,
        [pl.BlockSpec(memory_space=pltpu.SMEM), VMEM, ANY] + [VMEM] * (len(inputs) - 3),
        [
            jax.ShapeDtypeStruct((2, 8, BLOCK, 128), BF16),
            jax.ShapeDtypeStruct((2, 8, BLOCK, 128), BF16),
            jax.ShapeDtypeStruct((16, 128), F32),
            jax.ShapeDtypeStruct((8, 128), F32),
            jax.ShapeDtypeStruct((w.shape[1], 128), F32),
            jax.ShapeDtypeStruct((256, 128), F32),
        ],
        [VMEM] * 6,
        [
            pltpu.VMEM((2, 256, D), BF16),
            pltpu.VMEM((BLOCK, D), BF16),
            pltpu.VMEM((2, 16, 512), F32),
            pltpu.VMEM((8, 2, 16, 128), F32),
            pltpu.VMEM((2, 24, 128), F32),
            pltpu.VMEM((16, 24, 128), F32),
            pltpu.VMEM((2, 8, 128), F32),
            pltpu.VMEM((BLOCK, D), BF16),
            pltpu.SemaphoreType.DMA((5,)),
            pltpu.VMEM((ROWS, 384), BF16),
            pltpu.VMEM((ROWS, D), BF16),
            pltpu.VMEM((ROWS, 128), BF16),
            pltpu.VMEM((2, 256, D), BF16),
            pltpu.SemaphoreType.DMA((5,)),
        ]
        + BACK_SCRATCH
        + reduce_scratch()
        + pair_sems(15) * 2
        + pair_sems(7)
        + pair_sems(15)
        + collect_scratch(w.shape[1])
        + collect_scratch(256),
    )


def local(
    tokens,
    counts,
    cotangent,
    qkv_weight,
    out_weight,
    fc1_weight,
    fc2_weight,
    norm_gains,
    shifts,
    qv_bias,
    fc1_bias,
):
    me = Place()

    def images(v):
        v = jnp.pad(v.reshape(2, SEQ, 64), ((0, 0), (0, ROWS - SEQ), (0, 0)))
        return jnp.concatenate([v[:, : ROWS // 2], v[:, ROWS // 2 :]], axis=2)

    packs = [
        (
            jnp.concatenate([qkv_weight[l].T, out_weight[l]], axis=0),
            jnp.concatenate([fc1_weight[l].T, fc2_weight[l]], axis=0),
        )
        for l in range(LAYERS)
    ]
    def wide_rows(v, rows):
        v = v.reshape(rows, -1).astype(F32)
        return jnp.pad(v, ((0, 0), (0, 128 - v.shape[1])))

    small = jnp.concatenate(
        [wide_rows(norm_gains, 4), wide_rows(shifts, 8), wide_rows(qv_bias, 2), wide_rows(fc1_bias, 2)]
    )
    x, cot, packs, small = lax.optimization_barrier((images(tokens), images(cotangent), packs, small))
    first_in, state, wide_a, vectors, qkv_shift, up_bias, cot = open_call(x, cot, packs[0][0], small)
    first_state = state
    middle, second_in, wide_b, first_totals, first_bank, gradient_full, gradient = attention_call(
        1, 0, first_in, wide_a, qkv_shift, state, vectors, packs[0][1], counts, cot
    )
    first_middle = middle
    state, first_in, wide_a, feed_bank = feed_call(
        2, 0, second_in.reshape(ROWS, D), wide_b, up_bias, middle, vectors, packs[1][0]
    )
    first_in = first_in.reshape(ROWS, D)
    middle, second_in, wide_b, totals, mixed, attended = attention_call(
        3, 1, first_in, wide_a, qkv_shift, state, vectors, packs[1][1]
    )
    last_rows, gradient, up_sums, pending, low, up_bias_sums = turn_call(
        4, 1, second_in.reshape(ROWS, D), wide_b, up_bias, middle, vectors, gradient_full, gradient
    )
    owned = {}
    gradient, mid_sums, pending, low, mid_bias_sums, owned["b", 1] = attention_back_call(
        5, 1, low.reshape(ROWS, D), wide_a, mixed, totals, state, first_in, attended, gradient, vectors, pending
    )
    gradient, down_sums, pending, low, down_bias_sums, owned["a", 1] = feed_back_call(
        6, 0, low.reshape(ROWS, D), first_middle, gradient, vectors, feed_bank, pending
    )
    all_sums = [up_sums, mid_sums, down_sums]
    bias_sums = [up_bias_sums, mid_bias_sums, down_bias_sums]
    out_landed, grad_landed, vec, bias, owned["b", 0], owned["a", 0] = close_call(
        7, counts, low.reshape(ROWS, D), first_bank, first_totals, first_state, gradient, vectors, pending,
        last_rows, all_sums, bias_sums
    )

    def side(v, width, at):
        return lax.dynamic_slice_in_dim(v, at * width, width, axis=-1)

    def whole(v):
        return side(v, 64, me.c).reshape(2, ROWS, 64)[:, :SEQ].reshape(2 * SEQ, 64)

    vec = vec[:, :8]
    return (
        whole(out_landed),
        whole(grad_landed).astype(F32),
        jnp.stack([owned["a", l][:192].T for l in range(LAYERS)]),
        jnp.stack([owned["a", l][192:] for l in range(LAYERS)]),
        jnp.stack([owned["b", l][:256].T for l in range(LAYERS)]),
        jnp.stack([owned["b", l][256:] for l in range(LAYERS)]),
        vec[:4].reshape(LAYERS, 2, 1, 8),
        vec[4:12].reshape(LAYERS, 4, 1, 8),
        bias[4:6, :16].reshape(LAYERS, 1, 16),
        bias[:2, :32].reshape(LAYERS, 1, 32),
    )


def solution(mesh):
    placed = (
        P("dp", "tensor"),
        P(),
        P("dp", "tensor"),
        P(None, "dp", "tensor"),
        P(None, "tensor", "dp"),
        P(None, "dp", "tensor"),
        P(None, "tensor", "dp"),
        P(None, None, "tensor", "dp"),
        P(None, None, "tensor", "dp"),
        P(None, "tensor", "dp"),
        P(None, "tensor", "dp"),
    )
    return jax.shard_map(
        local,
        mesh=mesh,
        in_specs=placed,
        out_specs=(
            P("dp", "tensor"),
            P("dp", "tensor"),
            P(None, "dp", "tensor"),
            P(None, "tensor", "dp"),
            P(None, "dp", "tensor"),
            P(None, "tensor", "dp"),
            P(None, None, "tensor", "dp"),
            P(None, None, "tensor", "dp"),
            P(None, "tensor", "dp"),
            P(None, "tensor", "dp"),
        ),
        check_vma=False,
    )
```

```python
import functools

import jax
import jax.numpy as jnp
from jax import lax
from jax.experimental import pallas as pl
from jax.experimental.pallas import tpu as pltpu
from jax.sharding import PartitionSpec as P

MESH = pl.DeviceIdType.MESH
F32 = jnp.float32
BF16 = jnp.bfloat16
SEQ = 577
LAYERS = 2
BLOCK = 80
ROWS = 8 * BLOCK
D = 1024
EPS = 1e-06
VMEM = pl.BlockSpec(memory_space=pltpu.VMEM)
ANY = pl.BlockSpec(memory_space=pl.ANY)


class Place:
    def __init__(self):
        self.t = lax.axis_index("tensor")
        self.d = lax.axis_index("dp")
        self.z = self.t // 4
        self.xl = (self.t // 2) % 2
        self.c = self.t % 2
        self.w = self.d * 2 + self.xl
        self.j = self.z * 2 + self.c
        self.y = self.d // 2
        self.x = (self.d % 2) * 2 + self.xl
        self.zf, self.zb, self.zo = self.around(self.z)
        self.xf, self.xb, self.xo = self.around(self.x)
        self.yf, self.yb, self.yo = self.around(self.y)

    def around(self, at):
        return (at + 5 - 2 * self.c) % 4, (at + 3 + 2 * self.c) % 4, (at + 2) % 4

    def member(self, z, c):
        return (self.d, z * 4 + self.xl * 2 + c)

    def member_at(self, k):
        j = (self.j + k) % 8
        return self.member(j // 2, j % 2)

    def sharer(self, k):
        w = (self.w + k) % 16
        return (w // 2, self.z * 4 + (w % 2) * 2 + self.c)

    def plane(self, y, x):
        return (y * 2 + x // 2, self.z * 4 + (x % 2) * 2 + self.c)


def remote(src, dst, sems, role, device):
    return pltpu.make_async_remote_copy(
        src_ref=src,
        dst_ref=dst,
        send_sem=sems[0].at[role],
        recv_sem=sems[1].at[role],
        device_id=device,
        device_id_type=MESH,
    )


def hello(devices):
    barrier = pltpu.get_barrier_semaphore()
    for device in devices:
        pl.semaphore_signal(barrier, inc=1, device_id=device, device_id_type=MESH)
    return len(devices)


def met(count):
    pl.semaphore_wait(pltpu.get_barrier_semaphore(), count)


def greet(devices):
    met(hello(devices))


class Moves:
    def __init__(self, sems):
        self.sems, self.copies = sems, []

    def start(self, source, target):
        copy = pltpu.make_async_copy(source, target, self.sems.at[len(self.copies)])
        copy.start()
        self.copies.append(copy)

    def wait(self, *which):
        for k in which:
            self.copies[k].wait()

    def wait_all(self):
        self.wait(*range(len(self.copies)))


BANK = jax.ShapeDtypeStruct((24, D, D), BF16)


def attention_places(bank):
    rows = pl.ds(0, ROWS)
    return [
        bank.at[1, rows, pl.ds(0, 384)],
        bank.at[0, rows],
        bank.at[1, rows, pl.ds(384, 128)],
        bank.at[2, pl.ds(0, 256)],
        bank.at[2, pl.ds(256, 256)],
    ]


def feed_places(bank):
    rows = pl.ds(0, ROWS)
    return [
        bank.at[1, rows, pl.ds(512, 512)],
        bank.at[0, rows],
        bank.at[1, rows, pl.ds(0, 512)],
        bank.at[2, pl.ds(0, 512)],
        bank.at[2, pl.ds(512, 512)],
    ]


class Row:
    def __init__(self, ref, row):
        self.ref, self.row = ref, row

    def __getitem__(self, index):
        lanes = slice(None) if index is Ellipsis else index[1]
        return self.ref[self.row : self.row + 1, lanes]


def gain_row(l, n):
    return 2 * l + n


def shift_row(l, n):
    return 4 + 4 * l + n


def near(me):
    return [me.member(me.zf, me.c), me.member(me.zb, me.c), me.member(me.z, 1 - me.c)]


def cross(me):
    return [me.plane(me.y, me.xf), me.plane(me.y, me.xb), me.plane(me.yf, me.x), me.plane(me.yb, me.x)]


def nothing(point):
    pass


def gather_steps(out, me, sems):
    ahead, back, other = near(me)
    copies = []

    def send(z, role, device, half=None):
        part = out.at[z, me.c]
        if half is not None:
            part = part.at[half] if len(out.shape) == 5 else part.at[:, pl.ds(half * (D // 2), D // 2)]
        copies.append(remote(part, part, sems, role, device))
        copies[-1].start()
        return copies[-1]

    first, second = [], []
    for half in range(2):
        first.append(send(me.z, half, ahead, half))
        second.append(send(me.z, 2 + half, back, half))
    over = [send(me.z, 6, other)]
    yield
    third = []
    for half in range(2):
        first[half].wait_recv()
        third.append(send(me.zb, 4 + half, ahead, half))
    over.append(send(me.zb, 7, other))
    yield
    for half in range(2):
        second[half].wait_recv()
    over.append(send(me.zf, 8, other))
    for half in range(2):
        third[half].wait_recv()
        over.append(send(me.zo, 9 + half, other, half))
    yield
    for copy in over:
        copy.wait_recv()
    for copy in copies:
        copy.wait_send()


def gather(out, me, sems, beside=nothing):
    for point, _ in enumerate(gather_steps(out, me, sems)):
        beside(3 + point)


def reduce(part, crossed, held, landed, me, sems, produce, begin, beside):
    ahead, back, other = near(me)
    copies = []

    def made(role, z):
        produce(z)
        if role == 0:
            begin()
        copies.append(remote(part.at[z, 1 - me.c], crossed.at[role], sems, role, other))
        copies[-1].start()

    def both(role, z):
        copies[role].wait_recv()
        return part[z, me.c].astype(F32) + crossed[role].astype(F32)

    sent = []

    def send(slot, value, role, device, place=slice(None)):
        held[slot, :, place] = value.astype(BF16)
        copy = remote(held.at[slot, :, place], landed.at[slot, :, place], sems, role, device)
        copy.start()
        sent.append(copy)
        return copy

    halves = (slice(0, D // 2), slice(D // 2, D))
    made(0, me.zo)
    made(1, me.zf)
    beside(0)
    value = both(0, me.zo)
    long = [send(0, value[:, place], 4 + k, ahead, place) for k, place in enumerate(halves)]
    made(2, me.zb)
    short = send(1, both(1, me.zb), 6, back)
    made(3, me.z)
    beside(1)
    value = both(2, me.zf)
    last = []
    for k, place in enumerate(halves):
        long[k].wait_recv()
        last.append(send(2, value[:, place] + landed[0, :, place].astype(F32), 7 + k, ahead, place))
    beside(2)
    total = both(3, me.z)
    short.wait_recv()
    total = total + landed[1].astype(F32)
    for copy in last:
        copy.wait_recv()
    total = total + landed[2].astype(F32)
    return total, copies + sent


def reduce_steps(part, crossed, held, landed, me, sems, finish):
    ahead, back, other = near(me)
    copies = []

    def send(source, target, role, device):
        copies.append(remote(source, target, sems, role, device))
        copies[-1].start()

    def both(role, z):
        copies[role].wait_recv()
        return part[z, me.c].astype(F32) + crossed[role].astype(F32)

    for role, z in enumerate((me.zo, me.zf, me.zb, me.z)):
        send(part.at[z, 1 - me.c], crossed.at[role], role, other)
    yield
    for slot, (z, device) in enumerate(((me.zo, ahead), (me.zb, back))):
        held[slot] = both(slot, z).astype(BF16)
        send(held.at[slot], landed.at[slot], 4 + slot, device)
    yield
    copies[4].wait_recv()
    held[2] = (both(2, me.zf) + landed[0].astype(F32)).astype(BF16)
    send(held.at[2], landed.at[2], 6, ahead)
    yield
    total = both(3, me.z)
    for slot in (1, 2):
        copies[4 + slot].wait_recv()
        total = total + landed[slot].astype(F32)
    finish(total)
    for copy in copies:
        copy.wait_send()


def reduce_scratch():
    return [
        pltpu.VMEM((4, 2, BLOCK, D), BF16),
        pltpu.VMEM((4, BLOCK, D), BF16),
        pltpu.VMEM((3, BLOCK, D), BF16),
        pltpu.VMEM((3, BLOCK, D), BF16),
        pltpu.SemaphoreType.DMA((9,)),
        pltpu.SemaphoreType.DMA((9,)),
    ]


def pair_sems(count):
    return [pltpu.SemaphoreType.DMA((count,)), pltpu.SemaphoreType.DMA((count,))]


def lanes(at, width):
    return pl.ds(pl.multiple_of(at * 128, 128), width)


class Spread:
    def __init__(self, src, dst, me, sems, local):
        self.src, self.dst, self.me, self.sems = src, dst, me, sems
        half = src.shape[0] // 2
        self.a, self.b = pl.ds(0, half), pl.ds(half, half)
        self.copies = {}
        self.keep = pltpu.make_async_copy(src, dst.at[me.xl, :, lanes((me.x // 2) * 4 + me.y, 128)], local)

    def send(self, role, src, dst, device):
        self.copies[role] = remote(src, dst, self.sems, role, device)
        self.copies[role].start()

    def arrived(self, *roles):
        for role in roles:
            self.copies[role].wait_recv()

    def block(self, y, x, rows):
        return self.dst.at[x % 2, rows, lanes((x // 2) * 4 + y, 128)]

    def row(self, role, y, device):
        for hi in range(2):
            part = self.dst.at[:, self.a, lanes(hi * 4 + y, 128)]
            self.send(role + hi, part, part, device)

    def column(self, role, x, device):
        part = self.dst.at[x % 2, self.b, lanes((x // 2) * 4, 512)]
        self.send(role, part, part, device)

    def step(self, number):
        me = self.me
        xf, xb, yf, yb = cross(me)
        if number == 0:
            self.keep.start()
            for role, rows, device in ((0, self.a, xf), (1, self.a, xb), (2, self.b, yf), (3, self.b, yb)):
                self.send(role, self.src.at[rows], self.block(me.y, me.x, rows), device)
        elif number == 1:
            self.arrived(0, 2)
            self.send(4, self.block(me.y, me.xb, self.a), self.block(me.y, me.xb, self.a), xf)
            self.send(5, self.block(me.yb, me.x, self.b), self.block(me.yb, me.x, self.b), yf)
        elif number == 2:
            self.keep.wait()
            self.arrived(1, 4)
            self.row(6, me.y, yf)
            self.row(8, me.y, yb)
            self.arrived(3, 5)
            self.column(10, me.x, xf)
            self.column(11, me.x, xb)
        elif number == 3:
            self.arrived(6, 7)
            self.row(12, me.yb, yf)
            self.arrived(10)
            self.column(14, me.xb, xf)
        else:
            self.arrived(8, 9, 11, 12, 13, 14)
            for copy in self.copies.values():
                copy.wait_send()


def spread_scratch():
    return pair_sems(15) + [pltpu.SemaphoreType.DMA((1,))]


class Collect:
    def __init__(self, src, out, me, bufs):
        self.src, self.out, self.me = src, out, me
        self.rows_in, self.rows_held, self.cols_in, self.cols_held, self.one_in, self.one_held, *self.sems = bufs
        half = src.shape[1] // 2
        self.a, self.b = pl.ds(0, half), pl.ds(half, half)
        self.half = half
        self.copies = {}

    def send(self, role, src, dst, device):
        self.copies[role] = remote(src, dst, self.sems, role, device)
        self.copies[role].start()

    def arrived(self, *roles):
        for role in roles:
            self.copies[role].wait_recv()

    def column(self, x):
        return self.src.at[x % 2, self.a, lanes((x // 2) * 4, 512)]

    def row(self, y, hi):
        return self.src.at[:, self.b, lanes(hi * 4 + y, 128)]

    def step(self, number):
        me = self.me
        xf, xb, yf, yb = cross(me)
        if number == 0:
            self.send(0, self.column(me.xo), self.cols_in.at[0], xf)
            self.send(1, self.column(me.xb), self.cols_in.at[1], xb)
            for hi in range(2):
                self.send(3 + hi, self.row(me.yo, hi), self.rows_in.at[0, hi], yf)
                self.send(5 + hi, self.row(me.yb, hi), self.rows_in.at[1, hi], yb)
        elif number == 1:
            self.arrived(0)
            self.cols_held[0] = (self.column(me.xf)[...].astype(F32) + self.cols_in[0].astype(F32)).astype(BF16)
            self.send(2, self.cols_held.at[0], self.cols_in.at[2], xf)
            self.arrived(3, 4)
            for hi in range(2):
                self.rows_held[0, hi] = (self.row(me.yf, hi)[...].astype(F32) + self.rows_in[0, hi].astype(F32)).astype(BF16)
                self.send(7 + hi, self.rows_held.at[0, hi], self.rows_in.at[2, hi], yf)
        elif number == 2:
            self.arrived(1, 2)
            self.cols_held[1] = (
                self.column(me.x)[...].astype(F32) + self.cols_in[1].astype(F32) + self.cols_in[2].astype(F32)
            ).astype(BF16)
            self.send(9, self.cols_held.at[1, :, lanes(me.yo, 128)], self.one_in.at[0], yf)
            self.send(10, self.cols_held.at[1, :, lanes(me.yb, 128)], self.one_in.at[1], yb)
            self.arrived(5, 6, 7, 8)
            for hi in range(2):
                self.rows_held[1, hi] = (
                    self.row(me.y, hi)[...].astype(F32)
                    + self.rows_in[1, hi].astype(F32)
                    + self.rows_in[2, hi].astype(F32)
                ).astype(BF16)
            self.send(12, self.rows_held.at[1, me.xo // 2, me.xo % 2], self.one_in.at[3], xf)
            self.send(13, self.rows_held.at[1, me.xb // 2, me.xb % 2], self.one_in.at[4], xb)
        elif number == 3:
            self.arrived(9)
            self.one_held[0] = (self.cols_held[1, :, lanes(me.yf, 128)].astype(F32) + self.one_in[0].astype(F32)).astype(BF16)
            self.send(11, self.one_held.at[0], self.one_in.at[2], yf)
            self.arrived(12)
            self.one_held[1] = (self.rows_held[1, me.xf // 2, me.xf % 2].astype(F32) + self.one_in[3].astype(F32)).astype(BF16)
            self.send(14, self.one_held.at[1], self.one_in.at[5], xf)
        else:
            self.arrived(10, 11)
            self.out[self.a, :] = (
                self.cols_held[1, :, lanes(me.y, 128)].astype(F32)
                + self.one_in[1].astype(F32)
                + self.one_in[2].astype(F32)
            )
            self.arrived(13, 14)
            self.out[self.b, :] = (
                self.rows_held[1, me.x // 2, me.x % 2].astype(F32)
                + self.one_in[4].astype(F32)
                + self.one_in[5].astype(F32)
            )
            for copy in self.copies.values():
                copy.wait_send()


def collect_scratch(n):
    half = n // 2
    return [
        pltpu.VMEM((3, 2, 2, half, 128), BF16),
        pltpu.VMEM((2, 2, 2, half, 128), BF16),
        pltpu.VMEM((3, half, 512), BF16),
        pltpu.VMEM((2, half, 512), BF16),
        pltpu.VMEM((6, half, 128), BF16),
        pltpu.VMEM((2, half, 128), BF16),
    ] + pair_sems(15)


def row_stats(v):
    mean = jnp.sum(v, axis=1, keepdims=True) / D
    square = jnp.sum(v * v, axis=1, keepdims=True) / D
    return mean, lax.rsqrt(square - mean * mean + EPS)


def normed(v, gain, bias):
    mean, inv = row_stats(v)
    return ((v - mean) * inv * gain + bias).astype(BF16)


def call(body, identity, inputs, in_specs, out_shape, out_specs, scratch):
    return pl.pallas_call(
        body,
        out_shape=out_shape,
        in_specs=in_specs,
        out_specs=out_specs,
        scratch_shapes=scratch,
        cost_estimate=pl.CostEstimate(flops=20_000_000_000, bytes_accessed=40_000_000, transcendentals=0),
        compiler_params=pltpu.CompilerParams(
            collective_id=identity, has_side_effects=True, vmem_limit_bytes=24 * 1024 * 1024
        ),
    )(*inputs)


def half_swap(left, right, low):
    return jnp.where(low, left, pltpu.roll(right, 64, 1)), jnp.where(low, pltpu.roll(left, 64, 1), right)


def unfold(blocks, out, change):
    low = low_lanes(BLOCK)

    def rows(index, carry):
        start = pl.multiple_of(index * BLOCK, BLOCK)
        for z in range(4):
            for p in range(2):
                left, right = (blocks[z, c, p, pl.ds(start, BLOCK)].astype(F32) for c in range(2))
                for half, value in enumerate(half_swap(left, right, low)):
                    at = pl.ds(pl.multiple_of(half * (ROWS // 2) + start, BLOCK), BLOCK)
                    out[at, pl.ds((p * 4 + z) * 128, 128)] = change(value).astype(out.dtype)
        return carry

    lax.fori_loop(0, 4, rows, 0)


def open_kernel(
    x_ref, x2_ref, w_ref, s_ref, in_ref, state_ref, wide_ref, vec_ref, qkv_ref, up_ref, cot_ref,
    y_ref, tok_ref, sw_ref, st_ref, comp, local, *sems
):
    me = Place()
    greet([me.sharer(k) for k in range(1, 16)] + [me.member_at(k) for k in range(1, 8)])
    mine = y_ref.at[me.z, me.c, me.xl]
    neighbour = (me.d, me.z * 4 + (1 - me.xl) * 2 + me.c)
    swap = remote(x_ref.at[1 - me.xl], mine, sems[0:2], 0, neighbour)
    swap.start()
    keep = pltpu.make_async_copy(x_ref.at[me.xl], mine, local.at[0])
    keep.start()
    cot_ref[me.xl] = x2_ref[me.xl]
    small = [remote(s_ref, sw_ref.at[me.w], sems[2:4], k - 1, me.sharer(k)) for k in range(1, 16)]
    for copy in small:
        copy.start()
    wide = Spread(w_ref, wide_ref, me, sems[4:6], local.at[1])
    wide.step(0)
    swap_cot = remote(x2_ref.at[1 - me.xl], cot_ref.at[me.xl], sems[0:2], 1, neighbour)
    swap_cot.start()
    sw_ref[me.w] = s_ref[...]
    keep.wait()
    swap.wait()
    spread = []
    low = lax.broadcasted_iota(jnp.int32, (16, 128), 1) < 64

    def beside(point):
        wide.step(point - 2)
        if point == 3:
            for copy in small:
                copy.wait()
            comp[...] = sum(pltpu.roll(sw_ref[w], (w % 2) * 64 + (w // 2) * 8, 1) for w in range(16))
            st_ref[me.z, me.c] = comp[...]
            for k in range(1, 8):
                spread.append(remote(comp, st_ref.at[me.z, me.c], sems[6:8], k - 1, me.member_at(k)))
                spread[-1].start()
            pair = []
            for p in range(2):
                pair.append(sum(pltpu.roll(sw_ref[2 * d + p], d * 16, 1) for d in range(8)))
                for k in range(2):
                    value = sum(pltpu.roll(sw_ref[2 * d + p], (d % 4) * 32, 1) for d in range(4 * k, 4 * k + 4))
                    up_ref[:, (p * 2 + k) * 128 : (p * 2 + k + 1) * 128] = value
            swapped = half_swap(*pair, low)
            qkv_ref[:, :128] = jnp.where(low, pair[0], 0.0)
            qkv_ref[:, 128:256] = jnp.where(low, pltpu.roll(pair[0], 64, 1), swapped[0])
            qkv_ref[:, 256:] = jnp.where(low, 0.0, pair[1])

    gather(y_ref, me, sems[8:10], beside)
    for copy in spread:
        copy.wait()
    for z in range(4):
        for p, value in enumerate(half_swap(st_ref[z, 0], st_ref[z, 1], low)):
            vec_ref[:, (p * 4 + z) * 128 : (p * 4 + z + 1) * 128] = value
    unfold(y_ref, tok_ref, lambda v: v)

    def rows(index, carry):
        at = pl.ds(pl.multiple_of(index * BLOCK, BLOCK), BLOCK)
        in_ref[at, :] = normed(tok_ref[at, :], vec_ref[0:1, :], vec_ref[4:5, :])
        return carry

    lax.fori_loop(0, 8, rows, 0)
    state_ref[...] = tok_ref[pl.ds(pl.multiple_of(me.j * BLOCK, BLOCK), BLOCK), :]
    swap_cot.wait()
    wide.step(4)


FOLDED = (4, 2, 2, ROWS // 2, 128)


def open_call(x, x2, w, s):
    return call(
        open_kernel,
        0,
        (x, x2, w, s),
        [VMEM, VMEM, ANY, VMEM],
        [
            jax.ShapeDtypeStruct((ROWS, D), BF16),
            jax.ShapeDtypeStruct((BLOCK, D), F32),
            jax.ShapeDtypeStruct((2, w.shape[0], D), BF16),
            jax.ShapeDtypeStruct((16, D), F32),
            jax.ShapeDtypeStruct((16, 384), F32),
            jax.ShapeDtypeStruct((16, 512), F32),
            jax.ShapeDtypeStruct((2, ROWS // 2, 128), BF16),
        ],
        [VMEM] * 2 + [ANY] + [VMEM] * 4,
        [
            pltpu.VMEM(FOLDED, BF16),
            pltpu.VMEM((ROWS, D), F32),
            pltpu.VMEM((16, 16, 128), F32),
            pltpu.VMEM((4, 2, 16, 128), F32),
            pltpu.VMEM((16, 128), F32),
            pltpu.SemaphoreType.DMA((2,)),
        ]
        + pair_sems(2)
        + pair_sems(15)
        + pair_sems(15)
        + pair_sems(7)
        + pair_sems(11),
    )


PAIR = 2 * BLOCK
QKV_SCRATCH = [pltpu.VMEM((384, D), BF16), pltpu.VMEM((128, D), BF16), pltpu.VMEM((6, ROWS, 128), BF16)]


def pair_rows(z):
    return pl.ds(pl.multiple_of(z * PAIR, PAIR), PAIR)


def dot(a, b, contract=(1, 0)):
    return lax.dot_general(a, b, (((contract[0],), (contract[1],)), ((), ())), preferred_element_type=F32)


def low_lanes(rows):
    return lax.broadcasted_iota(jnp.int32, (rows, 128), 1) < 64


def load_projections(wide, wq, wo):
    for p in range(2):
        wq[p * 192 : (p + 1) * 192, :] = wide[p, 0:192, :]
        wo[p * 64 : (p + 1) * 64, :] = wide[p, 192:256, :]


def turn(at, tiles, turned):
    low = low_lanes(PAIR)
    swapped = [pltpu.roll(tile, 64, 1) for tile in tiles]
    for index, tile in enumerate(swapped):
        turned[index, at, :] = tile.astype(BF16)
    turned[3, at, :] = jnp.where(low, tiles[0], 0.0).astype(BF16)
    turned[4, at, :] = jnp.where(low, swapped[1], 0.0).astype(BF16)


def score_rows(head, at, mixed, turned):
    keys = turned[0] if head == 0 else mixed[:, 256:384]
    scores = 64 ** (-0.5) * dot(turned[3 + head, at, :], keys, (1, 1))
    return jnp.where(lax.broadcasted_iota(jnp.int32, scores.shape, 1) < SEQ, scores, -1e30)


def store_part(part, z, value):
    part[z] = value.astype(BF16).reshape(2, BLOCK, D)


def forward_tail(me, refs, produce, begin, wide, state, shift, gain, bias, new_ref, out_ref, complete):
    part, crossed, held, landed, s0, s1, s2, s3 = refs

    def beside(point):
        complete(point)
        if wide is not None and point in (1, 2, 4):
            wide.step((None, 1, 2, None, 3)[point])

    total, copies = reduce(part, crossed, held, landed, me, (s0, s1), produce, begin, beside)
    value = state[...] + (total + shift[...])
    new_ref[...] = value
    if out_ref is not None:
        out_ref[me.z, me.c] = normed(value, gain[...], bias[...])
        gather(out_ref, me, (s2, s3), beside)
    for copy in copies:
        copy.wait_send()
    if wide is not None:
        wide.step(4)


def attention_kernel(
    banked, layer, in_ref, mine_ref, qkv_ref, state, vec_ref, w_ref, *rest
):
    qkv_shift = Row(qkv_ref, 12 + layer)
    shift, gain, bias = (Row(vec_ref, r) for r in (shift_row(layer, 1), gain_row(layer, 1), shift_row(layer, 2)))
    if banked:
        counts_ref, x_ref, *rest = rest
    new_ref, out_ref, wide_ref, total_ref, *rest = rest
    if banked:
        bank, cot_ref, above_ref, mixed, attended, wq, wo, turned, *rest = rest
        moves = Moves(rest[11])
        places = attention_places(bank)
        moves.start(in_ref, places[1])
        for p in range(2):
            moves.start(mine_ref.at[p], places[3 + p])
    else:
        mixed, attended, wq, wo, turned, *rest = rest
    me = Place()
    count = hello(near(me) + cross(me))
    wide = Spread(w_ref, wide_ref, me, rest[8:10], rest[10].at[0])
    load_projections(mine_ref, wq, wo)

    def project(index, carry):
        at = pair_rows(index)
        value = dot(in_ref[at, :], wq[...], (1, 1)) + qkv_shift[...]
        mixed[at, :] = value.astype(BF16)
        turn(at, [value[:, k * 128 : (k + 1) * 128] for k in range(3)], turned)
        return carry

    project(0, 0)
    met(count)
    wide.step(0)
    if banked:
        folded, cot_sems = rest[12], rest[13:15]
        folded[me.z, me.c] = x_ref[...]
        cot_steps = gather_steps(folded, me, cot_sems)
        next(cot_steps)
    lax.fori_loop(1, 4, project, 0)

    def produce(z):
        at = pair_rows(z)
        parts = []
        for head in range(2):
            scores = score_rows(head, at, mixed, turned)
            row_max = jnp.max(scores, axis=1, keepdims=True)
            shifted = jnp.exp(scores - row_max)
            row_total = jnp.sum(shifted, axis=1, keepdims=True)
            soft = (shifted / row_total).astype(BF16)
            parts.append((dot(soft, mixed[:, 128 + head * 128 : 256 + head * 128]), row_max + jnp.log(row_total)))
        low = low_lanes(PAIR)
        value = jnp.where(low, parts[0][0], parts[1][0]).astype(BF16)
        attended[at, :] = value
        total_ref[at, :] = jnp.where(low, parts[0][1], parts[1][1])
        store_part(rest[0], z, dot(value, wo[...]))

    def complete(point):
        if banked and point == 1:
            moves.start(mixed, places[0])
            moves.start(attended, places[2])
        if banked and point in (1, 3, 5):
            next(cot_steps, None)

    forward_tail(me, rest[:8], produce, lambda: None, wide, state, shift, gain, bias, new_ref, out_ref, complete)
    if banked:
        live = jnp.where(me.xl < counts_ref[me.d], 1.0, 0.0)
        unfold(folded, cot_ref, lambda v: v * live)
        above_ref[...] = cot_ref[pl.ds(pl.multiple_of(me.j * BLOCK, BLOCK), BLOCK), :].astype(F32)
        moves.wait_all()


def attention_call(identity, layer, first_in, mine, qkv_shift, state, vectors, w, counts=None, x=None):
    banked = x is not None
    kept = [jax.ShapeDtypeStruct((ROWS, 384), BF16), jax.ShapeDtypeStruct((ROWS, 128), BF16)]
    return call(
        functools.partial(attention_kernel, banked, layer),
        identity,
        (first_in, mine, qkv_shift, state, vectors, w) + ((counts, x) if banked else ()),
        [VMEM] * 5 + [ANY] + ([pl.BlockSpec(memory_space=pltpu.SMEM), VMEM] if banked else []),
        [
            jax.ShapeDtypeStruct((BLOCK, D), F32),
            jax.ShapeDtypeStruct((4, 2, BLOCK, D), BF16),
            jax.ShapeDtypeStruct((2, w.shape[0], D), BF16),
            jax.ShapeDtypeStruct((ROWS, 128), F32),
        ]
        + ([BANK, jax.ShapeDtypeStruct((ROWS, D), BF16), jax.ShapeDtypeStruct((BLOCK, D), F32)] if banked else kept),
        [VMEM, VMEM, ANY, VMEM] + ([ANY, VMEM, VMEM] if banked else [VMEM] * 2),
        ([pltpu.VMEM(v.shape, v.dtype) for v in kept] if banked else [])
        + QKV_SCRATCH
        + reduce_scratch()
        + pair_sems(11)
        + spread_scratch()
        + (
            [pltpu.SemaphoreType.DMA((5,)), pltpu.VMEM(FOLDED, BF16)] + pair_sems(11)
            if banked
            else []
        ),
    )


def feed_rows(at, in_ref, mine, up_shift, activated, slope):
    rows = in_ref[at, :]
    total = 0.0
    for p in range(2):
        place = pl.ds(p * 256, 256)
        value = dot(rows, mine[p, 0:256, :], (1, 1)) + up_shift[:, place]
        normal = 0.5 * (1.0 + lax.erf(value * 0.5**0.5))
        active = (value * normal).astype(BF16)
        activated[at, place] = active
        slope[at, place] = (normal + value * jnp.exp(-0.5 * value * value) * (0.5 / jnp.pi) ** 0.5).astype(BF16)
        total = total + dot(active, mine[p, 256:512, :])
    return total


def feed_back_rows(at, grad_ref, mine, slope, d_pre):
    rows = grad_ref[at, :]
    total = 0.0
    for p in range(2):
        place = pl.ds(p * 256, 256)
        value = (dot(rows, mine[p, 256:512, :], (1, 1)) * slope[at, place]).astype(BF16)
        d_pre[at, place] = value
        total = total + dot(value, mine[p, 0:256, :])
    return total


def feed_kernel(
    layer, in_ref, mine, up_ref, state, vec_ref, w_ref, new_ref, out_ref, wide_ref, bank, activated, slope, *rest
):
    up_shift = Row(up_ref, 14 + layer)
    shift, gain, bias = (Row(vec_ref, r) for r in (shift_row(layer, 3), gain_row(layer + 1, 0), shift_row(layer + 1, 0)))
    moves = Moves(rest[11])
    places = feed_places(bank)
    moves.start(in_ref, places[1])
    for p in range(2):
        moves.start(mine.at[p], places[3 + p])
    me = Place()
    count = hello(near(me) + cross(me))
    wide = Spread(w_ref, wide_ref, me, rest[8:10], rest[10].at[0])

    def begin():
        met(count)
        wide.step(0)

    def produce(z):
        store_part(rest[0], z, feed_rows(pair_rows(z), in_ref, mine, up_shift, activated, slope))

    def complete(point):
        if point == 1:
            moves.start(slope, places[0])
            moves.start(activated, places[2])

    forward_tail(me, rest[:8], produce, begin, wide, state, shift, gain, bias, new_ref, out_ref, complete)
    moves.wait_all()


def feed_call(identity, layer, second_in, mine, up_shift, state, vectors, w):
    kept = [pltpu.VMEM((ROWS, 512), BF16)] * 2
    return call(
        functools.partial(feed_kernel, layer),
        identity,
        [second_in, mine, up_shift, state, vectors, w],
        [VMEM] * 5 + [ANY],
        [
            jax.ShapeDtypeStruct((BLOCK, D), F32),
            jax.ShapeDtypeStruct((4, 2, BLOCK, D), BF16),
            jax.ShapeDtypeStruct((2, w.shape[0], D), BF16),
            BANK,
        ],
        [VMEM, VMEM, ANY, ANY],
        kept + reduce_scratch() + pair_sems(11) + spread_scratch() + [pltpu.SemaphoreType.DMA((5,))],
    )


def weight_product(left, right, out, heads):
    size = left.shape[1] // 2

    def tile(index, carry):
        at = lanes(index * 2, 256)
        value = lax.dot_general(left[...], right[:, at], (((0,), (0,)), ((), ())), preferred_element_type=F32).astype(BF16)
        for p in range(2):
            out[p, pl.ds(heads, size), at] = value[p * size : (p + 1) * size]
        return carry

    lax.fori_loop(0, 4, tile, 0)


def norm_back(total, base, above, gain):
    mean, inv = row_stats(base)
    hat = (base - mean) * inv
    weighted = total * gain
    first = jnp.sum(weighted, axis=1, keepdims=True) / D
    second = jnp.sum(weighted * hat, axis=1, keepdims=True) / D
    return above + inv * (weighted - first - hat * second), total * hat


def backward_tail(
    me, refs, produce, begin, slots, products, weight_ref, base, above, gain, new_ref, sums_ref, out_ref, also=nothing
):
    part, crossed, held, landed, s0, s1, s2, s3 = refs

    def beside(point):
        also(point)
        if point == 1:
            weight_product(*products[0], weight_ref, 0)
        if point == 3:
            weight_product(*products[1], weight_ref, products[0][0].shape[1] // 2)
        if slots is not None and point in (2, 3, 4):
            slots.step(point - 1)

    total, copies = reduce(part, crossed, held, landed, me, (s0, s1), produce, begin, beside)
    value, by_hat = norm_back(total, base[...], above[...], gain[...])
    new_ref[...] = value
    low = value.astype(BF16)
    out_ref[me.z, me.c] = low
    for row, each in enumerate((by_hat, total, low.astype(F32), above[...])):
        sums_ref[row : row + 1, :] = jnp.sum(each, axis=0, keepdims=True)
    sums_ref[4:8, :] = jnp.zeros((4, D), F32)
    gather(out_ref, me, (s2, s3), beside)
    for copy in copies:
        copy.wait_send()
    if slots is not None:
        slots.step(4)


def feed_back_kernel(
    layer, grad_ref, base, above, vec_ref, bank, w_ref, new_ref, sums_ref, weight_ref, out_ref, bias_ref, owned_ref,
    slope, second_in, activated, mine, fetched, d_pre, *rest
):
    moves = Moves(fetched)
    for source, target in zip(feed_places(bank), (slope, second_in, activated, mine.at[0], mine.at[1])):
        moves.start(source, target)
    me = Place()
    count = hello(near(me) + cross(me))
    moves.wait_all()
    slots = Collect(w_ref, owned_ref, me, rest[8:])

    def begin():
        met(count)
        slots.step(0)

    def produce(z):
        store_part(rest[0], z, feed_back_rows(pair_rows(z), grad_ref, mine, slope, d_pre))

    products = ((d_pre, second_in), (activated, grad_ref))
    gain = Row(vec_ref, gain_row(layer, 1))
    backward_tail(
        me, rest[:8], produce, begin, slots, products, weight_ref, base, above, gain, new_ref, sums_ref, out_ref
    )
    bias_ref[...] = jnp.sum(d_pre[...].astype(F32), axis=0, keepdims=True)


def turn_kernel(
    layer, in_ref, mine, up_ref, state, vec_ref, grad_ref, above, last_ref, new_ref, sums_ref, weight_ref, out_ref,
    bias_ref, activated, slope, d_pre, *rest
):
    up_shift, shift, gain = Row(up_ref, 14 + layer), Row(vec_ref, shift_row(layer, 3)), Row(vec_ref, gain_row(layer, 1))
    me = Place()
    count = hello(near(me))
    second, s0, s1 = rest[8:12], rest[12], rest[13]

    def produce(z):
        at = pair_rows(z)
        store_part(second[0], z, feed_rows(at, in_ref, mine, up_shift, activated, slope))
        store_part(rest[0], z, feed_back_rows(at, grad_ref, mine, slope, d_pre))

    def finish(total):
        last_ref[...] = state[...] + (total + shift[...])

    steps = reduce_steps(*second, me, (s0, s1), finish)

    def also(point):
        if point in (1, 2, 3, 5):
            next(steps, None)

    products = ((d_pre, in_ref), (activated, grad_ref))
    begin = functools.partial(met, count)
    backward_tail(
        me, rest[:8], produce, begin, None, products, weight_ref, state, above, gain, new_ref, sums_ref, out_ref, also
    )
    bias_ref[...] = jnp.sum(d_pre[...].astype(F32), axis=0, keepdims=True)


def backward_shapes(size):
    return [
        jax.ShapeDtypeStruct((BLOCK, D), F32),
        jax.ShapeDtypeStruct((8, D), F32),
        jax.ShapeDtypeStruct((2, size, D), BF16),
        jax.ShapeDtypeStruct((4, 2, BLOCK, D), BF16),
    ]


def feed_back_call(identity, layer, grad, base, above, vectors, bank, w):
    out_shape = backward_shapes(512) + [
        jax.ShapeDtypeStruct((1, 512), F32),
        jax.ShapeDtypeStruct((w.shape[1], 128), F32),
    ]
    scratch = [
        pltpu.VMEM((ROWS, 512), BF16),
        pltpu.VMEM((ROWS, D), BF16),
        pltpu.VMEM((ROWS, 512), BF16),
        pltpu.VMEM((2, 512, D), BF16),
        pltpu.SemaphoreType.DMA((5,)),
        pltpu.VMEM((ROWS, 512), BF16),
    ]
    scratch += reduce_scratch() + pair_sems(11) + collect_scratch(w.shape[1])
    inputs = [grad, base, above, vectors, bank, w]
    in_specs = [VMEM] * 4 + [ANY, VMEM]
    body = functools.partial(feed_back_kernel, layer)
    return call(body, identity, inputs, in_specs, out_shape, [VMEM] * len(out_shape), scratch)


def turn_call(identity, layer, second_in, mine, up_shift, state, vectors, grad, above):
    out_shape = [jax.ShapeDtypeStruct((BLOCK, D), F32)] + backward_shapes(512) + [jax.ShapeDtypeStruct((1, 512), F32)]
    scratch = [pltpu.VMEM((ROWS, 512), BF16)] * 3 + reduce_scratch() + pair_sems(11) + reduce_scratch()
    inputs = [second_in, mine, up_shift, state, vectors, grad, above]
    body = functools.partial(turn_kernel, layer)
    return call(body, identity, inputs, [VMEM] * len(inputs), out_shape, [VMEM] * len(out_shape), scratch)


BACK_SCRATCH = QKV_SCRATCH + [
    pltpu.VMEM((ROWS, 384), BF16),
    pltpu.VMEM((3, ROWS, 128), BF16),
    pltpu.VMEM((6, ROWS, 128), F32),
]


def attention_back(grad_ref, mine, mixed, total_ref, bufs, begin, between=None):
    wq, wo, turned, d_mixed, d_att, sums = bufs
    load_projections(mine, wq, wo)
    low = low_lanes(PAIR)

    def ready(index, carry):
        at = pair_rows(index)
        tiles = [mixed[at, k * 128 : (k + 1) * 128].astype(F32) for k in range(3)]
        turn(at, tiles, turned)
        value = dot(grad_ref[at, :], wo[...], (1, 1))
        d_att[0, at, :] = value.astype(BF16)
        d_att[1, at, :] = jnp.where(low, value, 0.0).astype(BF16)
        d_att[2, at, :] = jnp.where(low, 0.0, value).astype(BF16)
        return carry

    lax.fori_loop(0, 4, ready, 0)
    begin()
    for k in range(2, 6):
        sums[k] = jnp.zeros((ROWS, 128), F32)

    def chunk(index, carry):
        at = pair_rows(index)
        grads = d_att[0, at, :]
        for head in range(2):
            soft = jnp.exp(score_rows(head, at, mixed, turned) - total_ref[at, head * 64 : head * 64 + 1])
            d_soft = dot(d_att[1 + head, at, :], mixed[:, 128 + head * 128 : 256 + head * 128], (1, 1))
            sums[2 + head] += dot(soft.astype(BF16), grads, (0, 0))
            d_scores = (soft * (d_soft - jnp.sum(soft * d_soft, axis=1, keepdims=True))).astype(BF16)
            sums[head, at, :] = dot(d_scores, turned[2 * head])
            sums[4 + head] += dot(d_scores, turned[head, at, :], (0, 0))
        return carry

    lax.fori_loop(0, 4, chunk, 0)
    if between is not None:
        between()

    def join(index, carry):
        at = pair_rows(index)
        scale = 64 ** (-0.5)
        d_mixed[at, 0:128] = (scale * jnp.where(low, sums[0, at, :], sums[4, at, :])).astype(BF16)
        d_mixed[at, 128:256] = jnp.where(low, sums[2, at, :], scale * sums[1, at, :]).astype(BF16)
        d_mixed[at, 256:384] = jnp.where(low, scale * sums[5, at, :], sums[3, at, :]).astype(BF16)
        return carry

    lax.fori_loop(0, 4, join, 0)

    def produce(part, z):
        store_part(part, z, dot(d_mixed[pair_rows(z), :], wq[...]))

    return produce


def attention_back_kernel(layer, grad_ref, *refs):
    kept, (above, vec_ref, w_ref, new_ref, sums_ref, weight_ref, out_ref, bias_ref, owned_ref) = refs[:6], refs[6:15]
    bufs, rest = refs[15:21], refs[21:]
    gain = Row(vec_ref, gain_row(layer, 0))
    mine, mixed, total_ref, base, first_in, attended = kept
    me = Place()
    count = hello(near(me) + cross(me))
    slots = Collect(w_ref, owned_ref, me, rest[8:])

    def begin():
        met(count)
        slots.step(0)

    produce = attention_back(grad_ref, mine, mixed, total_ref, bufs, begin)
    produce = functools.partial(produce, rest[0])
    products = ((bufs[3], first_in), (attended, grad_ref))
    backward_tail(
        me, rest[:8], produce, lambda: None, slots, products, weight_ref, base, above, gain, new_ref, sums_ref, out_ref
    )
    bias_ref[...] = jnp.sum(bufs[3][...].astype(F32), axis=0, keepdims=True)


def attention_back_call(identity, layer, grad, mine, mixed, totals, base, first_in, attended, above, vectors, w):
    inputs = [grad, mine, mixed, totals, base, first_in, attended, above, vectors, w]
    in_specs = [VMEM] * 10
    out_shape = backward_shapes(256) + [
        jax.ShapeDtypeStruct((1, 384), F32),
        jax.ShapeDtypeStruct((w.shape[1], 128), F32),
    ]
    scratch = BACK_SCRATCH + reduce_scratch() + pair_sems(11) + collect_scratch(w.shape[1])
    body = functools.partial(attention_back_kernel, layer)
    return call(body, identity, inputs, in_specs, out_shape, [VMEM] * len(out_shape), scratch)


def close_kernel(
    counts_ref, grad_in, bank, total_ref, base, above, vec_in, w_ref, state_ref, up_sums, mid_sums, down_sums,
    up_bias, mid_bias, down_bias,
    out_ref, grad_ref, vec_out, bias_out, owned_w, owned_p,
    product, low_ref, vec_ref, from_t, mine, from_w, own_bias, rows_ref, local,
    mixed, first_in, attended, weights, fetched, *rest
):
    me = Place()
    bufs, rest = rest[:6], rest[6:]
    part, crossed, held, landed, s0, s1 = rest[:6]
    sems, rest = rest[6:14], rest[14:]
    tensor = [(me.d, (me.t + k) % 16) for k in range(1, 16)]
    plane = [((me.d + k) % 8, me.z * 4 + xl * 2 + me.c) for k in range(1, 8) for xl in range(2)]
    moves = Moves(fetched)
    targets = (mixed, first_in, attended, weights.at[0], weights.at[1])
    for source, target in zip(attention_places(bank), targets):
        moves.start(source, target)
    count = hello(tensor + plane)
    moves.wait_all()
    slots_w = Collect(w_ref, owned_w, me, rest[:8])
    slots_p = Collect(product, owned_p, me, rest[8:])

    def scatter(source, target, sems, local):
        def features(t):
            return source.at[:, lanes(((t // 2) % 2) * 4 + t // 4, 128)]

        keep = pltpu.make_async_copy(features(me.t), target.at[me.xl, me.j], local)
        keep.start()
        copies = []
        for k in range(1, 16):
            t = (me.t + k) % 16
            copies.append(remote(features(t), target.at[me.xl, me.j], sems, k - 1, (me.d, t)))
            copies[-1].start()
        return keep, copies

    def share(source, target, sems, local):
        keep = pltpu.make_async_copy(source.at[me.xl], target.at[me.w], local)
        keep.start()
        copies = []
        for k in range(1, 16):
            xl = (me.w + k) % 2
            copies.append(remote(source.at[xl], target.at[me.w], sems, k - 1, me.sharer(k)))
            copies[-1].start()
        return keep, copies

    def finish(started):
        started[0].wait()
        for copy in started[1]:
            copy.wait()

    open_ends = []

    def beside(point):
        if point == 1:
            weight_product(bufs[3], first_in, product, 0)
            weight_product(attended, grad_in, product, 192)
            slots_p.step(0)
            slots_w.step(2)
            low = low_lanes(8)
            own_bias[...] = jnp.zeros_like(own_bias)
            for l, each in enumerate((down_bias, up_bias)):
                for p in range(2):
                    for k in range(2):
                        at = (2 * p + k) * 128
                        own_bias[p, 2 * l + k : 2 * l + k + 1, :] = each[:, at : at + 128]
            for l, each in enumerate((jnp.sum(bufs[3][...].astype(F32), axis=0, keepdims=True), mid_bias[...])):
                tiles = [jnp.broadcast_to(each[:, k * 128 : (k + 1) * 128], (8, 128)) for k in range(3)]
                turned = pltpu.roll(tiles[1], 64, 1)
                own_bias[0, 4 + l : 5 + l, :] = jnp.where(low, tiles[0], turned)[0:1]
                own_bias[1, 4 + l : 5 + l, :] = jnp.where(low, turned, tiles[2])[0:1]

    def begin():
        met(count)
        slots_w.step(0)
        live = jnp.where(me.xl < counts_ref[me.d], 1.0, 0.0)
        rows_ref[...] = (state_ref[...] * live).astype(BF16)
        open_ends.append(scatter(rows_ref, out_ref, sems[0:2], local.at[0]))

    produce = attention_back(grad_in, weights, mixed, total_ref, bufs, begin, lambda: slots_w.step(1))
    produce = functools.partial(produce, part)
    total, copies = reduce(part, crossed, held, landed, me, (s0, s1), produce, lambda: None, beside)
    value, by_hat = norm_back(total, base[...], above[...], vec_in[0:1, :])
    low_ref[...] = value.astype(BF16)
    own = [jnp.sum(each, axis=0, keepdims=True) for each in (by_hat, total)]
    up, mid, down = ([ref[row : row + 1, :] for row in range(4)] for ref in (up_sums, mid_sums, down_sums))
    order = (own[0], down[0], mid[0], up[0], own[1], down[2], down[1], mid[2], mid[1], up[2], up[1], up[3])
    vec_ref[...] = jnp.zeros_like(vec_ref)
    for row, each in enumerate(order):
        for p in range(2):
            vec_ref[p, row : row + 1, :] = each[:, p * 512 : (p + 1) * 512]

    def vec(z):
        return vec_ref.at[:, :, lanes(z, 128)]

    keep = pltpu.make_async_copy(vec(me.z), from_t.at[me.j], local.at[3])
    keep.start()
    first = []
    for k in range(1, 8):
        j = (me.j + k) % 8
        first.append(remote(vec(j // 2), from_t.at[me.j], sems[4:6], k - 1, me.member(j // 2, j % 2)))
        first[-1].start()
    slots_p.step(1)
    open_ends.append(scatter(low_ref, grad_ref, sems[2:4], local.at[1]))
    slots_w.step(3)
    finish((keep, first))
    mine[:, 0:16, :] = sum(from_t[j] for j in range(8))
    mine[:, 16:24, :] = own_bias[...]
    second = share(mine, from_w, sems[6:8], local.at[2])
    slots_p.step(2)
    slots_w.step(4)
    slots_p.step(3)
    finish(second)
    total = sum(from_w[w] for w in range(16))
    at_lane = 128 - (me.c * 64 + me.d * 8)
    vec_out[...] = pltpu.roll(total[0:16], at_lane % 128, 1)
    for started in open_ends:
        finish(started)
    bias = total[16:24]
    for l in range(LAYERS):
        fc1 = jnp.where(me.d < 4, bias[2 * l : 2 * l + 1], bias[2 * l + 1 : 2 * l + 2])
        bias_out[l : l + 1, :] = pltpu.roll(fc1, (128 - (me.d % 4) * 32) % 128, 1)
    bias_out[4:8, :] = pltpu.roll(bias[4:8], (128 - me.d * 16) % 128, 1)
    bias_out[2:4, :] = jnp.zeros((2, 128), F32)
    for copy in copies:
        copy.wait_send()
    slots_p.step(4)


def close_call(identity, counts, grad, bank, totals, base, above, vectors, w, rows, sums, bias_sums):
    inputs = [counts, grad, bank, totals, base, above, vectors, w, rows, *sums, *bias_sums]
    return call(
        close_kernel,
        identity,
        inputs,
        [pl.BlockSpec(memory_space=pltpu.SMEM), VMEM, ANY] + [VMEM] * (len(inputs) - 3),
        [
            jax.ShapeDtypeStruct((2, 8, BLOCK, 128), BF16),
            jax.ShapeDtypeStruct((2, 8, BLOCK, 128), BF16),
            jax.ShapeDtypeStruct((16, 128), F32),
            jax.ShapeDtypeStruct((8, 128), F32),
            jax.ShapeDtypeStruct((w.shape[1], 128), F32),
            jax.ShapeDtypeStruct((256, 128), F32),
        ],
        [VMEM] * 6,
        [
            pltpu.VMEM((2, 256, D), BF16),
            pltpu.VMEM((BLOCK, D), BF16),
            pltpu.VMEM((2, 16, 512), F32),
            pltpu.VMEM((8, 2, 16, 128), F32),
            pltpu.VMEM((2, 24, 128), F32),
            pltpu.VMEM((16, 24, 128), F32),
            pltpu.VMEM((2, 8, 128), F32),
            pltpu.VMEM((BLOCK, D), BF16),
            pltpu.SemaphoreType.DMA((5,)),
            pltpu.VMEM((ROWS, 384), BF16),
            pltpu.VMEM((ROWS, D), BF16),
            pltpu.VMEM((ROWS, 128), BF16),
            pltpu.VMEM((2, 256, D), BF16),
            pltpu.SemaphoreType.DMA((5,)),
        ]
        + BACK_SCRATCH
        + reduce_scratch()
        + pair_sems(15) * 2
        + pair_sems(7)
        + pair_sems(15)
        + collect_scratch(w.shape[1])
        + collect_scratch(256),
    )


def local(
    tokens,
    counts,
    cotangent,
    qkv_weight,
    out_weight,
    fc1_weight,
    fc2_weight,
    norm_gains,
    shifts,
    qv_bias,
    fc1_bias,
):
    me = Place()

    def images(v):
        v = jnp.pad(v.reshape(2, SEQ, 64), ((0, 0), (0, ROWS - SEQ), (0, 0)))
        return jnp.concatenate([v[:, : ROWS // 2], v[:, ROWS // 2 :]], axis=2)

    packs = [
        (
            jnp.concatenate([qkv_weight[l].T, out_weight[l]], axis=0),
            jnp.concatenate([fc1_weight[l].T, fc2_weight[l]], axis=0),
        )
        for l in range(LAYERS)
    ]
    def wide_rows(v, rows):
        v = v.reshape(rows, -1).astype(F32)
        return jnp.pad(v, ((0, 0), (0, 128 - v.shape[1])))

    small = jnp.concatenate(
        [wide_rows(norm_gains, 4), wide_rows(shifts, 8), wide_rows(qv_bias, 2), wide_rows(fc1_bias, 2)]
    )
    x, cot, packs, small = lax.optimization_barrier((images(tokens), images(cotangent), packs, small))
    first_in, state, wide_a, vectors, qkv_shift, up_bias, cot = open_call(x, cot, packs[0][0], small)
    first_state = state
    middle, second_in, wide_b, first_totals, first_bank, gradient_full, gradient = attention_call(
        1, 0, first_in, wide_a, qkv_shift, state, vectors, packs[0][1], counts, cot
    )
    first_middle = middle
    state, first_in, wide_a, feed_bank = feed_call(
        2, 0, second_in.reshape(ROWS, D), wide_b, up_bias, middle, vectors, packs[1][0]
    )
    first_in = first_in.reshape(ROWS, D)
    middle, second_in, wide_b, totals, mixed, attended = attention_call(
        3, 1, first_in, wide_a, qkv_shift, state, vectors, packs[1][1]
    )
    last_rows, gradient, up_sums, pending, low, up_bias_sums = turn_call(
        4, 1, second_in.reshape(ROWS, D), wide_b, up_bias, middle, vectors, gradient_full, gradient
    )
    owned = {}
    gradient, mid_sums, pending, low, mid_bias_sums, owned["b", 1] = attention_back_call(
        5, 1, low.reshape(ROWS, D), wide_a, mixed, totals, state, first_in, attended, gradient, vectors, pending
    )
    gradient, down_sums, pending, low, down_bias_sums, owned["a", 1] = feed_back_call(
        6, 0, low.reshape(ROWS, D), first_middle, gradient, vectors, feed_bank, pending
    )
    all_sums = [up_sums, mid_sums, down_sums]
    bias_sums = [up_bias_sums, mid_bias_sums, down_bias_sums]
    out_landed, grad_landed, vec, bias, owned["b", 0], owned["a", 0] = close_call(
        7, counts, low.reshape(ROWS, D), first_bank, first_totals, first_state, gradient, vectors, pending,
        last_rows, all_sums, bias_sums
    )

    def side(v, width, at):
        return lax.dynamic_slice_in_dim(v, at * width, width, axis=-1)

    def whole(v):
        return side(v, 64, me.c).reshape(2, ROWS, 64)[:, :SEQ].reshape(2 * SEQ, 64)

    vec = vec[:, :8]
    return (
        whole(out_landed),
        whole(grad_landed).astype(F32),
        jnp.stack([owned["a", l][:192].T for l in range(LAYERS)]),
        jnp.stack([owned["a", l][192:] for l in range(LAYERS)]),
        jnp.stack([owned["b", l][:256].T for l in range(LAYERS)]),
        jnp.stack([owned["b", l][256:] for l in range(LAYERS)]),
        vec[:4].reshape(LAYERS, 2, 1, 8),
        vec[4:12].reshape(LAYERS, 4, 1, 8),
        bias[4:6, :16].reshape(LAYERS, 1, 16),
        bias[:2, :32].reshape(LAYERS, 1, 32),
    )


def solution(mesh):
    placed = (
        P("dp", "tensor"),
        P(),
        P("dp", "tensor"),
        P(None, "dp", "tensor"),
        P(None, "tensor", "dp"),
        P(None, "dp", "tensor"),
        P(None, "tensor", "dp"),
        P(None, None, "tensor", "dp"),
        P(None, None, "tensor", "dp"),
        P(None, "tensor", "dp"),
        P(None, "tensor", "dp"),
    )
    return jax.shard_map(
        local,
        mesh=mesh,
        in_specs=placed,
        out_specs=(
            P("dp", "tensor"),
            P("dp", "tensor"),
            P(None, "dp", "tensor"),
            P(None, "tensor", "dp"),
            P(None, "dp", "tensor"),
            P(None, "tensor", "dp"),
            P(None, None, "tensor", "dp"),
            P(None, None, "tensor", "dp"),
            P(None, "tensor", "dp"),
            P(None, "tensor", "dp"),
        ),
        check_vma=False,
    )
```
